32 devices in a mesh: seq: 16 (over z, y, x), ch: 2 (over core).
Axes of the slice: x: 2, y: 2, z: 4, core: 2. Of those that a mesh axis runs over, the one named last changes fastest.
Arguments:
- tokens: bfloat16 [4, 1024, 768], P(None, 'seq', 'ch'), may hold values from -6 to 6
- valid_len: int32 [4], replicated, may hold values from 128 to 1024, as said below
- ln1_gain: float32 [768], replicated, may hold values from 0.5 to 1.5
- ln1_bias: float32 [768], replicated, may hold values from -2 to 2
- w_query: bfloat16 [768, 768], P(None, 'ch'), may hold values from -0.21875 to 0.21875
- w_key: bfloat16 [768, 768], P(None, 'ch'), may hold values from -0.21875 to 0.21875
- w_value: bfloat16 [768, 768], P(None, 'ch'), may hold values from -0.21875 to 0.21875
- shift_kernel: float32 [64, 768], P(None, 'ch'), may hold values from -0.75 to 0.75
- ssm_rate: float32 [12, 64], P('ch'), may hold values from 0.00048828125 to 0.1
- ssm_coef: float32 [768, 64], P('ch'), may hold values from -0.75 to 0.75
- w_out: bfloat16 [768, 768], P('ch'), may hold values from -0.21875 to 0.21875
- ln2_gain: float32 [768], replicated, may hold values from 0.5 to 1.5
- ln2_bias: float32 [768], replicated, may hold values from -2 to 2
- w_up: bfloat16 [768, 3072], P(None, 'ch'), may hold values from -0.21875 to 0.21875
- w_down: bfloat16 [3072, 768], P('ch'), may hold values from -0.109375 to 0.109375
- d_out: bfloat16 [4, 1024, 768], P(None, 'seq', 'ch'), may hold values from -6 to 6
Outputs:
- block_out: float32 [4, 1024, 768], P(None, 'seq', 'ch')
- grad_tokens: float32 [4, 1024, 768], P(None, 'seq', 'ch')
- grad_ln1_gain: float32 [768], replicated
- grad_ln1_bias: float32 [768], replicated
- grad_query: float32 [768, 768], P('seq', 'ch')
- grad_key: float32 [768, 768], P('seq', 'ch')
- grad_value: float32 [768, 768], P('seq', 'ch')
- grad_shift: float32 [64, 768], P(None, 'ch')
- grad_rate: float32 [12, 64], P('ch')
- grad_coef: float32 [768, 64], P('ch')
- grad_out: float32 [768, 768], P('ch', 'seq')
- grad_ln2_gain: float32 [768], replicated
- grad_ln2_bias: float32 [768], replicated
- grad_up: float32 [768, 3072], P('seq', 'ch')
- grad_down: float32 [3072, 768], P('ch', 'seq')
The draws below stay inside these ranges and needn't reach their ends.
Inputs may be any that keep to these rules, and one draw needn't show every extreme that they name: `valid_len`: valid leading positions of each bucket; one bucket, drawn from the seed, is full.
All inputs are finite; a program needn't handle non-finite values.
Results may differ from the reference program's by a relative error of at most 0.015.
Values may be sent and summed in bfloat16 or wider, within the bound.
No kernel may reach another device: no remote copies, remote signals or barrier semaphores. Data moves between devices by JAX's collectives and lax.ppermute only.
A program may use at most 384 MiB of HBM per device.

```python
import math
import jax
import jax.numpy as jnp
import numpy as np
from jax import lax

D = 768
HEADS = 12
FF = 3072
NSTATE = 64
TAPS = 64
BUCKET_DEV = 64
BUCKETS = 4
HEAD_DIM = 64
BUCKET_LEN = 1024


def draw_valid_len(key, part):
    key = jax.random.fold_in(key, 5)
    first, second = jax.random.split(key)
    counts = jax.random.randint(first, (BUCKETS,), BUCKET_LEN // 8, BUCKET_LEN + 1)
    order = jax.random.permutation(second, BUCKETS)
    counts = counts.at[order[0]].set(BUCKET_LEN)
    return counts.astype(jnp.int32)


def steps_of(key, extent, cuts, smallest, largest):
    def one(axis_at, parts):
        draws = jax.random.uniform(jax.random.fold_in(jax.random.fold_in(key, 6), axis_at), (parts,), jnp.float32, smallest / len(cuts), largest / len(cuts))
        return jnp.repeat(jnp.exp(draws), extent[axis_at] // parts).reshape((-1,) + (1,) * (len(extent) - axis_at - 1))

    level = one(*cuts[0])
    for cut in cuts[1:]:
        level = level * one(*cut)
    return level


def scatter_about(key, extent, scale, most, cuts=(), kind=jnp.bfloat16):
    array = scale * jax.random.normal(key, extent, jnp.float32)
    if cuts:
        array = array * steps_of(key, extent, cuts, -0.22, 0.18)
    return jnp.clip(array, -most, most).astype(kind)


def setup_inputs(seed: int = 0) -> dict:
    streams_of = jax.random.split(jax.random.key(seed), 17)
    return {
        "tokens": scatter_about(streams_of[0], (BUCKETS, BUCKET_LEN, D), 1.0, 6.0, ((1, 16), (2, 2))),
        "valid_len": draw_valid_len(jax.random.fold_in(streams_of[16], 71), 0),
        "ln1_gain": jnp.clip(1.0 + 0.1 * jax.random.normal(streams_of[2], (D,), jnp.float32), 0.5, 1.5),
        "ln1_bias": scatter_about(streams_of[3], (D,), 0.3, 2.0, (), jnp.float32),
        "w_query": scatter_about(streams_of[4], (D, D), D ** -0.5, 0.21875, ((1, 2),)),
        "w_key": scatter_about(streams_of[5], (D, D), D ** -0.5, 0.21875, ((1, 2),)),
        "w_value": scatter_about(streams_of[6], (D, D), D ** -0.5, 0.21875, ((1, 2),)),
        "shift_kernel": scatter_about(streams_of[7], (TAPS, D), TAPS ** -0.5, 0.75, ((1, 2),), jnp.float32),
        "ssm_rate": jnp.clip(jnp.exp(math.log(0.1) - 5.322034 * jax.random.uniform(streams_of[8], (HEADS, NSTATE), jnp.float32) ** steps_of(streams_of[8], (HEADS, NSTATE), ((0, 2),), -0.2, 0.2)), 0.00048828125, 0.1),
        "ssm_coef": scatter_about(streams_of[9], (D, NSTATE), NSTATE ** -0.5, 0.75, ((0, 2),), jnp.float32),
        "w_out": scatter_about(streams_of[10], (D, D), D ** -0.5, 0.21875, ((0, 2),)),
        "ln2_gain": jnp.clip(1.0 + 0.1 * jax.random.normal(streams_of[11], (D,), jnp.float32), 0.5, 1.5),
        "ln2_bias": scatter_about(streams_of[12], (D,), 0.3, 2.0, (), jnp.float32),
        "w_up": scatter_about(streams_of[13], (D, FF), D ** -0.5, 0.21875, ((1, 2),)),
        "w_down": scatter_about(streams_of[14], (FF, D), FF ** -0.5, 0.109375, ((0, 2),)),
        "d_out": scatter_about(streams_of[15], (BUCKETS, BUCKET_LEN, D), 1.0, 6.0, ((1, 16), (2, 2))),
    }


HIGH = lax.Precision.HIGHEST

@jax.custom_vjp
def low(v):
    return lax.optimization_barrier(v.astype(jnp.bfloat16)).astype(jnp.float32)

@jax.custom_vjp
def low_back(v):
    return v

def low_keep(v):
    return (low(v), None)

def low_pass(kept, grad):
    return (grad,)

def back_keep(v):
    return (v, None)

def back_low(kept, grad):
    return (low(grad),)
low.defvjp(low_keep, low_pass)
low_back.defvjp(back_keep, back_low)

def layer_norm(x, gain, bias):
    mean = lax.optimization_barrier(jnp.mean(x, axis=-1, keepdims=True))
    cent = x - mean
    var = lax.optimization_barrier(jnp.mean(cent * cent, axis=-1, keepdims=True))
    return cent * lax.rsqrt(var + 1e-05) * gain + bias

def matmul(left, right):
    return jnp.dot(left, right, precision=HIGH, preferred_element_type=jnp.float32)

def ssm_end(mixed, rate):
    span = mixed.shape[1]
    steps = jnp.arange(span, dtype=jnp.float32)
    scale = jnp.sqrt(-jnp.expm1(-2.0 * rate))
    weights = jnp.exp(-(span - 1.0 - steps)[:, None, None] * rate[None]) * scale[None]
    return jnp.einsum('shn,bshj->bhnj', weights, mixed, precision=HIGH)

def ssm_out(mixed, rate, coef, incoming):
    span = mixed.shape[1]
    steps = jnp.arange(span, dtype=jnp.float32)
    scale = jnp.sqrt(-jnp.expm1(-2.0 * rate))
    power = jnp.exp(-steps[:, None, None] * rate[None])
    kern = jnp.einsum('lhn,hjn->lhj', power * scale[None], coef, precision=HIGH)
    lag = np.arange(span)[:, None] - np.arange(span)[None, :]
    table = jnp.take(kern, np.clip(lag, 0, span - 1), axis=0) * (lag >= 0).astype(np.float32)[:, :, None, None]
    inner = jnp.einsum('tshj,bshj->bthj', table, mixed, precision=HIGH)
    ahead = jnp.exp(-(steps + 1.0)[:, None, None] * rate[None])
    carried = jnp.einsum('thn,hjn,bhnj->bthj', ahead, coef, incoming, precision=HIGH)
    return inner + carried

def ssm_ref(mixed, rate, coef):
    size, heads, width = mixed.shape
    blocks = mixed.reshape(size // BUCKET_DEV, 1, BUCKET_DEV, heads, width)
    decay = jnp.exp(-BUCKET_DEV * rate)

    def step(state, block):
        outputs = ssm_out(block, rate, coef, state)
        state = decay[None, :, :, None] * state + ssm_end(block, rate)
        return (state, outputs[0])
    start = jnp.zeros((1, rate.shape[0], rate.shape[1], width), jnp.float32)
    _, ys = lax.scan(jax.checkpoint(step), start, blocks)
    return ys.reshape(mixed.shape)

def shift_ref(keyed, kernel):
    taps = kernel.shape[0]
    length = keyed.shape[0]
    padded = jnp.pad(keyed, ((taps - 1, 0), (0, 0)))
    total = jnp.zeros_like(keyed)
    for lag in range(taps):
        total = total + kernel[lag] * padded[taps - 1 - lag:taps - 1 - lag + length]
    return total

def reference(tokens, valid_len, ln1_gain, ln1_bias, w_query, w_key, w_value, shift_kernel, ssm_rate, ssm_coef, w_out, ln2_gain, ln2_bias, w_up, w_down, d_out):
    params = tuple((p.astype(jnp.float32) for p in (ln1_gain, ln1_bias, w_query, w_key, w_value, shift_kernel, ssm_rate, ssm_coef, w_out, ln2_gain, ln2_bias, w_up, w_down)))

    def forward(x_all, g1, c1, wq, wk, wv, kernel, rate, coef, wo, g2, c2, wu, wd):

        def bucket(pair):
            row, limit = pair
            length = row.shape[0]
            norm1 = low(layer_norm(row, g1, c1))
            query = low_back(low(matmul(norm1, wq)))
            keyed = low_back(low(matmul(norm1, wk)))
            valued = low_back(low(matmul(norm1, wv)))
            shifted = shift_ref(keyed, kernel)
            mask = (jnp.arange(length) < limit).astype(jnp.float32)
            mixed = shifted * valued * mask[:, None]
            mixer = ssm_ref(mixed.reshape(length, HEADS, HEAD_DIM), rate, coef.reshape(HEADS, HEAD_DIM, NSTATE)).reshape(length, D)
            gated = low(query * mixer)
            branch = low_back(matmul(gated, wo))
            resid = row + branch
            norm2 = low(layer_norm(resid, g2, c2))
            hidden = low_back(matmul(norm2, wu))
            act = low(jax.nn.gelu(hidden))
            return resid + matmul(act, wd)
        return lax.map(jax.checkpoint(bucket), (x_all, valid_len))
    block_out, back = jax.vjp(forward, tokens.astype(jnp.float32), *params)
    grads = back(d_out.astype(jnp.float32))
    return (block_out, grads[0], grads[1], grads[2], grads[3], grads[4], grads[5], grads[6], grads[7], grads[8], grads[9], grads[10], grads[11], grads[12], grads[13])
```

```python
import functools

import jax
import jax.numpy as jnp
from jax import lax
from jax.experimental import pallas as pl
from jax.experimental.pallas import tpu as pltpu
from jax.sharding import PartitionSpec as P

LANES = 128
HIGH = lax.Precision.HIGHEST
F32 = jnp.float32
BF16 = jnp.bfloat16
VMEM = pl.BlockSpec(memory_space=pltpu.VMEM)
SMEM = pl.BlockSpec(memory_space=pltpu.SMEM)
PARAMS = pltpu.CompilerParams(vmem_limit_bytes=56 * 1024 * 1024)


def trade(value, step):
    count = lax.axis_size("seq")
    return lax.ppermute(value, "seq", [(i, i ^ step) for i in range(count)])


def swap(value):
    return lax.ppermute(value, "ch", [(0, 1), (1, 0)])


def xor_place(x, index):
    count = x.shape[0]
    bit = 1
    while bit < count:
        y = x.reshape((count // (2 * bit), 2, bit) + x.shape[1:])
        flipped = jnp.concatenate([y[:, 1:], y[:, :1]], axis=1)
        x = jnp.where((index & bit) != 0, flipped, y).reshape(x.shape)
        bit *= 2
    return x


def tree_sum(parts):
    parts = list(parts)
    while len(parts) > 1:
        parts = [parts[i] + parts[i + 1] for i in range(0, len(parts), 2)]
    return parts[0]


def reduce_rows(send, keep, order):
    for at, step in enumerate(order):
        got = trade(send, step)
        total = keep.astype(F32) + got.astype(F32)
        if at + 1 == len(order):
            return total
        half = total.shape[0] // 2
        send, keep = total[half:].astype(BF16), total[:half]


def layer_norm(x, gain, bias):
    mean = jnp.mean(x, axis=-1, keepdims=True)
    cent = x - mean
    var = jnp.mean(cent * cent, axis=-1, keepdims=True)
    return cent * lax.rsqrt(var + 1e-05) * gain + bias


def dot(left, right, contract=(1, 0), out=F32):
    return lax.dot_general(
        left, right, (((contract[0],), (contract[1],)), ((), ())), preferred_element_type=F32
    ).astype(out)


def fdot(left, right):
    return lax.dot_general(
        left, right, (((1,), (0,)), ((), ())), preferred_element_type=F32, precision=HIGH
    )


def rolled(x, r):
    return x if r == 0 else pltpu.roll(x, r % x.shape[0], 0)


def tables(rrow, rcol, span):
    step_r = lax.broadcasted_iota(jnp.int32, (span, LANES), 0).astype(F32)
    step_c = lax.broadcasted_iota(jnp.int32, (LANES, span), 1).astype(F32)
    return step_r, step_c, jnp.broadcast_to(rrow, (span, LANES)), rcol[:, :span]


def mix_forward(scal, tabs, rrow, taps, *refs, group, buckets, span):
    kv = refs[:group]
    outs = refs[group : 2 * group]
    kf, vf, shifted_ref, mixed_ref, states, ysc, kern_ref = refs[2 * group :]
    b, g, limit = scal[0], scal[1], scal[2]
    rcol, scol, coefm = tabs[0], tabs[1], tabs[3]
    hm = tabs[4]
    step_r, step_c, rr, rc = tables(rrow[...], rcol, span)
    kern_ref[...] = fdot(jnp.exp(-step_r * rr), scol * coefm)
    w_end = jnp.exp(-(span - 1.0 - step_c) * rc) * scol[:, :span]
    p_out = jnp.exp(-(step_r + 1.0) * rr)
    decay = jnp.exp(-float(span) * rcol)
    kf[pl.ds(0, span), :] = jnp.zeros((span, LANES), F32)
    for j in range(group):
        for k in range(buckets):
            row = pl.multiple_of((lax.bitwise_xor(b, k) * group + lax.bitwise_xor(g, j)) * span, span)
            kf[pl.ds(row + span, span), :] = kv[j][0, k].astype(F32)
            vf[pl.ds(row, span), :] = kv[j][1, k].astype(F32)
    row_id = lax.broadcasted_iota(jnp.int32, (span, LANES), 0)

    def chunk(c, state):
        start = pl.multiple_of(c * span, span)
        x = kf[pl.ds(start, 2 * span), :]
        acc = jnp.zeros((span, LANES), F32)
        for r in range(8):
            xr = rolled(x, r)
            for q in range(span // 8):
                acc = acc + taps[8 * q + r : 8 * q + r + 1, :] * xr[span - 8 * q : 2 * span - 8 * q]
        shifted_ref[pl.ds(start, span), :] = acc
        mixed = jnp.where(row_id + start < limit, acc * vf[pl.ds(start, span), :], 0.0)
        mixed_ref[pl.ds(start, span), :] = mixed
        states[c] = state
        y = fdot(p_out, coefm * state)
        tails = [y[8 * i : 8 * i + 8] for i in range(span // 8)]
        for r in range(8):
            mr = jnp.where(row_id >= r, rolled(mixed, r), 0.0)
            for q in range(span // 8):
                weight = kern_ref[8 * q + r : 8 * q + r + 1, :]
                for i in range(q, span // 8):
                    tails[i] = tails[i] + weight * mr[8 * (i - q) : 8 * (i - q) + 8]
        for i in range(span // 8):
            ysc[pl.ds(start + 8 * i, 8), :] = tails[i]
        return decay * state + fdot(w_end, mixed) * hm

    lax.fori_loop(0, group * buckets, chunk, jnp.zeros((LANES, LANES), F32))
    for j in range(group):
        for k in range(buckets):
            row = pl.multiple_of((lax.bitwise_xor(b, k) * group + lax.bitwise_xor(g, j)) * span, span)
            outs[j][k] = ysc[pl.ds(row, span), :].astype(BF16)


def mix_backward(scal, tabs, rrow, taps, vf, shifted_ref, *refs, group, buckets, span):
    d_in = refs[:group]
    outs = refs[group : 2 * group]
    dmf, dsf, adj, dks, dvs, kern_ref = refs[2 * group :]
    b, g, limit = scal[0], scal[1], scal[2]
    rcol, scol, coefm = tabs[0], tabs[1], tabs[3]
    step_r, step_c, rr, rc = tables(rrow[...], rcol, span)
    kern_ref[...] = fdot(jnp.exp(-step_r * rr), scol * coefm)
    p_rev = jnp.exp(-(span - 1.0 - step_r) * rr)
    p_in = jnp.exp(-(step_c + 1.0) * rc)
    decay = jnp.exp(-float(span) * rcol)
    chunks = group * buckets
    dsf[pl.ds(chunks * span, span), :] = jnp.zeros((span, LANES), F32)
    for j in range(group):
        for k in range(buckets):
            row = pl.multiple_of((lax.bitwise_xor(b, k) * group + lax.bitwise_xor(g, j)) * span, span)
            dmf[pl.ds(row, span), :] = d_in[j][k].astype(F32)
    row_id = lax.broadcasted_iota(jnp.int32, (span, LANES), 0)
    eighths = span // 8

    def chunk(turn, after):
        c = chunks - 1 - turn
        start = pl.multiple_of(c * span, span)
        dm = dmf[pl.ds(start, span), :]
        adj[c] = after
        y = fdot(p_rev, scol * after)
        heads = [y[8 * i : 8 * i + 8] for i in range(eighths)]
        for r in range(8):
            mr = jnp.where(row_id < span - r, rolled(dm, -r), 0.0)
            for q in range(eighths):
                weight = kern_ref[8 * q + r : 8 * q + r + 1, :]
                for i in range(eighths - q):
                    heads[i] = heads[i] + weight * mr[8 * (i + q) : 8 * (i + q) + 8]
        d_mixed = jnp.where(row_id + start < limit, jnp.concatenate(heads, axis=0), 0.0)
        dvs[pl.ds(start, span), :] = d_mixed * shifted_ref[pl.ds(start, span), :]
        dsf[pl.ds(start, span), :] = d_mixed * vf[pl.ds(start, span), :]
        x = dsf[pl.ds(start, 2 * span), :]
        acc = jnp.zeros((span, LANES), F32)
        for r in range(8):
            xr = rolled(x, -r)
            for q in range(eighths):
                acc = acc + taps[8 * q + r : 8 * q + r + 1, :] * xr[8 * q : 8 * q + span]
        dks[pl.ds(start, span), :] = acc
        return decay * after + coefm * fdot(p_in, dm)

    lax.fori_loop(0, chunks, chunk, jnp.zeros((LANES, LANES), F32))
    for j in range(group):
        for k in range(buckets):
            row = pl.multiple_of((lax.bitwise_xor(b, k) * group + lax.bitwise_xor(g, j)) * span, span)
            outs[j][0, k] = dks[pl.ds(row, span), :].astype(BF16)
            outs[j][1, k] = dvs[pl.ds(row, span), :].astype(BF16)


def mix_grads(
    tabs, rrow, kf, mixed_ref, states, dmf, dsf, adj, shift_out, coef_out, rate_out, acc_s, acc_k, *, span
):
    rcol, scol, dscol, coefm, hm = tabs[0], tabs[1], tabs[2], tabs[3], tabs[4]
    _, step_c, _, rc = tables(rrow[...], rcol, span)
    p_in = jnp.exp(-(step_c + 1.0) * rc)
    p_in1 = p_in * (step_c + 1.0)
    p_end = jnp.exp(-(span - 1.0 - step_c) * rc)
    p_end1 = p_end * (span - 1.0 - step_c)
    p_kern = jnp.exp(-step_c * rc)
    decay = jnp.exp(-float(span) * rcol)
    chunks = mixed_ref.shape[0] // span
    eighths = span // 8
    acc_s[...] = jnp.zeros_like(acc_s)
    acc_k[...] = jnp.zeros_like(acc_k)
    coef_out[...] = jnp.zeros_like(coef_out)
    rate_out[...] = jnp.zeros_like(rate_out)
    row_id = lax.broadcasted_iota(jnp.int32, (span, LANES), 0)

    def chunk(c, carry):
        start = pl.multiple_of(c * span, span)
        x = kf[pl.ds(start, 2 * span), :]
        ds = dsf[pl.ds(start, span), :]
        mixed = mixed_ref[pl.ds(start, span), :]
        dm = dmf[pl.ds(start, span), :]
        for r in range(8):
            xr = rolled(x, r)
            mr = jnp.where(row_id >= r, rolled(mixed, r), 0.0)
            for q in range(eighths):
                whole = ds * xr[span - 8 * q : 2 * span - 8 * q]
                acc_s[8 * q + r] += jnp.sum(whole.reshape(eighths, 8, LANES), axis=0)
                part = dm[8 * q :] * mr[: span - 8 * q]
                acc_k[8 * q + r] += jnp.sum(part.reshape(eighths - q, 8, LANES), axis=0)
        state, after = states[c], adj[c]
        coef_out[...] += state * fdot(p_in, dm)
        rate_out[...] += (
            after * (dscol * fdot(p_end, mixed) - scol * fdot(p_end1, mixed) - span * decay * state)
            - coefm * state * fdot(p_in1, dm)
        )
        return carry

    lax.fori_loop(0, chunks, chunk, 0)
    shift_out[...] = jnp.sum(acc_s[...], axis=1)
    gk = jnp.sum(acc_k[...], axis=1)
    m0 = fdot(p_kern, gk)
    m1 = fdot(p_kern * step_c, gk)
    coef_out[...] = (coef_out[...] + scol * m0) * hm
    rate_out[...] = rate_out[...] + coefm * (dscol * m0 - scol * m1)


def body(
    tokens,
    valid_len,
    ln1_gain,
    ln1_bias,
    w_query,
    w_key,
    w_value,
    shift_kernel,
    ssm_rate,
    ssm_coef,
    w_out,
    ln2_gain,
    ln2_bias,
    w_up,
    w_down,
    d_out,
):
    buckets, span, share = tokens.shape
    rows = buckets * span
    heads, nstate = ssm_rate.shape
    head_width = share // heads
    width = w_query.shape[0]
    count = lax.axis_size("seq")
    group = count // buckets
    part = share // group
    place = lax.axis_index("seq")
    member = lax.axis_index("ch")
    b, g = place // group, place % group

    def whole_rows(mine):
        other = swap(mine)
        return jnp.where(
            member == 0,
            jnp.concatenate([mine, other], axis=1),
            jnp.concatenate([other, mine], axis=1),
        )

    def to_bucket(x):
        x = xor_place(x, b)
        return jnp.concatenate([x[:1]] + [trade(x[k : k + 1], k * group) for k in range(1, buckets)], axis=0)

    def from_bucket(x):
        x = x.reshape(buckets, span, x.shape[-1])
        x = jnp.concatenate([x[:1]] + [trade(x[k : k + 1], k * group) for k in range(1, buckets)], axis=0)
        return xor_place(x, b)

    lane = jnp.arange(LANES, dtype=jnp.int32)
    chan = g * part + lane
    lane_ok = lane < part
    lane_head = chan // head_width
    first_head = (g * part) // head_width
    row = jnp.arange(LANES, dtype=jnp.int32)
    row_head = jnp.minimum(first_head + row // nstate, heads - 1)
    hm = ((first_head + row // nstate)[:, None] == lane_head[None, :]) & lane_ok[None, :]
    hm = hm.astype(F32)
    head_hot = (row_head[:, None] == jnp.arange(heads)[None, :]).astype(F32)
    two = lax.dynamic_slice_in_dim(
        jnp.concatenate([ssm_rate, ssm_rate[-1:]], axis=0), first_head, 2, 0
    ).reshape(1, 2 * nstate)
    rate_col = jnp.broadcast_to(two.reshape(-1, 1), (LANES, LANES))
    scale_col = jnp.sqrt(-jnp.expm1(-2.0 * rate_col))
    dscale_col = jnp.exp(-2.0 * rate_col) / scale_col
    coef_part = lax.dynamic_slice_in_dim(ssm_coef, g * part, part, 0)
    coef_part = jnp.pad(coef_part, ((0, LANES - part), (0, 0))).T
    coefm = jnp.concatenate([coef_part, coef_part], axis=0) * hm
    tabs = jnp.stack([rate_col, scale_col, dscale_col, coefm, hm])
    taps = jnp.pad(lax.dynamic_slice_in_dim(shift_kernel, g * part, part, 1), ((0, 0), (0, LANES - part)))
    scal = jnp.stack([b, g, lax.dynamic_index_in_dim(valid_len, b, 0, False)]).astype(jnp.int32)
    channel = jnp.arange(share, dtype=jnp.int32)
    spread = [
        ((channel[:, None] == (g ^ j) * part + lane[None, :]) & lane_ok[None, :]).astype(BF16)
        for j in range(group)
    ]

    def to_channels(blocks):
        total = dot(blocks[0], spread[0], (1, 1))
        for j in range(1, group):
            total = total + dot(blocks[j], spread[j], (1, 1))
        return total

    def trade_group(blocks):
        return [blocks[0]] + [trade(blocks[j], j) for j in range(1, group)]

    flat_x = whole_rows(to_bucket(tokens).reshape(rows, share)).astype(F32)
    grad_full = whole_rows(to_bucket(d_out).reshape(rows, share))
    norm1_f, ln1_back = jax.vjp(layer_norm, flat_x, ln1_gain, ln1_bias)
    norm1 = norm1_f.astype(BF16)
    query = dot(norm1, w_query, out=BF16)
    keyed = dot(norm1, w_key, out=BF16)
    valued = dot(norm1, w_value, out=BF16)
    kv = [
        jnp.stack([dot(keyed, spread[j], out=BF16), dot(valued, spread[j], out=BF16)]).reshape(
            2, buckets, span, LANES
        )
        for j in range(group)
    ]
    kv = trade_group(kv)
    length = count * span
    f32 = lambda *shape: jax.ShapeDtypeStruct(shape, F32)
    small = jax.ShapeDtypeStruct((buckets, span, LANES), BF16)
    forward_out = pl.pallas_call(
        functools.partial(mix_forward, group=group, buckets=buckets, span=span),
        in_specs=[SMEM] + [VMEM] * (3 + group),
        out_specs=[VMEM] * (group + 5),
        out_shape=[small] * group
        + [
            f32(length + span, LANES),
            f32(length, LANES),
            f32(length, LANES),
            f32(length, LANES),
            f32(count, LANES, LANES),
        ],
        scratch_shapes=[pltpu.VMEM((length, LANES), F32), pltpu.VMEM((span, LANES), F32)],
        compiler_params=PARAMS,
        name="mix_forward",
    )(scal, tabs, two, taps, *kv)
    mixer_parts = trade_group(forward_out[:group])
    kf, vf, shifted, mixed, states = forward_out[group:]
    mixer = to_channels([p.reshape(rows, LANES) for p in mixer_parts])
    query_f = query.astype(F32)
    gated = (query_f * mixer).astype(BF16)
    branch = dot(gated, w_out, out=BF16)
    resid = flat_x + (branch.astype(F32) + swap(branch).astype(F32))
    norm2_f, ln2_back = jax.vjp(layer_norm, resid, ln2_gain, ln2_bias)
    norm2 = norm2_f.astype(BF16)
    hidden = dot(norm2, w_up)
    act_f, gelu_back = jax.vjp(jax.nn.gelu, hidden)
    act = act_f.astype(BF16)
    d_act = dot(grad_full, w_down, (1, 1))
    d_hidden = gelu_back(d_act)[0].astype(BF16)
    d_norm2 = dot(d_hidden, w_up, (1, 1), out=BF16)
    d_norm2 = d_norm2.astype(F32) + swap(d_norm2).astype(F32)
    d_resid_ln, grad_g2, grad_c2 = ln2_back(d_norm2)
    d_resid = grad_full.astype(F32) + d_resid_ln
    d_branch = d_resid.astype(BF16)
    d_gated = dot(d_branch, w_out, (1, 1))
    d_mixer = (d_gated * query_f).astype(BF16)
    d_mixer_parts = trade_group([dot(d_mixer, spread[j], out=BF16).reshape(buckets, span, LANES) for j in range(group)])
    pair = jax.ShapeDtypeStruct((2, buckets, span, LANES), BF16)
    backward_out = pl.pallas_call(
        functools.partial(mix_backward, group=group, buckets=buckets, span=span),
        in_specs=[SMEM] + [VMEM] * (5 + group),
        out_specs=[VMEM] * (group + 3),
        out_shape=[pair] * group
        + [f32(length, LANES), f32(length + span, LANES), f32(count, LANES, LANES)],
        scratch_shapes=[
            pltpu.VMEM((length, LANES), F32),
            pltpu.VMEM((length, LANES), F32),
            pltpu.VMEM((span, LANES), F32),
        ],
        compiler_params=PARAMS,
        name="mix_backward",
    )(scal, tabs, two, taps, vf, shifted, *d_mixer_parts)
    d_kv = trade_group(backward_out[:group])
    dmf, dsf, adj = backward_out[group:]
    d_keyed = to_channels([p[0].reshape(rows, LANES) for p in d_kv]).astype(BF16)
    d_valued = to_channels([p[1].reshape(rows, LANES) for p in d_kv]).astype(BF16)
    d_query = (d_gated * mixer).astype(BF16)
    shift_part, coef_grad, rate_grad = pl.pallas_call(
        functools.partial(mix_grads, span=span),
        in_specs=[VMEM] * 8,
        out_specs=[VMEM] * 3,
        out_shape=[f32(span, LANES), f32(LANES, LANES), f32(LANES, LANES)],
        scratch_shapes=[pltpu.VMEM((span, 8, LANES), F32), pltpu.VMEM((span, 8, LANES), F32)],
        compiler_params=PARAMS,
        name="mix_grads",
    )(tabs, two, kf, mixed, states, dmf, dsf, adj)
    d_norm1 = (
        dot(d_query, w_query, (1, 1)) + dot(d_keyed, w_key, (1, 1)) + dot(d_valued, w_value, (1, 1))
    ).astype(BF16)
    d_norm1 = d_norm1.astype(F32) + swap(d_norm1).astype(F32)
    d_x_ln, grad_g1, grad_c1 = ln1_back(d_norm1)

    mine = lambda a: lax.dynamic_slice_in_dim(a, member * share, share, 1)
    down = dot(act, w_down, out=BF16)
    other_half = lax.dynamic_slice_in_dim(down, (1 - member) * share, share, 1)
    block_mine = mine(resid) + (mine(down).astype(F32) + swap(other_half).astype(F32))
    block_out = from_bucket(block_mine.astype(BF16)).astype(F32)
    grad_tokens = from_bucket(mine(d_resid + d_x_ln).astype(BF16)).astype(F32)

    bits = [1 << i for i in range(count.bit_length() - 1)]
    block = width // count

    def relative(left, order):
        rel = jnp.arange(width, dtype=jnp.int32)
        at = rel // block
        target = jnp.zeros_like(at)
        for i, step in enumerate(order):
            target = target + ((at >> (len(order) - 1 - i)) & 1) * step
        source = (target ^ place) * block + rel % block
        hot = (jnp.arange(width, dtype=jnp.int32)[:, None] == source[None, :]).astype(BF16)
        return dot(left, hot, out=BF16)

    def summed(left, right, order):
        left = relative(left, order)
        half = width // 2
        send = dot(left[:, half:], right, (0, 0), out=BF16)
        keep = dot(left[:, :half], right, (0, 0), out=BF16)
        return reduce_rows(send, keep, order)

    order_a = bits
    order_b = [bits[1], bits[0]] + bits[2:]
    grad_up = summed(norm2, d_hidden, order_a)
    grad_down = summed(grad_full, act, order_b).T
    grad_out = summed(d_branch, gated, order_a).T
    grad_query = summed(norm1, d_query, order_b)
    grad_key = summed(norm1, d_keyed, order_a)
    grad_value = summed(norm1, d_valued, order_b)

    rate_heads = lax.dot_general(
        head_hot, jnp.sum(rate_grad, axis=1, keepdims=True) * jnp.eye(LANES, dtype=F32),
        (((0,), (0,)), ((), ())), precision=HIGH,
    )
    rate_heads = rate_heads[:, :nstate] + rate_heads[:, nstate:]
    coef_n = coef_grad[:nstate] + coef_grad[nstate:]

    def all_buckets(x):
        return tree_sum([x] + [trade(x, k * group) for k in range(1, buckets)])

    def all_group(x):
        return [x] + [trade(x, j) for j in range(1, group)]

    vectors = jnp.stack([grad_g2, grad_c2])
    mixer_small = all_buckets(jnp.concatenate([shift_part, coef_n], axis=0))
    wide = jnp.zeros((heads, width), F32).at[:, :nstate].set(rate_heads)
    other_small = all_buckets(jnp.concatenate([vectors, wide], axis=0))
    mixer_all = all_group(mixer_small)
    spread_f = [m.astype(F32) for m in spread]
    placed = sum(
        lax.dot_general(mixer_all[j], spread_f[j], (((1,), (1,)), ((), ())), precision=HIGH) for j in range(group)
    )
    grad_shift = placed[:span]
    grad_coef = placed[span:].T
    other_small = tree_sum(all_group(other_small))
    grad_g2, grad_c2 = other_small[0], other_small[1]
    grad_rate = other_small[2:, :nstate]
    tail = tree_sum(all_group(all_buckets(jnp.stack([grad_g1, grad_c1]))))
    grad_g1, grad_c1 = tail[0], tail[1]
    return (
        block_out,
        grad_tokens,
        grad_g1,
        grad_c1,
        grad_query,
        grad_key,
        grad_value,
        grad_shift,
        grad_rate,
        grad_coef,
        grad_out,
        grad_g2,
        grad_c2,
        grad_up,
        grad_down,
    )


def solution(mesh):
    in_specs = (
        P(None, "seq", "ch"),
        P(),
        P(),
        P(),
        P(None, "ch"),
        P(None, "ch"),
        P(None, "ch"),
        P(None, "ch"),
        P("ch", None),
        P("ch", None),
        P("ch", None),
        P(),
        P(),
        P(None, "ch"),
        P("ch", None),
        P(None, "seq", "ch"),
    )
    out_specs = (
        P(None, "seq", "ch"),
        P(None, "seq", "ch"),
        P(),
        P(),
        P("seq", "ch"),
        P("seq", "ch"),
        P("seq", "ch"),
        P(None, "ch"),
        P("ch", None),
        P("ch", None),
        P("ch", "seq"),
        P(),
        P(),
        P("seq", "ch"),
        P("ch", "seq"),
    )
    return jax.shard_map(body, mesh=mesh, in_specs=in_specs, out_specs=out_specs, check_vma=False)
```

```python
import functools

import jax
import jax.numpy as jnp
from jax import lax
from jax.experimental import pallas as pl
from jax.experimental.pallas import tpu as pltpu
from jax.sharding import PartitionSpec as P

LANES = 128
HIGH = lax.Precision.HIGHEST
F32 = jnp.float32
BF16 = jnp.bfloat16
VMEM = pl.BlockSpec(memory_space=pltpu.VMEM)
SMEM = pl.BlockSpec(memory_space=pltpu.SMEM)
MIB = 1024 * 1024

CUTS = (0.34, 0.67)
OUT_IN = 2
MERGE = {}
ORDER = ('turn_up', 'g0', 'resid', 'g1', 'mixer', 'turn_out', 'f0s2', 'g2', 'project', 'f1s2', 'tokens', 'parameters', 'place', 'pe', 'f0z', 'f1z', 'f0e', 'f2s2', 'f1e', 'bucket', 'f2z', 'group', 'f2e')
LATE = {'c1s1': ('dm1', 'dm2', 'dm3'), 'c0s2': ('dkv1', 'dkv2', 'dkv3'), 'c2s1': ('dkv1', 'dkv2', 'dkv3'), 'c2s2': ('pieces1', 'pieces2', 'pieces3'), 'c1s2': ('d_norm1',), 'c2z0': ('d_norm1',)}
COST = {'project': 1.0, 'turn': 1.0, 'mix_forward': 9.0, 'gate_out': 2.0, 'feed_forward': 6.0, 'resid_back': 0.1, 'turn_up': 0.1, 'turn_out': 0.1, 'grads0': 0.1, 'grads1': 0.1, 'grads2': 0.1, 'mix_backward': 0.1, 'project_back': 0.1, 'tokens_back': 0.1, 'param_grads': 0.1, 'bucket_sum': 0.1, 'group_place': 0.1, 'finish': 1.0, 'fold_0s2': 0.1, 'fold_1s2': 0.1, 'fold_0z0': 0.1, 'fold_1z0': 0.1, 'fold_0z1': 0.1, 'fold_1z1': 0.1, 'parameter_fold': 0.1, 'place_pieces': 0.1}


class Order:
    def __init__(self):
        self.last = None

    def __call__(self, kernel, name, outs, *args, scratch=(), vmem=20 * MIB, smem=0, tag=None, **grid):
        grid.setdefault("in_specs", [SMEM] * smem + [VMEM] * (len(args) - smem))
        grid.setdefault("out_specs", [VMEM] * len(outs))
        args = list(args)
        if self.last is not None:
            args[smem] = after(args[smem], self.last)
        made = pl.pallas_call(
            kernel,
            out_shape=list(outs),
            scratch_shapes=list(scratch),
            compiler_params=pltpu.CompilerParams(vmem_limit_bytes=vmem),
            cost_estimate=pl.CostEstimate(
                flops=int(COST.get(tag or name, 2.0) * 1e9), bytes_accessed=0, transcendentals=0
            ),
            name=name,
            **grid,
        )(*args)
        self.last = made[0]
        return made


def shape(dtype, *dims):
    return jax.ShapeDtypeStruct(dims, dtype)


def trade(value, step):
    count = lax.axis_size("seq")
    return lax.ppermute(value, "seq", [(i, i ^ step) for i in range(count)])


def swap(value):
    return lax.ppermute(value, "ch", [(0, 1), (1, 0)])


def xor_place(x, index):
    count = x.shape[0]
    bit = 1
    while bit < count:
        y = x.reshape((count // (2 * bit), 2, bit) + x.shape[1:])
        flipped = jnp.concatenate([y[:, 1:], y[:, :1]], axis=1)
        x = jnp.where((index & bit) != 0, flipped, y).reshape(x.shape)
        bit *= 2
    return x


def tree_sum(parts):
    parts = list(parts)
    while len(parts) > 1:
        parts = [parts[i] + parts[i + 1] for i in range(0, len(parts), 2)]
    return parts[0]


def in_hbm(x):
    return pltpu.with_memory_space_constraint(x, pltpu.HBM)


def in_vmem(x):
    return pltpu.with_memory_space_constraint(x, pltpu.VMEM)


def after(x, *others):
    return lax.optimization_barrier((x,) + others)[0]


def dot(left, right, contract=(1, 0), out=F32):
    return lax.dot_general(
        left, right, (((contract[0],), (contract[1],)), ((), ())), preferred_element_type=F32
    ).astype(out)


def fdot(left, right, contract=(1, 0)):
    return lax.dot_general(
        left, right, (((contract[0],), (contract[1],)), ((), ())), preferred_element_type=F32, precision=HIGH
    )


def spread(scal, j, share, part, dtype=BF16):
    channel = lax.broadcasted_iota(jnp.int32, (share, LANES), 0)
    lane = lax.broadcasted_iota(jnp.int32, (share, LANES), 1)
    first = lax.bitwise_xor(scal[1], j) * part
    return jnp.where(jnp.where(lane < part, lane + first, -1) == channel, 1.0, 0.0).astype(dtype)


def lanes_of(member, share):
    return pl.ds(pl.multiple_of(member * share, LANES), share)


def centred(x):
    mean = jnp.mean(x, axis=-1, keepdims=True)
    cent = x - mean
    var = jnp.mean(cent * cent, axis=-1, keepdims=True)
    inverse = lax.rsqrt(var + 1e-05)
    return cent * inverse, inverse


def norm_back(d_norm, unit, inverse, gain):
    scaled = d_norm * gain
    first = jnp.mean(scaled, axis=-1, keepdims=True)
    second = jnp.mean(scaled * unit, axis=-1, keepdims=True)
    return (
        inverse * (scaled - first - unit * second),
        jnp.sum(d_norm * unit, axis=0, keepdims=True),
        jnp.sum(d_norm, axis=0, keepdims=True),
    )


def pick_pieces(scal, tokens, d_out, *refs):
    outs, sems = refs[:-1], refs[-1]
    copies = []
    for k, out in enumerate(outs):
        at = lax.bitwise_xor(scal[0], k)
        for i, ref in enumerate((tokens, d_out)):
            copies.append(pltpu.make_async_copy(ref.at[at], out.at[i], sems.at[2 * k + i]))
            copies[-1].start()
    for copy in copies:
        copy.wait()


def by_lanes(x):
    return jnp.concatenate([x[:, at : at + LANES] for at in range(0, x.shape[1], LANES)], axis=0)


def from_lanes(x, columns):
    rows = x.shape[0] // (columns // LANES)
    return jnp.concatenate([x[at : at + rows] for at in range(0, x.shape[0], rows)], axis=1)


def two_parts(x):
    high = x.astype(BF16)
    return jnp.concatenate([high, (x - high.astype(F32)).astype(BF16)], axis=0)


def one_part(x):
    half = x.shape[0] // 2
    return x[:half].astype(F32) + x[half:].astype(F32)


def assemble(*refs):
    for k, ref in enumerate(refs[:-1]):
        refs[-1][k] = ref[...]


def project(scal, gain, bias, w_query, w_key, w_value, *refs, buckets, span, group, part):
    own, other, x_ref, g_ref, norm_ref, half_ref, query_ref = refs[:7]
    kv = refs[7:]
    share = own.shape[-1]
    rows = buckets * span
    mine, others = lanes_of(scal[4], share), lanes_of(1 - scal[4], share)
    for k in range(buckets):
        at = pl.ds(k * span, span)
        for i, ref in enumerate((x_ref, g_ref)):
            ref[at, mine] = own[k, i]
            ref[at, others] = other[k, i]
    unit, _ = centred(x_ref[...].astype(F32))
    norm = (unit * gain[...] + bias[...]).astype(BF16)
    norm_ref[...] = norm
    half_ref[...] = norm_ref[pl.ds(pl.multiple_of(scal[4] * (rows // 2), rows // 2), rows // 2), :]
    keyed = dot(norm, w_key[...], out=BF16)
    valued = dot(norm, w_value[...], out=BF16)
    for j in range(group):
        hot = spread(scal, j, share, part)
        kv[j][0] = dot(keyed, hot, out=BF16).reshape(buckets, span, LANES)
        kv[j][1] = dot(valued, hot, out=BF16).reshape(buckets, span, LANES)
    query_ref[...] = dot(norm, w_query[...], out=BF16)


def gate_out(scal, query, w_out, *refs, rows, part):
    parts, (mixer_ref, gated_ref, branch_ref) = refs[:-3], refs[-3:]
    share = query.shape[-1]
    mixer = jnp.zeros((rows, share), F32)
    for j, ref in enumerate(parts):
        mixer = mixer + dot(ref[...].reshape(rows, LANES), spread(scal, j, share, part), (1, 1))
    mixer_ref[...] = mixer.astype(BF16)
    gated = (query[...].astype(F32) * mixer).astype(BF16)
    gated_ref[...] = gated
    branch_ref[...] = dot(gated, w_out[...], out=BF16)


def resid_of(x, branch, branch_other):
    return x[...].astype(F32) + (branch[...].astype(F32) + branch_other[...].astype(F32))


def feed_forward(
    scal, x, branch, branch_other, gain, bias, g, w_up, w_down, norm_ref, act_ref, d_hidden_ref, swap_ref, mine_ref, total, down
):
    step = pl.program_id(0)
    share = mine_ref.shape[-1]
    width = x.shape[-1]

    @pl.when(step == 0)
    def _():
        unit, _ = centred(resid_of(x, branch, branch_other))
        norm_ref[...] = (unit * gain[...] + bias[...]).astype(BF16)
        total[...] = jnp.zeros_like(total)
        down[...] = jnp.zeros_like(down)

    up = w_up[...]
    hidden = dot(norm_ref[...], up)
    d_act = dot(g[...], w_down[...], (1, 1))
    root = 0.7978845608028654
    square = hidden * hidden
    tanh = jnp.tanh(root * (hidden + 0.044715 * (square * hidden)))
    half = 0.5 * (1.0 + tanh)
    act = (hidden * half).astype(BF16)
    act_ref[...] = act
    slope = half + 0.5 * hidden * (1.0 - tanh * tanh) * (root + (3.0 * 0.044715 * root) * square)
    d_hidden = (d_act * slope).astype(BF16)
    d_hidden_ref[...] = d_hidden
    total[...] += dot(d_hidden, up, (1, 1))
    down[...] += dot(act, w_down[...])

    @pl.when(step == pl.num_programs(0) - 1)
    def _():
        mine, others = lanes_of(scal[4], share), lanes_of(1 - scal[4], share)
        swap_ref[:, :width] = total[...].astype(BF16)
        swap_ref[:, width:] = down[:, others].astype(BF16)
        resid = x[:, mine].astype(F32) + (branch[:, mine].astype(F32) + branch_other[:, mine].astype(F32))
        mine_ref[...] = resid + down[:, mine]


def resid_back(
    scal, x, branch, branch_other, mine, other, gain, g, w_out, query, mixer, *refs, buckets, span, group, part
):
    d_branch_ref, d_query_ref, d_mine_ref, vectors = refs[:4]
    outs = refs[4:]
    share = query.shape[-1]
    unit, inverse = centred(resid_of(x, branch, branch_other))
    width = x.shape[-1]
    d_norm2 = mine[:, :width].astype(F32) + other[:, :width].astype(F32)
    d_x, d_gain, d_bias = norm_back(d_norm2, unit, inverse, gain[...])
    d_resid = g[...].astype(F32) + d_x
    d_branch = d_resid.astype(BF16)
    d_branch_ref[...] = d_branch
    d_gated = dot(d_branch, w_out[...], (1, 1))
    d_mixer = (d_gated * query[...].astype(F32)).astype(BF16)
    for j in range(group):
        outs[j][...] = dot(d_mixer, spread(scal, j, share, part), out=BF16).reshape(buckets, span, LANES)
    d_query_ref[...] = (d_gated * mixer[...].astype(F32)).astype(BF16)
    vectors[0:1, :] = d_gain
    vectors[1:2, :] = d_bias
    d_mine_ref[...] = jnp.where(scal[4] == 0, d_resid[:, :share], d_resid[:, share:])


def project_back(scal, d_query, w_query, w_key, w_value, *refs, rows, part):
    parts, d_norm_ref = refs[:-1], refs[-1]
    share = d_query.shape[-1]
    sums = [jnp.zeros((rows, share), F32) for _ in range(2)]
    for j, ref in enumerate(parts):
        hot = spread(scal, j, share, part)
        for i in range(2):
            sums[i] = sums[i] + dot(ref[i].reshape(rows, LANES), hot, (1, 1))
    d_keyed, d_valued = sums[0].astype(BF16), sums[1].astype(BF16)
    d_norm_ref[...] = (
        dot(d_query[...], w_query[...], (1, 1))
        + dot(d_keyed, w_key[...], (1, 1))
        + dot(d_valued, w_value[...], (1, 1))
    ).astype(BF16)


def key_value_grads(scal, norm, mine, theirs, d_kv, total, *, buckets, group):
    rows = norm.shape[0]
    half = buckets // 2
    for i in range(2):
        grad = dot(norm[...], d_kv[0][i].reshape(rows, LANES), (0, 0))
        for j in range(1, group):
            for ref, member in ((mine[j - 1], scal[4]), (theirs[j - 1], 1 - scal[4])):
                right = d_kv[j][i, pl.ds(member * half, half)].reshape(rows // 2, LANES)
                grad = grad + dot(ref[...], right, (0, 0))
        total[:, LANES * i : LANES * i + LANES] = grad


def small_sum(mine, got, plain, fine):
    plains = mine[:plain].astype(F32) + got[:plain].astype(F32)
    return plains, one_part(mine[plain : plain + 2 * fine]) + one_part(got[plain : plain + 2 * fine])


def parameter_fold(mine, keep, got, send, keep_out, *, plain, fine):
    plains, fines = small_sum(mine, got, plain, fine)
    small = plain + 2 * fine
    send[pl.ds(0, plain), :] = plains.astype(BF16)
    send[pl.ds(plain, 2 * fine), :] = two_parts(fines)
    half = keep.shape[0] // 2
    keep_out[...] = keep[:half] + got[small : small + half].astype(F32)
    send[pl.ds(small, half), :] = (keep[half:] + got[small + half :].astype(F32)).astype(BF16)


def place_pieces(scal, *refs, span):
    pieces, (tokens_ref, block_ref, vector_ref) = refs[:-3], refs[-3:]
    share = tokens_ref.shape[-1]
    rows = span * (share // LANES)
    vec_rows = 2 * vector_ref.shape[0]
    vectors = []
    for k, ref in enumerate(pieces):
        at = lax.bitwise_xor(scal[0], k)
        tokens_ref[at] = from_lanes(ref[:rows], share).astype(F32)
        block_ref[at] = from_lanes(ref[rows : 2 * rows], share).astype(F32)
        vectors.append(one_part(ref[2 * rows : 2 * rows + vec_rows]))
    vector_ref[...] = tree_sum(vectors)


def bucket_sum(scal, vector, mine, keep, got, *outs, group, plain, fine):
    plain_sum, fine_sum = small_sum(mine, got, plain, fine)
    matrix = keep[...] + got[plain + 2 * fine :].astype(F32)
    matrix = from_lanes(matrix, 2 * LANES).astype(BF16)
    total = matrix.shape[0]
    block = total // group
    out_row = lax.broadcasted_iota(jnp.int32, (total, total), 0)
    in_row = lax.broadcasted_iota(jnp.int32, (total, total), 1)
    source = lax.bitwise_xor(out_row // block, scal[1]) * block + lax.rem(out_row, block)
    matrix = dot(jnp.where(source == in_row, 1.0, 0.0).astype(BF16), matrix, out=BF16)
    sums = jnp.concatenate([plain_sum.astype(BF16), two_parts(fine_sum), two_parts(vector[...])], axis=0)
    small = sums.shape[0]
    for j, out in enumerate(outs):
        out[pl.ds(0, small), :] = sums
        out[pl.ds(small, 2 * block), :] = by_lanes(matrix[j * block : j * block + block])


def group_place(scal, *refs, part, span, nstate, fine, vec):
    parts, (key_ref, value_ref, shift_ref, coef_ref, fine_ref, vec_ref) = refs[:-6], refs[-6:]
    share = shift_ref.shape[-1]
    sums = [jnp.zeros(key_ref.shape, F32) for _ in range(2)]
    shift = jnp.zeros(shift_ref.shape, F32)
    coef = jnp.zeros(coef_ref.shape, F32)
    fines, vectors = [], []
    block = key_ref.shape[0]
    for j, ref in enumerate(parts):
        hot = spread(scal, j, share, part)
        shift = shift + dot(ref[:span], hot, (1, 1))
        coef = coef + dot(hot, ref[span : span + nstate], (1, 1))
        first = span + nstate
        fines.append(one_part(ref[first : first + 2 * fine]))
        first += 2 * fine
        vectors.append(one_part(ref[first : first + 2 * vec]))
        first += 2 * vec
        for i in range(2):
            sums[i] = sums[i] + dot(ref[first + i * block : first + i * block + block], hot, (1, 1))
    key_ref[...] = sums[0]
    value_ref[...] = sums[1]
    shift_ref[...] = shift
    coef_ref[...] = coef
    fine_ref[...] = tree_sum(fines)
    vec_ref[...] = tree_sum(vectors)


def turn(*refs, pairs):
    for i in range(pairs):
        source, left, out = refs[2 * i], refs[2 * i + 1], refs[2 * pairs + i]
        width = left.shape[1]
        lane = lax.broadcasted_iota(jnp.int32, (width, LANES), 1)
        hot = jnp.concatenate(
            [jnp.where(source[...] == lane + m, 1.0, 0.0).astype(BF16) for m in range(0, width, LANES)], axis=1
        )
        out[...] = dot(hot, left[...], (1, 1), out=BF16)


def row_grads(*refs, streams):
    pairs = sum(len(s) for s in streams)
    i = 0
    for t, stream in enumerate(streams):
        send, keep = refs[2 * pairs + 2 * t], refs[2 * pairs + 2 * t + 1]
        at = 0
        for first, last in stream:
            turned, right = refs[2 * i], refs[2 * i + 1]
            half = turned.shape[0] // 2
            operand = right[:, first:last]
            send[:, at : at + last - first] = dot(turned[half:], operand, out=BF16)
            keep[:, at : at + last - first] = dot(turned[:half], operand, out=BF16)
            at += last - first
            i += 1


def finish(*refs, plan):
    sums = len(plan)
    outs = refs[2 * sums :]
    for i in range(sums):
        total = refs[2 * i][...].astype(F32) + refs[2 * i + 1][...].astype(F32)
        for first, last, out, at in plan[i]:
            outs[out][:, at : at + last - first] = total[:, first:last]


def fold(*refs, pairs):
    ins, outs = refs[: 2 * pairs], refs[2 * pairs :]
    at = 0
    for i in range(pairs):
        keep, got = ins[2 * i], ins[2 * i + 1]
        half, columns = keep.shape[0] // 2, keep.shape[1]
        if len(outs) == 2:
            here, columns_at = outs, pl.ds(at, columns)
        else:
            here, columns_at = outs[2 * i : 2 * i + 2], pl.ds(0, columns)
        here[0][:, columns_at] = (keep[half:].astype(F32) + got[half:].astype(F32)).astype(BF16)
        here[1][:, columns_at] = keep[:half].astype(F32) + got[:half].astype(F32)
        at += columns


def tokens_back(scal, x, d_norm, d_norm_other, gain, d_mine, block_mine, swapped, *refs, span):
    share = d_mine.shape[-1]
    width = x.shape[-1]
    unit, inverse = centred(x[...].astype(F32))
    d_norm1 = d_norm[...].astype(F32) + d_norm_other[...].astype(F32)
    d_x, d_gain, d_bias = norm_back(d_norm1, unit, inverse, gain[...])
    total = (d_mine[...] + jnp.where(scal[4] == 0, d_x[:, :share], d_x[:, share:])).astype(BF16)
    block = (block_mine[...] + swapped[:, width:].astype(F32)).astype(BF16)
    vectors = jnp.concatenate([by_lanes(d_gain), by_lanes(d_bias)], axis=0)
    high = vectors.astype(BF16).astype(F32)
    pad = -(4 * (width // LANES)) % 16
    vectors = jnp.concatenate([high, vectors - high] + [jnp.zeros((pad, LANES), F32)] * (pad > 0), axis=0).astype(BF16)
    rows = span * (share // LANES)
    for k, out in enumerate(refs):
        out[pl.ds(0, rows), :] = by_lanes(total[k * span : k * span + span])
        out[pl.ds(rows, rows), :] = by_lanes(block[k * span : k * span + span])
        out[pl.ds(2 * rows, vectors.shape[0]), :] = vectors


def rolled(x, r):
    return x if r == 0 else pltpu.roll(x, r % x.shape[0], 0)


def split(x):
    high = x.astype(BF16)
    return high, (x - high.astype(F32)).astype(BF16)


def split_dot(left, right):
    lh, ll = split(left)
    rh, rl = split(right)
    return jnp.dot(
        jnp.concatenate([lh, lh, ll], axis=1),
        jnp.concatenate([rh, rl, rh], axis=0),
        preferred_element_type=F32,
    )


def half_dot(left, right):
    lh, ll = split(left)
    rh = right.astype(BF16)
    return jnp.dot(
        jnp.concatenate([lh, ll], axis=1), jnp.concatenate([rh, rh], axis=0), preferred_element_type=F32
    )


def powers_by_step(rrow, span, reverse, shift):
    step = lax.broadcasted_iota(jnp.int32, (span, LANES), 0).astype(F32)
    step = (span - 1.0 - step) if reverse else step + shift
    return jnp.exp(-step * rrow)


def powers_by_state(rcol, span, reverse, shift):
    step = lax.broadcasted_iota(jnp.int32, (LANES, span), 1).astype(F32)
    step = (span - 1.0 - step) if reverse else step + shift
    return jnp.exp(-step * rcol[:, :span]), step


def chunk_row(scal, j, k, group, span):
    return pl.multiple_of(
        (lax.bitwise_xor(scal[0], k) * group + lax.bitwise_xor(scal[1], j)) * span, span
    )


def wide(ref, first, batch, span):
    return jnp.concatenate(
        [ref[pl.ds(pl.multiple_of((first + i) * span, span), span), :] for i in range(batch)], axis=1
    )


def mix_forward(scal, valid, tabs, rrow, taps, *refs, group, buckets, span, batch):
    kv = refs[:group]
    outs = refs[group : 2 * group]
    kf, vf, shifted_ref, mixed_ref, states, ysc, kern_ref = refs[2 * group :]
    limit = valid[scal[0]]
    rcol, scol, coefm, hm = tabs[0], tabs[1], tabs[3], tabs[4]
    eighths = span // 8
    chunks = group * buckets
    kern_ref[...] = split_dot(powers_by_step(rrow[...], span, False, 0.0), scol * coefm)
    w_end = powers_by_state(rcol, span, True, 0.0)[0] * scol[:, :span]
    p_out = powers_by_step(rrow[...], span, False, 1.0)
    decay = jnp.exp(-float(span) * rcol)
    kf[pl.ds(0, span), :] = jnp.zeros((span, LANES), F32)
    for j in range(group):
        for k in range(buckets):
            row = chunk_row(scal, j, k, group, span)
            kf[pl.ds(row + span, span), :] = kv[j][0, k].astype(F32)
            vf[pl.ds(row, span), :] = kv[j][1, k].astype(F32)
    row_id = lax.broadcasted_iota(jnp.int32, (span, LANES), 0)

    def filtered(c, carry):
        start = pl.multiple_of(c * span, span)
        x = kf[pl.ds(start, 2 * span), :]
        acc = jnp.zeros((span, LANES), F32)
        for r in range(8):
            xr = rolled(x, r)
            for q in range(eighths):
                acc = acc + taps[8 * q + r : 8 * q + r + 1, :] * xr[span - 8 * q : 2 * span - 8 * q]
        shifted_ref[pl.ds(start, span), :] = acc
        mixed_ref[pl.ds(start, span), :] = jnp.where(
            row_id + start < limit, acc * vf[pl.ds(start, span), :], 0.0
        )
        return carry

    lax.fori_loop(0, chunks, filtered, 0)

    def carried(turn, state):
        first = turn * batch
        ends = split_dot(w_end, wide(mixed_ref, first, batch, span))
        begins = []
        for i in range(batch):
            states[first + i] = state
            begins.append(coefm * state)
            state = decay * state + ends[:, LANES * i : LANES * i + LANES] * hm
        y = split_dot(p_out, jnp.concatenate(begins, axis=1))
        for i in range(batch):
            ysc[pl.ds(pl.multiple_of((first + i) * span, span), span), :] = y[:, LANES * i : LANES * i + LANES]
        return state

    lax.fori_loop(0, chunks // batch, carried, jnp.zeros((LANES, LANES), F32))

    def inner(c, carry):
        start = pl.multiple_of(c * span, span)
        mixed = mixed_ref[pl.ds(start, span), :]
        y = ysc[pl.ds(start, span), :]
        tails = [y[8 * i : 8 * i + 8] for i in range(eighths)]
        for r in range(8):
            mr = jnp.where(row_id >= r, rolled(mixed, r), 0.0)
            for q in range(eighths):
                weight = kern_ref[8 * q + r : 8 * q + r + 1, :]
                for i in range(q, eighths):
                    tails[i] = tails[i] + weight * mr[8 * (i - q) : 8 * (i - q) + 8]
        for i in range(eighths):
            ysc[pl.ds(start + 8 * i, 8), :] = tails[i]
        return carry

    lax.fori_loop(0, chunks, inner, 0)
    for j in range(group):
        for k in range(buckets):
            outs[j][k] = ysc[pl.ds(chunk_row(scal, j, k, group, span), span), :].astype(BF16)


def mix_backward(scal, valid, tabs, rrow, taps, vf, shifted_ref, *refs, group, buckets, span, batch):
    d_in = refs[:group]
    outs = refs[group : 2 * group]
    dmf, dsf, adj, dks, dvs, kern_ref = refs[2 * group :]
    limit = valid[scal[0]]
    rcol, scol, coefm = tabs[0], tabs[1], tabs[3]
    kern_ref[...] = split_dot(powers_by_step(rrow[...], span, False, 0.0), scol * coefm)
    p_rev = powers_by_step(rrow[...], span, True, 0.0)
    p_in = powers_by_state(rcol, span, False, 1.0)[0]
    decay = jnp.exp(-float(span) * rcol)
    chunks = group * buckets
    eighths = span // 8
    dsf[pl.ds(chunks * span, span), :] = jnp.zeros((span, LANES), F32)
    for j in range(group):
        for k in range(buckets):
            dmf[pl.ds(chunk_row(scal, j, k, group, span), span), :] = d_in[j][k].astype(F32)
    row_id = lax.broadcasted_iota(jnp.int32, (span, LANES), 0)

    def carried(turn, after):
        first = chunks - batch - turn * batch
        seeds = half_dot(p_in, wide(dmf, first, batch, span))
        ends = [None] * batch
        for i in reversed(range(batch)):
            adj[first + i] = after
            ends[i] = scol * after
            after = decay * after + coefm * seeds[:, LANES * i : LANES * i + LANES]
        y = split_dot(p_rev, jnp.concatenate(ends, axis=1))
        for i in range(batch):
            dks[pl.ds(pl.multiple_of((first + i) * span, span), span), :] = y[:, LANES * i : LANES * i + LANES]
        return after

    lax.fori_loop(0, chunks // batch, carried, jnp.zeros((LANES, LANES), F32))

    def chunk(turn, carry):
        start = pl.multiple_of((chunks - 1 - turn) * span, span)
        dm = dmf[pl.ds(start, span), :]
        y = dks[pl.ds(start, span), :]
        heads = [y[8 * i : 8 * i + 8] for i in range(eighths)]
        for r in range(8):
            mr = jnp.where(row_id < span - r, rolled(dm, -r), 0.0)
            for q in range(eighths):
                weight = kern_ref[8 * q + r : 8 * q + r + 1, :]
                for i in range(eighths - q):
                    heads[i] = heads[i] + weight * mr[8 * (i + q) : 8 * (i + q) + 8]
        d_mixed = jnp.where(row_id + start < limit, jnp.concatenate(heads, axis=0), 0.0)
        dvs[pl.ds(start, span), :] = d_mixed * shifted_ref[pl.ds(start, span), :]
        dsf[pl.ds(start, span), :] = d_mixed * vf[pl.ds(start, span), :]
        x = dsf[pl.ds(start, 2 * span), :]
        acc = jnp.zeros((span, LANES), F32)
        for r in range(8):
            xr = rolled(x, -r)
            for q in range(eighths):
                acc = acc + taps[8 * q + r : 8 * q + r + 1, :] * xr[8 * q : 8 * q + span]
        dks[pl.ds(start, span), :] = acc
        return carry

    lax.fori_loop(0, chunks, chunk, 0)
    for j in range(group):
        for k in range(buckets):
            row = chunk_row(scal, j, k, group, span)
            outs[j][0, k] = dks[pl.ds(row, span), :].astype(BF16)
            outs[j][1, k] = dvs[pl.ds(row, span), :].astype(BF16)


def param_grads(scal, tabs, rrow, kf, mixed_ref, states, dmf, dsf, adj, vectors, norm, *refs, span, batch, nstate, group, buckets):
    mine, theirs = refs[: group - 1], refs[group - 1 : 2 * group - 2]
    d_kv = refs[2 * group - 2 : 3 * group - 2]
    first = 3 * group - 2
    send, keep, out, total, coef_out, rate_out, acc_s, acc_k = refs[first:]
    key_value_grads(scal, norm, mine, theirs, d_kv, total, buckets=buckets, group=group)
    rcol, scol, dscol, coefm, hm = tabs[0], tabs[1], tabs[2], tabs[3], tabs[4]
    p_in, step = powers_by_state(rcol, span, False, 1.0)
    into = jnp.concatenate([p_in, p_in * step], axis=0)
    p_end, step = powers_by_state(rcol, span, True, 0.0)
    ends = jnp.concatenate([p_end, p_end * step], axis=0)
    p_kern, step = powers_by_state(rcol, span, False, 0.0)
    decay = float(span) * jnp.exp(-float(span) * rcol)
    chunks = mixed_ref.shape[0] // span
    eighths = span // 8
    acc_s[...] = jnp.zeros_like(acc_s)
    acc_k[...] = jnp.zeros_like(acc_k)
    coef_out[...] = jnp.zeros_like(coef_out)
    rate_out[...] = jnp.zeros_like(rate_out)
    row_id = lax.broadcasted_iota(jnp.int32, (span, LANES), 0)

    def chunk(c, carry):
        start = pl.multiple_of(c * span, span)
        x = kf[pl.ds(start, 2 * span), :]
        ds = dsf[pl.ds(start, span), :]
        mixed = mixed_ref[pl.ds(start, span), :]
        dm = dmf[pl.ds(start, span), :]
        for r in range(8):
            xr = rolled(x, r)
            mr = jnp.where(row_id >= r, rolled(mixed, r), 0.0)
            for q in range(eighths):
                whole = ds * xr[span - 8 * q : 2 * span - 8 * q]
                acc_s[8 * q + r] += jnp.sum(whole.reshape(eighths, 8, LANES), axis=0)
                part = dm[8 * q :] * mr[: span - 8 * q]
                acc_k[8 * q + r] += jnp.sum(part.reshape(eighths - q, 8, LANES), axis=0)
        return carry

    lax.fori_loop(0, chunks, chunk, 0)

    def rates(turn, carry):
        first = turn * batch
        z = half_dot(into, wide(dmf, first, batch, span))
        u = split_dot(ends, wide(mixed_ref, first, batch, span))
        coef = coef_out[...]
        rate = rate_out[...]
        for i in range(batch):
            state, after = states[first + i], adj[first + i]
            at = slice(LANES * i, LANES * i + LANES)
            coef = coef + state * z[:LANES, at]
            rate = (
                rate
                + after * (dscol * u[:LANES, at] - scol * u[LANES:, at] - decay * state)
                - coefm * state * z[LANES:, at]
            )
        coef_out[...] = coef
        rate_out[...] = rate
        return carry

    lax.fori_loop(0, chunks // batch, rates, 0)
    out[pl.ds(0, span), :] = jnp.sum(acc_s[...], axis=1)
    gk = jnp.sum(acc_k[...], axis=1)
    m = split_dot(jnp.concatenate([p_kern, p_kern * step], axis=0), gk)
    m0, m1 = m[:LANES], m[LANES:]
    coef = (coef_out[...] + scol * m0) * hm
    out[pl.ds(span, nstate), :] = coef[:nstate] + coef[nstate:]
    at = span + nstate
    pieces_across = vectors.shape[1] // LANES
    for v in range(2):
        for i in range(pieces_across):
            out[pl.ds(at + v * pieces_across + i, 1), :] = vectors[v : v + 1, LANES * i : LANES * i + LANES]
    at = out.shape[0] - 8
    done = span + nstate + 2 * pieces_across
    out[pl.ds(done, at - done), :] = jnp.zeros((at - done, LANES), F32)
    rate = rate_out[...] + coefm * (dscol * m0 - scol * m1)
    rate = jnp.broadcast_to(jnp.sum(rate, axis=1, keepdims=True), (LANES, LANES))
    row = lax.broadcasted_iota(jnp.int32, (LANES, LANES), 0)
    lane = lax.broadcasted_iota(jnp.int32, (LANES, LANES), 1)
    rate = jnp.where(lax.rem(row, nstate) == lane, rate, 0.0)
    head = lax.broadcasted_iota(jnp.int32, (8, LANES), 0)
    owner = lax.broadcasted_iota(jnp.int32, (8, LANES), 1) // nstate + scal[3]
    out[pl.ds(at, 8), :] = fdot(jnp.where(head == owner, 1.0, 0.0), rate)
    plain = out[pl.ds(0, span + nstate), :].astype(BF16)
    fine = two_parts(out[pl.ds(span + nstate, out.shape[0] - span - nstate), :])
    plane = total.shape[0] // buckets
    small = plain.shape[0] + fine.shape[0]
    send[pl.ds(0, plain.shape[0]), :] = plain
    send[pl.ds(plain.shape[0], fine.shape[0]), :] = fine
    for k in range(buckets):
        at = pl.multiple_of(lax.bitwise_xor(scal[0], k) * plane, plane)
        rows = total[pl.ds(at, plane), :]
        if k % 2:
            send[pl.ds(small + (k // 2) * 2 * plane, 2 * plane), :] = by_lanes(rows.astype(BF16))
        else:
            keep[pl.ds((k // 2) * 2 * plane, 2 * plane), :] = by_lanes(rows)


def body(
    tokens,
    valid_len,
    ln1_gain,
    ln1_bias,
    w_query,
    w_key,
    w_value,
    shift_kernel,
    ssm_rate,
    ssm_coef,
    w_out,
    ln2_gain,
    ln2_bias,
    w_up,
    w_down,
    d_out,
):
    buckets, span, share = tokens.shape
    rows = buckets * span
    heads, nstate = ssm_rate.shape
    head_width = share // heads
    width, hidden = w_up.shape
    count = lax.axis_size("seq")
    group = count // buckets
    part = share // group
    place = lax.axis_index("seq")
    member = lax.axis_index("ch")
    b, g = place // group, place % group
    first_head = (g * part) // head_width
    scal = jnp.stack([b, g, place, first_head, member]).astype(jnp.int32)
    as_row = lambda v: v.reshape(1, -1)
    ANY = pl.BlockSpec(memory_space=pl.ANY)

    def trade_buckets(pieces):
        return [pieces[0]] + [trade(pieces[k], k * group) for k in range(1, buckets)]

    def trade_group(blocks):
        return [blocks[0]] + [trade(blocks[j], j) for j in range(1, group)]

    call = Order()

    own = call(
        pick_pieces,
        "pick_pieces",
        [pltpu.VMEM((2, span, share), BF16)] * buckets,
        scal,
        in_hbm(tokens),
        in_hbm(d_out),
        scratch=[pltpu.SemaphoreType.DMA((2 * buckets,))],
        in_specs=[SMEM, ANY, ANY],
        smem=1,
    )
    own = trade_buckets(own)
    (own,) = call(assemble, "assemble", [shape(BF16, buckets, 2, span, share)], *own)
    other = swap(own)

    lane = jnp.arange(LANES, dtype=jnp.int32)
    row_head = first_head + lane // nstate
    hm = (row_head[:, None] == ((g * part + lane) // head_width)[None, :]) & (lane < part)[None, :]
    hm = hm.astype(F32)
    two = lax.dynamic_slice_in_dim(
        jnp.concatenate([ssm_rate, ssm_rate[-1:]], axis=0), first_head, 2, 0
    ).reshape(1, 2 * nstate)
    rate_col = jnp.broadcast_to(two.reshape(-1, 1), (LANES, LANES))
    scale_col = jnp.sqrt(-jnp.expm1(-2.0 * rate_col))
    dscale_col = jnp.exp(-2.0 * rate_col) / scale_col
    coef_part = lax.dynamic_slice_in_dim(ssm_coef, g * part, part, 0)
    coef_part = jnp.pad(coef_part, ((0, LANES - part), (0, 0))).T
    coefm = jnp.concatenate([coef_part, coef_part], axis=0) * hm
    tabs = jnp.stack([rate_col, scale_col, dscale_col, coefm, hm])
    taps = jnp.pad(lax.dynamic_slice_in_dim(shift_kernel, g * part, part, 1), ((0, 0), (0, LANES - part)))

    bits = [1 << i for i in range(count.bit_length() - 1)]
    row_block = width // count

    def source_of(order):
        rel = jnp.arange(width, dtype=jnp.int32)
        at = rel // row_block
        target = jnp.zeros_like(at)
        for i, step in enumerate(order):
            target = target + ((at >> (len(order) - 1 - i)) & 1) * step
        source = (target ^ place) * row_block + rel % row_block
        return jnp.broadcast_to(source[:, None], (width, LANES))

    order_a = bits
    order_b = [bits[1], bits[0]] + bits[2:]
    source_a, source_b = source_of(order_a), source_of(order_b)
    turned_shape = shape(BF16, width, rows)
    half = width // 2

    def turned(*pairs, tag):
        operands = [a for p in pairs for a in p]
        return call(
            functools.partial(turn, pairs=len(pairs)), "turn", [turned_shape] * len(pairs), *operands, tag=tag
        )

    def grads(streams, tag):
        outs = [shape(BF16, half, sum(p[3] - p[2] for p in st)) for st in streams for _ in range(2)]
        operands = [a for st in streams for p in st for a in p[:2]]
        columns = [[p[2:] for p in st] for st in streams]
        return call(functools.partial(row_grads, streams=columns), "row_grads", outs, *operands, tag=tag)

    def folded(ins, joined, tag):
        pairs = len(ins) // 2
        rows_out = ins[0].shape[0] // 2
        columns = [a.shape[1] for a in ins[::2]]
        if rows_out % 16:
            totals = [ins[2 * i].astype(F32) + ins[2 * i + 1].astype(F32) for i in range(pairs)]
            if joined:
                totals = [jnp.concatenate(totals, axis=1)]
            return [v for t in totals for v in (t[rows_out:].astype(BF16), t[:rows_out])]
        if joined:
            columns = [sum(columns)]
        outs = [shape(kind, rows_out, c) for c in columns for kind in (BF16, F32)]
        return call(functools.partial(fold, pairs=pairs), "fold", outs, *ins, tag=tag)

    wide_rows, narrow_rows = shape(BF16, rows, width), shape(BF16, rows, share)
    pair = shape(BF16, 2, buckets, span, LANES)
    small = shape(BF16, buckets, span, LANES)
    sizes = dict(buckets=buckets, span=span, group=group, part=part)
    x, grad_full, norm1, norm1_half, query, *kv = call(
        functools.partial(project, **sizes),
        "project",
        [pltpu.HBM((rows, width), BF16)] * 3 + [pltpu.HBM((rows // 2, width), BF16), pltpu.HBM((rows, share), BF16)] + [pair] * group,
        scal, as_row(ln1_gain), as_row(ln1_bias), w_query, w_key, w_value, own, other,
        smem=1,
    )
    kv = trade_group(kv)
    mine_halves = [trade(norm1_half, j) for j in range(1, group)]
    turned_b, turned_q = turned((source_b, grad_full), (source_b, norm1), tag="turn")
    length = count * span
    long, longer, per_chunk = shape(F32, length, LANES), shape(F32, length + span, LANES), shape(F32, count, LANES, LANES)
    mix_sizes = dict(group=group, buckets=buckets, span=span, batch=min(count, 8))
    mix_vmem = min(14 * MIB + 12 * length * LANES * 4, 60 * MIB)
    forward_out = call(
        functools.partial(mix_forward, **mix_sizes),
        "mix_forward",
        [small] * group + [longer, long, long, long, per_chunk],
        scal, valid_len, tabs, two, taps, *kv,
        scratch=[pltpu.VMEM((length, LANES), F32), pltpu.VMEM((span, LANES), F32)],
        smem=2,
        vmem=mix_vmem,
    )
    kf, vf, shifted, mixed, states = forward_out[group:]
    mixer_parts = trade_group(forward_out[:group])
    mixer, gated, branch = call(
        functools.partial(gate_out, rows=rows, part=part),
        "gate_out",
        [narrow_rows, narrow_rows, wide_rows],
        scal, after(query, *mine_halves), w_out, *mixer_parts,
        smem=1,
    )
    branch_other = swap(branch)
    other_halves = [swap(p) for p in mine_halves]
    steps = 4
    block = hidden // steps
    fixed = pl.BlockSpec((rows, width), lambda i: (0, 0))
    vector = pl.BlockSpec((1, width), lambda i: (0, 0))
    column = pl.BlockSpec((rows, block), lambda i: (0, i))
    norm2, act, d_hidden, to_swap, block_mine = call(
        feed_forward,
        "feed_forward",
        [wide_rows, shape(BF16, rows, hidden), shape(BF16, rows, hidden), shape(BF16, rows, width + share)]
        + [shape(F32, rows, share)],
        scal, x, branch, branch_other, as_row(ln2_gain), as_row(ln2_bias), grad_full, w_up, w_down,
        scratch=[pltpu.VMEM((rows, width), F32)] * 2,
        grid=(steps,),
        in_specs=[SMEM, fixed, fixed, fixed, vector, vector, fixed]
        + [pl.BlockSpec((width, block), lambda i: (0, i)), pl.BlockSpec((block, width), lambda i: (i, 0))],
        out_specs=[fixed, column, column, pl.BlockSpec((rows, width + share), lambda i: (0, 0))]
        + [pl.BlockSpec((rows, share), lambda i: (0, 0))],
        smem=1,
    )
    swapped = swap(to_swap)

    plane_rows = width // buckets
    vector_rows = 2 * (width // LANES)
    small_rows = -(-(span + nstate + vector_rows + 8) // 16) * 16
    fine = small_rows - span - nstate
    small_out = span + nstate + 2 * fine
    vec_rows = 4 * (width // LANES)
    piece_rows = 2 * span * (share // LANES) + -(-vec_rows // 16) * 16
    block_rows = span + nstate + 2 * fine + vec_rows + 2 * row_block
    ours = shape(F32, buckets, span, share)
    chunks = len(CUTS) + 1
    cuts = [0] + [int(c * hidden) // LANES * LANES for c in CUTS] + [hidden]
    got = {}

    def sent(name, value, move):
        others = [got[n] for n in LATE.get(name, ())]
        got[name] = move(after(value, *others) if others else value)
        return got[name]

    def sent_all(name, values, move):
        moved = move([after(values[0], *[got[n] for n in LATE[name]])] + list(values[1:]) if name in LATE else values)
        got[name] = moved[1]
        for i, value in enumerate(moved[1:]):
            got[name + str(i + 1)] = value
        return moved

    def late(name, values):
        others = [got[n] for n in LATE.get(name, ())]
        return [after(v, *others) for v in values] if others else list(values)

    def resid_step():
        got["d_branch"], got["d_query"], got["d_mine"], got["vectors2"], *d_mixer = call(
            functools.partial(resid_back, **sizes),
            "resid_back",
            [wide_rows, narrow_rows, shape(F32, rows, share), shape(F32, 2, width)] + [small] * group,
            scal, x, branch, branch_other, to_swap, swapped, as_row(ln2_gain), grad_full, w_out, query, mixer,
            smem=1,
        )
        moved = trade_group(late("dm", d_mixer))
        got["d_mixer"] = moved
        for i in range(1, group):
            got["dm%d" % i] = moved[i]

    def turn_up_step():
        (got["turned_a"],) = turned((source_a, norm2), tag="turn_up")

    def turn_out_step():
        (got["turned_o"],) = turned((source_a, got["d_branch"]), tag="turn_out")

    def grads_step(i):
        streams = [[(got["turned_a"], d_hidden, cuts[i], cuts[i + 1])], [(turned_b, act, cuts[i], cuts[i + 1])]]
        if i == OUT_IN:
            streams[0].append((got["turned_o"], gated, 0, share))
            streams[1].append((turned_q, got["d_query"], 0, share))
        name = "c%d" % i
        send_a, keep_a, send_b, keep_b = grads(streams, "grads%d" % i)
        send_a, send_b = late(name + "s1", [send_a, send_b])
        got[name] = [keep_a, trade(send_a, order_a[0]), keep_b, trade(send_b, order_b[0])]
        got[name + "s1"], got[name + "s1b"] = got[name][1], got[name][3]

    def second_step(i):
        name = "c%d" % i
        send_a, keep_a, send_b, keep_b = folded(got[name], False, "fold_%ds2" % i)
        send_a, send_b = late(name + "s2", [send_a, send_b])
        got[name] = [keep_a, trade(send_a, order_a[1]), keep_b, trade(send_b, order_b[1])]
        got[name + "s2"], got[name + "s2b"] = got[name][1], got[name][3]

    def joint_step(i, at):
        name = "c%d" % i
        ins = got[name]
        if at == 0:
            for other in MERGE.get(i, ()):
                ins = got["c%d" % other] + ins
        send, keep = folded(ins, True, "fold_%dz%d" % (i, at))
        (send,) = late("%sz%d" % (name, at), [send])
        got[name] = [keep, trade(send, bits[2 + at])]
        got["%sz%d" % (name, at)] = got[name][1]

    def mixer_step():
        outs = call(
            functools.partial(mix_backward, **mix_sizes),
            "mix_backward",
            [pair] * group + [long, longer, per_chunk],
            scal, valid_len, tabs, two, taps, vf, shifted, *got["d_mixer"],
            scratch=[pltpu.VMEM((length, LANES), F32), pltpu.VMEM((length, LANES), F32), pltpu.VMEM((span, LANES), F32)],
            smem=2,
            vmem=mix_vmem,
        )
        got["own_kv"], (got["dmf"], got["dsf"], got["adj"]) = outs[:group], outs[group:]
        got["mixer"] = outs[0]
        got["d_kv"] = trade_group(late("dkv", outs[:group]))
        for i in range(1, group):
            got["dkv%d" % i] = got["d_kv"][i]

    def project_step():
        (d_norm1,) = call(
            functools.partial(project_back, rows=rows, part=part), "project_back", [wide_rows],
            scal, got["d_query"], w_query, w_key, w_value, *got["d_kv"], smem=1,
        )
        got["d_norm1"], got["d_norm1_other"] = d_norm1, swap(d_norm1)

    def tokens_step():
        pieces = call(
            functools.partial(tokens_back, span=span),
            "tokens_back",
            [shape(BF16, piece_rows, LANES)] * buckets,
            scal, x, got["d_norm1"], got["d_norm1_other"], as_row(ln1_gain), got["d_mine"], block_mine, swapped,
            smem=1,
        )
        got["tokens"] = pieces[0]
        got["rows"] = trade_buckets(late("pieces", pieces))
        for i in range(1, buckets):
            got["pieces%d" % i] = got["rows"][i]

    def parameters_step():
        kept = buckets // 2 * 2 * plane_rows
        send, keep = call(
            functools.partial(param_grads, span=span, batch=mix_sizes["batch"], nstate=nstate, group=group, buckets=buckets),
            "param_grads",
            [shape(BF16, small_out + kept, LANES), shape(F32, kept, LANES)],
            scal, tabs, two, kf, mixed, states, got["dmf"], got["dsf"], got["adj"], got["vectors2"],
            norm1, *mine_halves, *other_halves, *got["own_kv"],
            scratch=[pltpu.VMEM((small_rows, LANES), F32), pltpu.VMEM((width, 2 * LANES), F32)]
            + [pltpu.VMEM((LANES, LANES), F32)] * 2
            + [pltpu.VMEM((span, 8, LANES), F32)] * 2,
            smem=1,
            vmem=mix_vmem,
        )
        got["parameters"] = send
        (send,) = late("p0", [send])
        got["p"] = [send, keep, trade(send, group)]
        got["p0"] = got["p"][2]

    def parameter_fold_step(at):
        kept = got["p"][1].shape[0] // 2
        send, keep = call(
            functools.partial(parameter_fold, plain=span + nstate, fine=fine),
            "parameter_fold",
            [shape(BF16, small_out + kept, LANES), shape(F32, kept, LANES)],
            *got["p"],
        )
        (send,) = late("p%d" % at, [send])
        got["p"] = [send, keep, trade(send, group << at)]
        got["p%d" % at] = got["p"][2]

    def place_step():
        got["grad_tokens"], got["block_out"], got["vector"] = call(
            functools.partial(place_pieces, span=span),
            "place_pieces",
            [ours, ours, shape(F32, vector_rows, LANES)],
            scal, *got["rows"],
            smem=1,
        )

    def bucket_step():
        blocks = call(
            functools.partial(bucket_sum, group=group, plain=span + nstate, fine=fine),
            "bucket_sum",
            [shape(BF16, block_rows, LANES)] * group,
            scal, got["vector"], *got["p"],
            smem=1,
        )
        got["blocks"] = trade_group(late("plane", blocks))

    def group_step():
        got["group"] = call(
            functools.partial(group_place, part=part, span=span, nstate=nstate, fine=fine, vec=vector_rows),
            "group_place",
            [shape(F32, row_block, share)] * 2
            + [shape(F32, span, share), shape(F32, share, nstate), shape(F32, fine, LANES), shape(F32, vector_rows, LANES)],
            scal, *got["blocks"],
            smem=1,
        )

    named = dict(
        resid=resid_step, turn_up=turn_up_step, turn_out=turn_out_step, mixer=mixer_step, project=project_step,
        tokens=tokens_step, parameters=parameters_step, place=place_step, bucket=bucket_step, group=group_step,
    )
    for name in ORDER:
        if name in named:
            named[name]()
        elif name == "pe":
            for at in range(1, buckets.bit_length() - 1):
                parameter_fold_step(at)
        elif name.startswith("g"):
            grads_step(int(name[1:]))
        else:
            i, kind = int(name[1]), name[2:]
            if kind == "s2":
                second_step(i)
            elif kind == "z":
                joint_step(i, 0)
            else:
                for at in range(1, len(bits) - 2):
                    joint_step(i, at)
    plan, ends = [], []
    for i in range(chunks):
        if any(i in m for m in MERGE.values()):
            continue
        columns, at = [], 0
        for c in [*reversed(MERGE.get(i, ())), i]:
            for stream in range(2):
                columns.append((at, at + cuts[c + 1] - cuts[c], stream, cuts[c]))
                at += cuts[c + 1] - cuts[c]
                if c == OUT_IN:
                    columns.append((at, at + share, 2 + stream, 0))
                    at += share
        plan.append(columns)
        ends += got["c%d" % i]
    grad_up, grad_down, grad_out, grad_query = call(
        functools.partial(finish, plan=plan),
        "finish",
        [shape(F32, row_block, hidden)] * 2 + [shape(F32, row_block, share)] * 2,
        *ends,
    )
    grad_down, grad_out = grad_down.T, grad_out.T
    grad_key, grad_value, grad_shift, grad_coef, rest, vectors1 = got["group"]
    block_out, grad_tokens = got["block_out"], got["grad_tokens"]
    grad_g2, grad_c2 = rest[:vector_rows].reshape(2, width)
    grad_rate = rest[fine - 8 : fine - 8 + heads, :nstate]
    grad_g1, grad_c1 = vectors1.reshape(2, width)
    return (
        block_out,
        grad_tokens,
        grad_g1,
        grad_c1,
        grad_query,
        grad_key,
        grad_value,
        grad_shift,
        grad_rate,
        grad_coef,
        grad_out,
        grad_g2,
        grad_c2,
        grad_up,
        grad_down,
    )


def solution(mesh):
    in_specs = (
        P(None, "seq", "ch"),
        P(),
        P(),
        P(),
        P(None, "ch"),
        P(None, "ch"),
        P(None, "ch"),
        P(None, "ch"),
        P("ch", None),
        P("ch", None),
        P("ch", None),
        P(),
        P(),
        P(None, "ch"),
        P("ch", None),
        P(None, "seq", "ch"),
    )
    out_specs = (
        P(None, "seq", "ch"),
        P(None, "seq", "ch"),
        P(),
        P(),
        P("seq", "ch"),
        P("seq", "ch"),
        P("seq", "ch"),
        P(None, "ch"),
        P("ch", None),
        P("ch", None),
        P("ch", "seq"),
        P(),
        P(),
        P("seq", "ch"),
        P("ch", "seq"),
    )
    return jax.shard_map(body, mesh=mesh, in_specs=in_specs, out_specs=out_specs, check_vma=False)
```

```python
import functools

import jax
import jax.numpy as jnp
from jax import lax
from jax.experimental import pallas as pl
from jax.experimental.pallas import tpu as pltpu
from jax.sharding import PartitionSpec as P

LANES = 128
HIGH = lax.Precision.HIGHEST
F32 = jnp.float32
BF16 = jnp.bfloat16
VMEM = pl.BlockSpec(memory_space=pltpu.VMEM)
SMEM = pl.BlockSpec(memory_space=pltpu.SMEM)
MIB = 1024 * 1024

CUTS = (0.34, 0.67)
OUT_IN = 2
MERGE = {}
ORDER = (
    "turn_up", "g0", "resid", "g1", "turn_out", "f0s2", "mixer", "f0z", "t1s1", "g2", "f0e", "project", "f1s2", "t2s1",
    "tokens", "parameters", "place", "t1s2", "f2s2", "pe", "f1z", "x0", "bucket", "f1e", "f2z", "f2e", "group",
)
LATE = {
    "c2s1": ('d_norm1',),
}
COST = dict(
    project=1.0, turn=1.0, mix_forward=9.0, gate_out=2.0, feed_forward=0.1, resid_back=0.1, turn_up=0.1, turn_out=0.1,
    grads0=0.1, grads1=0.1, grads2=0.1, mix_backward=10.0, project_back=6.0, tokens_back=0.1, param_grads=10.0, bucket_sum=0.1,
    group_place=0.1, finish=1.0, fold_0s2=0.1, fold_1s2=0.1, fold_0z0=0.1, fold_1z0=0.1, fold_0z1=0.1, fold_1z1=0.1,
    parameter_fold=0.1, place_pieces=0.1,
)


class Order:
    def __init__(self):
        self.last = None

    def __call__(self, kernel, name, outs, *args, scratch=(), vmem=20 * MIB, smem=0, tag=None, **grid):
        grid.setdefault("in_specs", [SMEM] * smem + [VMEM] * (len(args) - smem))
        grid.setdefault("out_specs", [VMEM] * len(outs))
        args = list(args)
        if self.last is not None:
            args[smem] = after(args[smem], self.last)
        made = pl.pallas_call(
            kernel,
            out_shape=list(outs),
            scratch_shapes=list(scratch),
            compiler_params=pltpu.CompilerParams(vmem_limit_bytes=vmem),
            cost_estimate=pl.CostEstimate(
                flops=int(COST.get(tag or name, 2.0) * 1e9), bytes_accessed=0, transcendentals=0
            ),
            name=name,
            **grid,
        )(*args)
        self.last = made[0]
        return made


def shape(dtype, *dims):
    return jax.ShapeDtypeStruct(dims, dtype)


def trade(value, step):
    count = lax.axis_size("seq")
    return lax.ppermute(value, "seq", [(i, i ^ step) for i in range(count)])


def swap(value):
    return lax.ppermute(value, "ch", [(0, 1), (1, 0)])


def xor_place(x, index):
    count = x.shape[0]
    bit = 1
    while bit < count:
        y = x.reshape((count // (2 * bit), 2, bit) + x.shape[1:])
        flipped = jnp.concatenate([y[:, 1:], y[:, :1]], axis=1)
        x = jnp.where((index & bit) != 0, flipped, y).reshape(x.shape)
        bit *= 2
    return x


def tree_sum(parts):
    parts = list(parts)
    while len(parts) > 1:
        parts = [parts[i] + parts[i + 1] for i in range(0, len(parts), 2)]
    return parts[0]


def in_hbm(x):
    return pltpu.with_memory_space_constraint(x, pltpu.HBM)


def in_vmem(x):
    return pltpu.with_memory_space_constraint(x, pltpu.VMEM)


def after(x, *others):
    return lax.optimization_barrier((x,) + others)[0]


def dot(left, right, contract=(1, 0), out=F32):
    return lax.dot_general(
        left, right, (((contract[0],), (contract[1],)), ((), ())), preferred_element_type=F32
    ).astype(out)


def fdot(left, right, contract=(1, 0)):
    return lax.dot_general(
        left, right, (((contract[0],), (contract[1],)), ((), ())), preferred_element_type=F32, precision=HIGH
    )


def spread(scal, j, share, part, dtype=BF16):
    channel = lax.broadcasted_iota(jnp.int32, (share, LANES), 0)
    lane = lax.broadcasted_iota(jnp.int32, (share, LANES), 1)
    first = lax.bitwise_xor(scal[1], j) * part
    return jnp.where(jnp.where(lane < part, lane + first, -1) == channel, 1.0, 0.0).astype(dtype)


def lanes_of(member, share):
    return pl.ds(pl.multiple_of(member * share, LANES), share)


def centred(x):
    mean = jnp.mean(x, axis=-1, keepdims=True)
    cent = x - mean
    var = jnp.mean(cent * cent, axis=-1, keepdims=True)
    inverse = lax.rsqrt(var + 1e-05)
    return cent * inverse, inverse


def norm_back(d_norm, unit, inverse, gain):
    scaled = d_norm * gain
    first = jnp.mean(scaled, axis=-1, keepdims=True)
    second = jnp.mean(scaled * unit, axis=-1, keepdims=True)
    return (
        inverse * (scaled - first - unit * second),
        jnp.sum(d_norm * unit, axis=0, keepdims=True),
        jnp.sum(d_norm, axis=0, keepdims=True),
    )


def pick_pieces(scal, tokens, d_out, *refs):
    outs, sems = refs[:-1], refs[-1]
    half = len(outs) // 2
    copies = []
    for k in range(half):
        at = lax.bitwise_xor(scal[0], k)
        for i, ref in enumerate((tokens, d_out)):
            copies.append(pltpu.make_async_copy(ref.at[at], outs[half * i + k], sems.at[2 * k + i]))
            copies[-1].start()
    for copy in copies:
        copy.wait()


def by_lanes(x):
    return jnp.concatenate([x[:, at : at + LANES] for at in range(0, x.shape[1], LANES)], axis=0)


def from_lanes(x, columns):
    rows = x.shape[0] // (columns // LANES)
    return jnp.concatenate([x[at : at + rows] for at in range(0, x.shape[0], rows)], axis=1)


def two_parts(x):
    high = x.astype(BF16)
    return jnp.concatenate([high, (x - high.astype(F32)).astype(BF16)], axis=0)


def one_part(x):
    half = x.shape[0] // 2
    return x[:half].astype(F32) + x[half:].astype(F32)


def assemble(*refs):
    rows = refs[0].shape[0]
    for k, ref in enumerate(refs[:-1]):
        refs[-1][pl.ds(k * rows, rows), :] = ref[...]


def join(scal, own, other, out):
    share = own.shape[-1]
    out[:, lanes_of(scal[4], share)] = own[...]
    out[:, lanes_of(1 - scal[4], share)] = other[...]


def project(scal, gain, bias, w_query, w_key, w_value, *refs, buckets, span, group, part):
    own, other, x_ref, norm_ref, half_ref, query_ref = refs[:6]
    kv = refs[6:]
    share = own.shape[-1]
    rows = buckets * span
    mine, others = lanes_of(scal[4], share), lanes_of(1 - scal[4], share)
    x_ref[:, mine] = own[...]
    x_ref[:, others] = other[...]
    unit, _ = centred(x_ref[...].astype(F32))
    norm = (unit * gain[...] + bias[...]).astype(BF16)
    norm_ref[...] = norm
    half_ref[...] = norm_ref[pl.ds(pl.multiple_of(scal[4] * (rows // 2), rows // 2), rows // 2), :]
    keyed = dot(norm, w_key[...], out=BF16)
    valued = dot(norm, w_value[...], out=BF16)
    for j in range(group):
        hot = spread(scal, j, share, part)
        kv[j][0] = dot(keyed, hot, out=BF16).reshape(buckets, span, LANES)
        kv[j][1] = dot(valued, hot, out=BF16).reshape(buckets, span, LANES)
    query_ref[...] = dot(norm, w_query[...], out=BF16)


def gate_out(scal, query, w_out, *refs, rows, part):
    parts, (mixer_ref, gated_ref, branch_ref) = refs[:-3], refs[-3:]
    share = query.shape[-1]
    mixer = jnp.zeros((rows, share), F32)
    for j, ref in enumerate(parts):
        mixer = mixer + dot(ref[...].reshape(rows, LANES), spread(scal, j, share, part), (1, 1))
    mixer_ref[...] = mixer.astype(BF16)
    gated = (query[...].astype(F32) * mixer).astype(BF16)
    gated_ref[...] = gated
    branch_ref[...] = dot(gated, w_out[...], out=BF16)


def resid_of(x, branch, branch_other):
    return x[...].astype(F32) + (branch[...].astype(F32) + branch_other[...].astype(F32))


def feed_forward(
    scal, x, branch, branch_other, gain, bias, g, w_up, w_down, norm_ref, act_ref, d_hidden_ref, swap_ref, mine_ref, total, down
):
    step = pl.program_id(0)
    share = mine_ref.shape[-1]
    width = x.shape[-1]

    @pl.when(step == 0)
    def _():
        unit, _ = centred(resid_of(x, branch, branch_other))
        norm_ref[...] = (unit * gain[...] + bias[...]).astype(BF16)
        total[...] = jnp.zeros_like(total)
        down[...] = jnp.zeros_like(down)

    up = w_up[...]
    hidden = dot(norm_ref[...], up)
    d_act = dot(g[...], w_down[...], (1, 1))
    root = 0.7978845608028654
    square = hidden * hidden
    half = 0.5 + 0.5 * jnp.tanh(hidden * (root + (0.044715 * root) * square))
    product = hidden * half
    act = product.astype(BF16)
    act_ref[...] = act
    slope = half + product * (1.0 - half) * (2.0 * root + (6.0 * 0.044715 * root) * square)
    d_hidden = (d_act * slope).astype(BF16)
    d_hidden_ref[...] = d_hidden
    total[...] += dot(d_hidden, up, (1, 1))
    down[...] += dot(act, w_down[...])

    @pl.when(step == pl.num_programs(0) - 1)
    def _():
        mine, others = lanes_of(scal[4], share), lanes_of(1 - scal[4], share)
        swap_ref[:, :width] = total[...].astype(BF16)
        swap_ref[:, width:] = down[:, others].astype(BF16)
        resid = x[:, mine].astype(F32) + (branch[:, mine].astype(F32) + branch_other[:, mine].astype(F32))
        mine_ref[...] = resid + down[:, mine]


def resid_back(
    scal, x, branch, branch_other, mine, other, gain, g, w_out, query, mixer, *refs, buckets, span, group, part
):
    d_branch_ref, d_query_ref, d_mine_ref, vectors = refs[:4]
    outs = refs[4:]
    share = query.shape[-1]
    unit, inverse = centred(resid_of(x, branch, branch_other))
    width = x.shape[-1]
    d_norm2 = mine[:, :width].astype(F32) + other[:, :width].astype(F32)
    d_x, d_gain, d_bias = norm_back(d_norm2, unit, inverse, gain[...])
    d_resid = g[...].astype(F32) + d_x
    d_branch = d_resid.astype(BF16)
    d_branch_ref[...] = d_branch
    d_gated = dot(d_branch, w_out[...], (1, 1))
    d_mixer = (d_gated * query[...].astype(F32)).astype(BF16)
    for j in range(group):
        outs[j][...] = dot(d_mixer, spread(scal, j, share, part), out=BF16).reshape(buckets, span, LANES)
    d_query_ref[...] = (d_gated * mixer[...].astype(F32)).astype(BF16)
    vectors[0:1, :] = d_gain
    vectors[1:2, :] = d_bias
    d_mine_ref[...] = jnp.where(scal[4] == 0, d_resid[:, :share], d_resid[:, share:])


def project_back(scal, d_query, w_query, w_key, w_value, *refs, rows, part):
    parts, d_norm_ref = refs[:-1], refs[-1]
    share = d_query.shape[-1]
    sums = [jnp.zeros((rows, share), F32) for _ in range(2)]
    for j, ref in enumerate(parts):
        hot = spread(scal, j, share, part)
        for i in range(2):
            sums[i] = sums[i] + dot(ref[i].reshape(rows, LANES), hot, (1, 1))
    d_keyed, d_valued = sums[0].astype(BF16), sums[1].astype(BF16)
    d_norm_ref[...] = (
        dot(d_query[...], w_query[...], (1, 1))
        + dot(d_keyed, w_key[...], (1, 1))
        + dot(d_valued, w_value[...], (1, 1))
    ).astype(BF16)


def key_value_grads(scal, norm, mine, theirs, d_kv, total, *, buckets, group):
    rows = norm.shape[0]
    half = buckets // 2
    for i in range(2):
        grad = dot(norm[...], d_kv[0][i].reshape(rows, LANES), (0, 0))
        for j in range(1, group):
            for ref, member in ((mine[j - 1], scal[4]), (theirs[j - 1], 1 - scal[4])):
                right = d_kv[j][i, pl.ds(member * half, half)].reshape(rows // 2, LANES)
                grad = grad + dot(ref[...], right, (0, 0))
        total[:, LANES * i : LANES * i + LANES] = grad


def small_sum(mine, got, plain, fine):
    plains = mine[:plain].astype(F32) + got[:plain].astype(F32)
    return plains, one_part(mine[plain : plain + 2 * fine]) + one_part(got[plain : plain + 2 * fine])


def parameter_fold(mine, keep, got, send, keep_out, *, plain, fine):
    plains, fines = small_sum(mine, got, plain, fine)
    small = plain + 2 * fine
    send[pl.ds(0, plain), :] = plains.astype(BF16)
    send[pl.ds(plain, 2 * fine), :] = two_parts(fines)
    half = keep.shape[0] // 2
    keep_out[...] = keep[:half] + got[small : small + half].astype(F32)
    send[pl.ds(small, half), :] = (keep[half:] + got[small + half :].astype(F32)).astype(BF16)


def place_pieces(scal, *refs, span):
    pieces, (tokens_ref, block_ref, vector_ref) = refs[:-3], refs[-3:]
    share = tokens_ref.shape[-1]
    rows = span * (share // LANES)
    vec_rows = 2 * vector_ref.shape[0]
    vectors = []
    for k, ref in enumerate(pieces):
        at = lax.bitwise_xor(scal[0], k)
        tokens_ref[at] = from_lanes(ref[:rows], share).astype(F32)
        block_ref[at] = from_lanes(ref[rows : 2 * rows], share).astype(F32)
        vectors.append(one_part(ref[2 * rows : 2 * rows + vec_rows]))
    vector_ref[...] = tree_sum(vectors)


def bucket_sum(scal, vector, mine, keep, got, *outs, group, plain, fine):
    plain_sum, fine_sum = small_sum(mine, got, plain, fine)
    matrix = keep[...] + got[plain + 2 * fine :].astype(F32)
    matrix = from_lanes(matrix, 2 * LANES).astype(BF16)
    total = matrix.shape[0]
    block = total // group
    out_row = lax.broadcasted_iota(jnp.int32, (total, total), 0)
    in_row = lax.broadcasted_iota(jnp.int32, (total, total), 1)
    source = lax.bitwise_xor(out_row // block, scal[1]) * block + lax.rem(out_row, block)
    matrix = dot(jnp.where(source == in_row, 1.0, 0.0).astype(BF16), matrix, out=BF16)
    sums = jnp.concatenate([plain_sum.astype(BF16), two_parts(fine_sum), two_parts(vector[...])], axis=0)
    small = sums.shape[0]
    for j, out in enumerate(outs):
        out[pl.ds(0, small), :] = sums
        out[pl.ds(small, 2 * block), :] = by_lanes(matrix[j * block : j * block + block])


def group_place(scal, *refs, part, span, nstate, fine, vec):
    parts, (key_ref, value_ref, shift_ref, coef_ref, fine_ref, vec_ref) = refs[:-6], refs[-6:]
    share = shift_ref.shape[-1]
    block = key_ref.shape[0]
    plain = span + nstate
    sums = jnp.zeros((plain, share), F32)
    matrix = jnp.zeros((2 * block, share), F32)
    fines, vectors = [], []
    for j, ref in enumerate(parts):
        hot = spread(scal, j, share, part)
        first = plain + 2 * (fine + vec)
        sums = sums + dot(ref[:plain], hot, (1, 1))
        matrix = matrix + dot(ref[first : first + 2 * block], hot, (1, 1))
        fines.append(one_part(ref[plain : plain + 2 * fine]))
        vectors.append(one_part(ref[plain + 2 * fine : first]))
    key_ref[...] = matrix[:block]
    value_ref[...] = matrix[block:]
    shift_ref[...] = sums[:span]
    coef_ref[...] = sums[span:]
    fine_ref[...] = tree_sum(fines)
    vec_ref[...] = tree_sum(vectors)


def turn(*refs, pairs):
    for i in range(pairs):
        source, left, out = refs[2 * i], refs[2 * i + 1], refs[2 * pairs + i]
        width = left.shape[1]
        lane = lax.broadcasted_iota(jnp.int32, (width, LANES), 1)
        hot = jnp.concatenate(
            [jnp.where(source[...] == lane + m, 1.0, 0.0).astype(BF16) for m in range(0, width, LANES)], axis=1
        )
        out[...] = dot(hot, left[...], (1, 1), out=BF16)


def row_grads(*refs, streams):
    pairs = sum(len(s) for s in streams)
    i = 0
    for t, stream in enumerate(streams):
        send, keep = refs[2 * pairs + 2 * t], refs[2 * pairs + 2 * t + 1]
        at = 0
        for first, last in stream:
            turned, right = refs[2 * i], refs[2 * i + 1]
            half = turned.shape[0] // 2
            operand = right[:, first:last]
            send[:, at : at + last - first] = dot(turned[half:], operand, out=BF16)
            keep[:, at : at + last - first] = dot(turned[:half], operand, out=BF16)
            at += last - first
            i += 1


def add(keep, got, out):
    out[...] = keep[...].astype(F32) + got[...].astype(F32)


def finish(*refs, plan):
    outs = refs[sum(terms for terms, _ in plan) :]
    i = 0
    for terms, columns in plan:
        total = refs[i][...].astype(F32)
        if terms == 2:
            total = total + refs[i + 1][...].astype(F32)
        i += terms
        for first, last, out, at in columns:
            outs[out][:, at : at + last - first] = total[:, first:last]


def fold(*refs, pairs):
    ins, outs = refs[: 2 * pairs], refs[2 * pairs :]
    at = 0
    for i in range(pairs):
        keep, got = ins[2 * i], ins[2 * i + 1]
        half, columns = keep.shape[0] // 2, keep.shape[1]
        if len(outs) == 2:
            here, columns_at = outs, pl.ds(at, columns)
        else:
            here, columns_at = outs[2 * i : 2 * i + 2], pl.ds(0, columns)
        here[0][:, columns_at] = (keep[half:].astype(F32) + got[half:].astype(F32)).astype(BF16)
        here[1][:, columns_at] = keep[:half].astype(F32) + got[:half].astype(F32)
        at += columns


def tokens_back(scal, x, d_norm, d_norm_other, gain, d_mine, block_mine, swapped, *refs, span):
    share = d_mine.shape[-1]
    width = x.shape[-1]
    unit, inverse = centred(x[...].astype(F32))
    d_norm1 = d_norm[...].astype(F32) + d_norm_other[...].astype(F32)
    d_x, d_gain, d_bias = norm_back(d_norm1, unit, inverse, gain[...])
    total = (d_mine[...] + jnp.where(scal[4] == 0, d_x[:, :share], d_x[:, share:])).astype(BF16)
    block = (block_mine[...] + swapped[:, width:].astype(F32)).astype(BF16)
    vectors = jnp.concatenate([by_lanes(d_gain), by_lanes(d_bias)], axis=0)
    high = vectors.astype(BF16).astype(F32)
    pad = -(4 * (width // LANES)) % 16
    vectors = jnp.concatenate([high, vectors - high] + [jnp.zeros((pad, LANES), F32)] * (pad > 0), axis=0).astype(BF16)
    rows = span * (share // LANES)
    for k, out in enumerate(refs):
        out[pl.ds(0, rows), :] = by_lanes(total[k * span : k * span + span])
        out[pl.ds(rows, rows), :] = by_lanes(block[k * span : k * span + span])
        out[pl.ds(2 * rows, vectors.shape[0]), :] = vectors


def rolled(x, r):
    return x if r == 0 else pltpu.roll(x, r % x.shape[0], 0)


def split(x):
    high = x.astype(BF16)
    return high, (x - high.astype(F32)).astype(BF16)


def split_dot(left, right):
    lh, ll = split(left)
    rh, rl = split(right)
    return jnp.dot(
        jnp.concatenate([lh, lh, ll], axis=1),
        jnp.concatenate([rh, rl, rh], axis=0),
        preferred_element_type=F32,
    )


def half_dot(left, right):
    lh, ll = split(left)
    rh = right.astype(BF16)
    return jnp.dot(
        jnp.concatenate([lh, ll], axis=1), jnp.concatenate([rh, rh], axis=0), preferred_element_type=F32
    )


def powers_by_step(rrow, span, reverse, shift):
    step = lax.broadcasted_iota(jnp.int32, (span, LANES), 0).astype(F32)
    step = (span - 1.0 - step) if reverse else step + shift
    return jnp.exp(-step * rrow)


def powers_by_state(rcol, span, reverse, shift):
    step = lax.broadcasted_iota(jnp.int32, (LANES, span), 1).astype(F32)
    step = (span - 1.0 - step) if reverse else step + shift
    return jnp.exp(-step * rcol[:, :span]), step


def chunk_row(scal, j, k, group, span):
    return pl.multiple_of(
        (lax.bitwise_xor(scal[0], k) * group + lax.bitwise_xor(scal[1], j)) * span, span
    )


def wide(ref, first, batch, span):
    return jnp.concatenate(
        [ref[pl.ds(pl.multiple_of((first + i) * span, span), span), :] for i in range(batch)], axis=1
    )


def mix_forward(scal, valid, tabs, rrow, taps, *refs, group, buckets, span, batch):
    kv = refs[:group]
    outs = refs[group : 2 * group]
    kf, vf, shifted_ref, mixed_ref, states, ysc, kern_ref = refs[2 * group :]
    limit = valid[scal[0]]
    rcol, scol, coefm, hm = tabs[0], tabs[1], tabs[3], tabs[4]
    eighths = span // 8
    chunks = group * buckets
    kern_ref[...] = split_dot(powers_by_step(rrow[...], span, False, 0.0), scol * coefm)
    w_end = powers_by_state(rcol, span, True, 0.0)[0] * scol[:, :span]
    p_out = powers_by_step(rrow[...], span, False, 1.0)
    decay = jnp.exp(-float(span) * rcol)
    kf[pl.ds(0, span), :] = jnp.zeros((span, LANES), F32)
    for j in range(group):
        for k in range(buckets):
            row = chunk_row(scal, j, k, group, span)
            kf[pl.ds(row + span, span), :] = kv[j][0, k].astype(F32)
            vf[pl.ds(row, span), :] = kv[j][1, k].astype(F32)
    row_id = lax.broadcasted_iota(jnp.int32, (span, LANES), 0)

    def filtered(c, carry):
        start = pl.multiple_of(c * span, span)
        x = kf[pl.ds(start, 2 * span), :]
        acc = jnp.zeros((span, LANES), F32)
        for r in range(8):
            xr = rolled(x, r)
            for q in range(eighths):
                acc = acc + taps[8 * q + r : 8 * q + r + 1, :] * xr[span - 8 * q : 2 * span - 8 * q]
        shifted_ref[pl.ds(start, span), :] = acc
        mixed_ref[pl.ds(start, span), :] = jnp.where(
            row_id + start < limit, acc * vf[pl.ds(start, span), :], 0.0
        )
        return carry

    lax.fori_loop(0, chunks, filtered, 0)

    def carried(turn, state):
        first = turn * batch
        ends = split_dot(w_end, wide(mixed_ref, first, batch, span))
        begins = []
        for i in range(batch):
            states[first + i] = state
            begins.append(coefm * state)
            state = decay * state + ends[:, LANES * i : LANES * i + LANES] * hm
        y = split_dot(p_out, jnp.concatenate(begins, axis=1))
        for i in range(batch):
            ysc[pl.ds(pl.multiple_of((first + i) * span, span), span), :] = y[:, LANES * i : LANES * i + LANES]
        return state

    lax.fori_loop(0, chunks // batch, carried, jnp.zeros((LANES, LANES), F32))

    def inner(c, carry):
        start = pl.multiple_of(c * span, span)
        mixed = mixed_ref[pl.ds(start, span), :]
        y = ysc[pl.ds(start, span), :]
        tails = [y[8 * i : 8 * i + 8] for i in range(eighths)]
        for r in range(8):
            mr = jnp.where(row_id >= r, rolled(mixed, r), 0.0)
            for q in range(eighths):
                weight = kern_ref[8 * q + r : 8 * q + r + 1, :]
                for i in range(q, eighths):
                    tails[i] = tails[i] + weight * mr[8 * (i - q) : 8 * (i - q) + 8]
        for i in range(eighths):
            ysc[pl.ds(start + 8 * i, 8), :] = tails[i]
        return carry

    lax.fori_loop(0, chunks, inner, 0)
    for j in range(group):
        for k in range(buckets):
            outs[j][k] = ysc[pl.ds(chunk_row(scal, j, k, group, span), span), :].astype(BF16)


def mix_backward(scal, valid, tabs, rrow, taps, vf, shifted_ref, *refs, group, buckets, span, batch):
    d_in = refs[:group]
    outs = refs[group : 2 * group]
    dmf, dsf, adj, dks, dvs, kern_ref = refs[2 * group :]
    limit = valid[scal[0]]
    rcol, scol, coefm = tabs[0], tabs[1], tabs[3]
    kern_ref[...] = split_dot(powers_by_step(rrow[...], span, False, 0.0), scol * coefm)
    p_rev = powers_by_step(rrow[...], span, True, 0.0)
    p_in = powers_by_state(rcol, span, False, 1.0)[0]
    decay = jnp.exp(-float(span) * rcol)
    chunks = group * buckets
    eighths = span // 8
    dsf[pl.ds(chunks * span, span), :] = jnp.zeros((span, LANES), F32)
    for j in range(group):
        for k in range(buckets):
            dmf[pl.ds(chunk_row(scal, j, k, group, span), span), :] = d_in[j][k].astype(F32)
    row_id = lax.broadcasted_iota(jnp.int32, (span, LANES), 0)

    def carried(turn, after):
        first = chunks - batch - turn * batch
        seeds = half_dot(p_in, wide(dmf, first, batch, span))
        ends = [None] * batch
        for i in reversed(range(batch)):
            adj[first + i] = after
            ends[i] = scol * after
            after = decay * after + coefm * seeds[:, LANES * i : LANES * i + LANES]
        y = split_dot(p_rev, jnp.concatenate(ends, axis=1))
        for i in range(batch):
            dks[pl.ds(pl.multiple_of((first + i) * span, span), span), :] = y[:, LANES * i : LANES * i + LANES]
        return after

    lax.fori_loop(0, chunks // batch, carried, jnp.zeros((LANES, LANES), F32))

    def chunk(turn, carry):
        start = pl.multiple_of((chunks - 1 - turn) * span, span)
        dm = dmf[pl.ds(start, span), :]
        y = dks[pl.ds(start, span), :]
        heads = [y[8 * i : 8 * i + 8] for i in range(eighths)]
        for r in range(8):
            mr = jnp.where(row_id < span - r, rolled(dm, -r), 0.0)
            for q in range(eighths):
                weight = kern_ref[8 * q + r : 8 * q + r + 1, :]
                for i in range(eighths - q):
                    heads[i] = heads[i] + weight * mr[8 * (i + q) : 8 * (i + q) + 8]
        d_mixed = jnp.where(row_id + start < limit, jnp.concatenate(heads, axis=0), 0.0)
        dvs[pl.ds(start, span), :] = d_mixed * shifted_ref[pl.ds(start, span), :]
        dsf[pl.ds(start, span), :] = d_mixed * vf[pl.ds(start, span), :]
        x = dsf[pl.ds(start, 2 * span), :]
        acc = jnp.zeros((span, LANES), F32)
        for r in range(8):
            xr = rolled(x, -r)
            for q in range(eighths):
                acc = acc + taps[8 * q + r : 8 * q + r + 1, :] * xr[8 * q : 8 * q + span]
        dks[pl.ds(start, span), :] = acc
        return carry

    lax.fori_loop(0, chunks, chunk, 0)
    for j in range(group):
        for k in range(buckets):
            row = chunk_row(scal, j, k, group, span)
            outs[j][0, k] = dks[pl.ds(row, span), :].astype(BF16)
            outs[j][1, k] = dvs[pl.ds(row, span), :].astype(BF16)


def param_grads(scal, tabs, rrow, kf, mixed_ref, states, dmf, dsf, adj, vectors, norm, *refs, span, batch, nstate, group, buckets):
    mine, theirs = refs[: group - 1], refs[group - 1 : 2 * group - 2]
    d_kv = refs[2 * group - 2 : 3 * group - 2]
    first = 3 * group - 2
    send, keep, out, total, coef_out, rate_out, acc_s, acc_k = refs[first:]
    key_value_grads(scal, norm, mine, theirs, d_kv, total, buckets=buckets, group=group)
    rcol, scol, dscol, coefm, hm = tabs[0], tabs[1], tabs[2], tabs[3], tabs[4]
    p_in, step = powers_by_state(rcol, span, False, 1.0)
    into = jnp.concatenate([p_in, p_in * step], axis=0)
    p_end, step = powers_by_state(rcol, span, True, 0.0)
    ends = jnp.concatenate([p_end, p_end * step], axis=0)
    p_kern, step = powers_by_state(rcol, span, False, 0.0)
    decay = float(span) * jnp.exp(-float(span) * rcol)
    chunks = mixed_ref.shape[0] // span
    eighths = span // 8
    acc_s[...] = jnp.zeros_like(acc_s)
    acc_k[...] = jnp.zeros_like(acc_k)
    coef_out[...] = jnp.zeros_like(coef_out)
    rate_out[...] = jnp.zeros_like(rate_out)
    row_id = lax.broadcasted_iota(jnp.int32, (span, LANES), 0)

    def chunk(c, carry):
        start = pl.multiple_of(c * span, span)
        x = kf[pl.ds(start, 2 * span), :]
        ds = dsf[pl.ds(start, span), :]
        mixed = mixed_ref[pl.ds(start, span), :]
        dm = dmf[pl.ds(start, span), :]
        for r in range(8):
            xr = rolled(x, r)
            mr = jnp.where(row_id >= r, rolled(mixed, r), 0.0)
            for q in range(eighths):
                whole = ds * xr[span - 8 * q : 2 * span - 8 * q]
                acc_s[8 * q + r] += jnp.sum(whole.reshape(eighths, 8, LANES), axis=0)
                part = dm[8 * q :] * mr[: span - 8 * q]
                acc_k[8 * q + r] += jnp.sum(part.reshape(eighths - q, 8, LANES), axis=0)
        return carry

    lax.fori_loop(0, chunks, chunk, 0)

    def rates(turn, carry):
        first = turn * batch
        z = half_dot(into, wide(dmf, first, batch, span))
        u = split_dot(ends, wide(mixed_ref, first, batch, span))
        coef = coef_out[...]
        rate = rate_out[...]
        for i in range(batch):
            state, after = states[first + i], adj[first + i]
            at = slice(LANES * i, LANES * i + LANES)
            coef = coef + state * z[:LANES, at]
            rate = (
                rate
                + after * (dscol * u[:LANES, at] - scol * u[LANES:, at] - decay * state)
                - coefm * state * z[LANES:, at]
            )
        coef_out[...] = coef
        rate_out[...] = rate
        return carry

    lax.fori_loop(0, chunks // batch, rates, 0)
    out[pl.ds(0, span), :] = jnp.sum(acc_s[...], axis=1)
    gk = jnp.sum(acc_k[...], axis=1)
    m = split_dot(jnp.concatenate([p_kern, p_kern * step], axis=0), gk)
    m0, m1 = m[:LANES], m[LANES:]
    coef = (coef_out[...] + scol * m0) * hm
    out[pl.ds(span, nstate), :] = coef[:nstate] + coef[nstate:]
    at = span + nstate
    pieces_across = vectors.shape[1] // LANES
    for v in range(2):
        for i in range(pieces_across):
            out[pl.ds(at + v * pieces_across + i, 1), :] = vectors[v : v + 1, LANES * i : LANES * i + LANES]
    at = out.shape[0] - 8
    done = span + nstate + 2 * pieces_across
    out[pl.ds(done, at - done), :] = jnp.zeros((at - done, LANES), F32)
    rate = rate_out[...] + coefm * (dscol * m0 - scol * m1)
    rate = jnp.broadcast_to(jnp.sum(rate, axis=1, keepdims=True), (LANES, LANES))
    row = lax.broadcasted_iota(jnp.int32, (LANES, LANES), 0)
    lane = lax.broadcasted_iota(jnp.int32, (LANES, LANES), 1)
    rate = jnp.where(lax.rem(row, nstate) == lane, rate, 0.0)
    head = lax.broadcasted_iota(jnp.int32, (8, LANES), 0)
    owner = lax.broadcasted_iota(jnp.int32, (8, LANES), 1) // nstate + scal[3]
    out[pl.ds(at, 8), :] = fdot(jnp.where(head == owner, 1.0, 0.0), rate)
    plain = out[pl.ds(0, span + nstate), :].astype(BF16)
    fine = two_parts(out[pl.ds(span + nstate, out.shape[0] - span - nstate), :])
    plane = total.shape[0] // buckets
    small = plain.shape[0] + fine.shape[0]
    send[pl.ds(0, plain.shape[0]), :] = plain
    send[pl.ds(plain.shape[0], fine.shape[0]), :] = fine
    for k in range(buckets):
        at = pl.multiple_of(lax.bitwise_xor(scal[0], k) * plane, plane)
        rows = total[pl.ds(at, plane), :]
        if k % 2:
            send[pl.ds(small + (k // 2) * 2 * plane, 2 * plane), :] = by_lanes(rows.astype(BF16))
        else:
            keep[pl.ds((k // 2) * 2 * plane, 2 * plane), :] = by_lanes(rows)


def body(
    tokens,
    valid_len,
    ln1_gain,
    ln1_bias,
    w_query,
    w_key,
    w_value,
    shift_kernel,
    ssm_rate,
    ssm_coef,
    w_out,
    ln2_gain,
    ln2_bias,
    w_up,
    w_down,
    d_out,
):
    buckets, span, share = tokens.shape
    rows = buckets * span
    heads, nstate = ssm_rate.shape
    head_width = share // heads
    width, hidden = w_up.shape
    count = lax.axis_size("seq")
    group = count // buckets
    part = share // group
    place = lax.axis_index("seq")
    member = lax.axis_index("ch")
    b, g = place // group, place % group
    first_head = (g * part) // head_width
    scal = jnp.stack([b, g, place, first_head, member]).astype(jnp.int32)
    as_row = lambda v: v.reshape(1, -1)
    ANY = pl.BlockSpec(memory_space=pl.ANY)

    def trade_buckets(pieces):
        return [pieces[0]] + [trade(pieces[k], k * group) for k in range(1, buckets)]

    def trade_group(blocks):
        return [blocks[0]] + [trade(blocks[j], j) for j in range(1, group)]

    call = Order()

    picked = call(
        pick_pieces,
        "pick_pieces",
        [pltpu.VMEM((span, share), BF16)] * (2 * buckets),
        scal,
        in_hbm(tokens),
        in_hbm(d_out),
        scratch=[pltpu.SemaphoreType.DMA((2 * buckets,))],
        in_specs=[SMEM, ANY, ANY],
        smem=1,
    )
    (own,) = call(assemble, "assemble", [shape(BF16, rows, share)], *trade_buckets(picked[:buckets]))
    other = swap(own)
    own_out = trade_buckets(picked[buckets:])

    lane = jnp.arange(LANES, dtype=jnp.int32)
    row_head = first_head + lane // nstate
    hm = (row_head[:, None] == ((g * part + lane) // head_width)[None, :]) & (lane < part)[None, :]
    hm = hm.astype(F32)
    two = lax.dynamic_slice_in_dim(
        jnp.concatenate([ssm_rate, ssm_rate[-1:]], axis=0), first_head, 2, 0
    ).reshape(1, 2 * nstate)
    rate_col = jnp.broadcast_to(two.reshape(-1, 1), (LANES, LANES))
    scale_col = jnp.sqrt(-jnp.expm1(-2.0 * rate_col))
    dscale_col = jnp.exp(-2.0 * rate_col) / scale_col
    coef_part = lax.dynamic_slice_in_dim(ssm_coef, g * part, part, 0)
    coef_part = jnp.pad(coef_part, ((0, LANES - part), (0, 0))).T
    coefm = jnp.concatenate([coef_part, coef_part], axis=0) * hm
    tabs = jnp.stack([rate_col, scale_col, dscale_col, coefm, hm])
    taps = jnp.pad(lax.dynamic_slice_in_dim(shift_kernel, g * part, part, 1), ((0, 0), (0, LANES - part)))

    bits = [1 << i for i in range(count.bit_length() - 1)]
    row_block = width // count

    def source_of(order):
        rel = jnp.arange(width, dtype=jnp.int32)
        at = rel // row_block
        target = jnp.zeros_like(at)
        for i, step in enumerate(order):
            target = target + ((at >> (len(order) - 1 - i)) & 1) * step
        source = (target ^ place) * row_block + rel % row_block
        return jnp.broadcast_to(source[:, None], (width, LANES))

    order_a = bits
    order_b = [bits[1], bits[0]] + bits[2:]
    source_a, source_b = source_of(order_a), source_of(order_b)
    turned_shape = shape(BF16, width, rows)
    half = width // 2

    def turned(*pairs, tag):
        operands = [a for p in pairs for a in p]
        return call(
            functools.partial(turn, pairs=len(pairs)), "turn", [turned_shape] * len(pairs), *operands, tag=tag
        )

    def grads(streams, tag):
        outs = [shape(BF16, half, sum(p[3] - p[2] for p in st)) for st in streams for _ in range(2)]
        operands = [a for st in streams for p in st for a in p[:2]]
        columns = [[p[2:] for p in st] for st in streams]
        return call(functools.partial(row_grads, streams=columns), "row_grads", outs, *operands, tag=tag)

    def folded(ins, joined, tag):
        pairs = len(ins) // 2
        rows_out = ins[0].shape[0] // 2
        columns = [a.shape[1] for a in ins[::2]]
        if rows_out % 16:
            totals = [ins[2 * i].astype(F32) + ins[2 * i + 1].astype(F32) for i in range(pairs)]
            if joined:
                totals = [jnp.concatenate(totals, axis=1)]
            return [v for t in totals for v in (t[rows_out:].astype(BF16), t[:rows_out])]
        if joined:
            columns = [sum(columns)]
        outs = [shape(kind, rows_out, c) for c in columns for kind in (BF16, F32)]
        return call(functools.partial(fold, pairs=pairs), "fold", outs, *ins, tag=tag)

    wide_rows, narrow_rows = shape(BF16, rows, width), shape(BF16, rows, share)
    pair = shape(BF16, 2, buckets, span, LANES)
    small = shape(BF16, buckets, span, LANES)
    sizes = dict(buckets=buckets, span=span, group=group, part=part)
    x, norm1, norm1_half, query, *kv = call(
        functools.partial(project, **sizes),
        "project",
        [pltpu.HBM((rows, width), BF16)] * 2 + [pltpu.HBM((rows // 2, width), BF16), pltpu.HBM((rows, share), BF16)] + [pair] * group,
        scal, as_row(ln1_gain), as_row(ln1_bias), w_query, w_key, w_value, own, other,
        smem=1,
    )
    kv = trade_group(kv)
    mine_halves = [trade(norm1_half, j) for j in range(1, group)]
    length = count * span
    long, longer, per_chunk = shape(F32, length, LANES), shape(F32, length + span, LANES), shape(F32, count, LANES, LANES)
    mix_sizes = dict(group=group, buckets=buckets, span=span, batch=min(count, 8))
    mix_vmem = min(14 * MIB + 12 * length * LANES * 4, 60 * MIB)
    forward_out = call(
        functools.partial(mix_forward, **mix_sizes),
        "mix_forward",
        [small] * group + [longer, long, long, long, per_chunk],
        scal, valid_len, tabs, two, taps, *kv,
        scratch=[pltpu.VMEM((length, LANES), F32), pltpu.VMEM((span, LANES), F32)],
        smem=2,
        vmem=mix_vmem,
    )
    kf, vf, shifted, mixed, states = forward_out[group:]
    mixer_parts = trade_group(forward_out[:group])
    (own_out,) = call(assemble, "assemble", [shape(BF16, rows, share)], *own_out)
    other_out = swap(own_out)
    mixer, gated, branch = call(
        functools.partial(gate_out, rows=rows, part=part),
        "gate_out",
        [narrow_rows, narrow_rows, wide_rows],
        scal, after(query, *mine_halves), w_out, *mixer_parts,
        smem=1,
    )
    branch_other = swap(branch)
    (grad_full,) = call(join, "join", [shape(BF16, rows, width)], scal, own_out, other_out, smem=1)
    other_halves = [swap(p) for p in mine_halves]
    steps = 4
    block = hidden // steps
    fixed = pl.BlockSpec((rows, width), lambda i: (0, 0))
    vector = pl.BlockSpec((1, width), lambda i: (0, 0))
    column = pl.BlockSpec((rows, block), lambda i: (0, i))
    norm2, act, d_hidden, to_swap, block_mine = call(
        feed_forward,
        "feed_forward",
        [wide_rows, shape(BF16, rows, hidden), shape(BF16, rows, hidden), shape(BF16, rows, width + share)]
        + [shape(F32, rows, share)],
        scal, x, branch, branch_other, as_row(ln2_gain), as_row(ln2_bias), grad_full, w_up, w_down,
        scratch=[pltpu.VMEM((rows, width), F32)] * 2,
        grid=(steps,),
        in_specs=[SMEM, fixed, fixed, fixed, vector, vector, fixed]
        + [pl.BlockSpec((width, block), lambda i: (0, i)), pl.BlockSpec((block, width), lambda i: (i, 0))],
        out_specs=[fixed, column, column, pl.BlockSpec((rows, width + share), lambda i: (0, 0))]
        + [pl.BlockSpec((rows, share), lambda i: (0, 0))],
        smem=1,
    )
    swapped = swap(to_swap)

    plane_rows = width // buckets
    vector_rows = 2 * (width // LANES)
    small_rows = -(-(span + nstate + vector_rows + 8) // 16) * 16
    fine = small_rows - span - nstate
    small_out = span + nstate + 2 * fine
    vec_rows = 4 * (width // LANES)
    piece_rows = 2 * span * (share // LANES) + -(-vec_rows // 16) * 16
    block_rows = span + nstate + 2 * fine + vec_rows + 2 * row_block
    ours = shape(F32, buckets, span, share)
    chunks = len(CUTS) + 1
    cuts = [0] + [int(c * hidden) // LANES * LANES for c in CUTS] + [hidden]
    got = {}

    def sent(name, value, move):
        others = [got[n] for n in LATE.get(name, ())]
        got[name] = move(after(value, *others) if others else value)
        return got[name]

    def sent_all(name, values, move):
        moved = move([after(values[0], *[got[n] for n in LATE[name]])] + list(values[1:]) if name in LATE else values)
        got[name] = moved[1]
        for i, value in enumerate(moved[1:]):
            got[name + str(i + 1)] = value
        return moved

    def late(name, values):
        others = [got[n] for n in LATE.get(name, ())]
        return [after(v, *others) for v in values] if others else list(values)

    def resid_step():
        got["d_branch"], got["d_query"], got["d_mine"], got["vectors2"], *d_mixer = call(
            functools.partial(resid_back, **sizes),
            "resid_back",
            [wide_rows, narrow_rows, shape(F32, rows, share), shape(F32, 2, width)] + [small] * group,
            scal, x, branch, branch_other, to_swap, swapped, as_row(ln2_gain), grad_full, w_out, query, mixer,
            smem=1,
        )
        moved = trade_group(late("dm", d_mixer))
        got["d_mixer"] = moved
        for i in range(1, group):
            got["dm%d" % i] = moved[i]

    def turn_up_step():
        got["turned_a"], got["turned_b"] = turned((source_a, norm2), (source_b, grad_full), tag="turn_up")

    def turn_out_step():
        got["turned_o"], got["turned_q"] = turned((source_a, got["d_branch"]), (source_b, norm1), tag="turn_out")

    def grads_step(i):
        streams = [[(got["turned_a"], d_hidden, cuts[i], cuts[i + 1])], [(got["turned_b"], act, cuts[i], cuts[i + 1])]]
        if i == OUT_IN:
            streams[0].append((got["turned_o"], gated, 0, share))
            streams[1].append((got["turned_q"], got["d_query"], 0, share))
        got["c%d" % i] = grads(streams, "grads%d" % i)
        if "t%ds1" % i not in ORDER:
            pair_step(i, 0)

    def pair_step(i, at):
        name = "c%d" % i
        step = name + "s%d" % (at + 1)
        send_a, keep_a, send_b, keep_b = got[name]
        send_a, send_b = late(step, [send_a, send_b])
        got[name] = [keep_a, trade(send_a, order_a[at]), keep_b, trade(send_b, order_b[at])]
        got[step], got[step + "b"] = got[name][1], got[name][3]

    def second_step(i):
        got["c%d" % i] = folded(got["c%d" % i], False, "fold_%ds2" % i)
        if "t%ds2" % i not in ORDER:
            pair_step(i, 1)

    def add_step(i):
        ins = got["c%d" % i]
        got["c%d" % i] = call(add, "add", [shape(F32, *ins[0].shape)], *ins)

    def joint_step(i, at):
        name = "c%d" % i
        ins = got[name]
        if at == 0:
            for other in MERGE.get(i, ()):
                ins = got["c%d" % other] + ins
        send, keep = folded(ins, True, "fold_%dz%d" % (i, at))
        (send,) = late("%sz%d" % (name, at), [send])
        got[name] = [keep, trade(send, bits[2 + at])]
        got["%sz%d" % (name, at)] = got[name][1]

    def mixer_step():
        outs = call(
            functools.partial(mix_backward, **mix_sizes),
            "mix_backward",
            [pair] * group + [long, longer, per_chunk],
            scal, valid_len, tabs, two, taps, vf, shifted, *got["d_mixer"],
            scratch=[pltpu.VMEM((length, LANES), F32), pltpu.VMEM((length, LANES), F32), pltpu.VMEM((span, LANES), F32)],
            smem=2,
            vmem=mix_vmem,
        )
        got["own_kv"], (got["dmf"], got["dsf"], got["adj"]) = outs[:group], outs[group:]
        got["mixer"] = outs[0]
        got["d_kv"] = trade_group(late("dkv", outs[:group]))
        for i in range(1, group):
            got["dkv%d" % i] = got["d_kv"][i]

    def project_step():
        (d_norm1,) = call(
            functools.partial(project_back, rows=rows, part=part), "project_back", [wide_rows],
            scal, got["d_query"], w_query, w_key, w_value, *got["d_kv"], smem=1,
        )
        got["d_norm1"], got["d_norm1_other"] = d_norm1, swap(d_norm1)

    def tokens_step():
        pieces = call(
            functools.partial(tokens_back, span=span),
            "tokens_back",
            [shape(BF16, piece_rows, LANES)] * buckets,
            scal, x, got["d_norm1"], got["d_norm1_other"], as_row(ln1_gain), got["d_mine"], block_mine, swapped,
            smem=1,
        )
        got["tokens"] = pieces[0]
        got["rows"] = trade_buckets(late("pieces", pieces))
        for i in range(1, buckets):
            got["pieces%d" % i] = got["rows"][i]

    def parameters_step():
        kept = buckets // 2 * 2 * plane_rows
        send, keep = call(
            functools.partial(param_grads, span=span, batch=mix_sizes["batch"], nstate=nstate, group=group, buckets=buckets),
            "param_grads",
            [shape(BF16, small_out + kept, LANES), shape(F32, kept, LANES)],
            scal, tabs, two, kf, mixed, states, got["dmf"], got["dsf"], got["adj"], got["vectors2"],
            norm1, *mine_halves, *other_halves, *got["own_kv"],
            scratch=[pltpu.VMEM((small_rows, LANES), F32), pltpu.VMEM((width, 2 * LANES), F32)]
            + [pltpu.VMEM((LANES, LANES), F32)] * 2
            + [pltpu.VMEM((span, 8, LANES), F32)] * 2,
            smem=1,
            vmem=mix_vmem,
        )
        got["parameters"] = send
        (send,) = late("p0", [send])
        got["p"] = [send, keep, trade(send, group)]
        got["p0"] = got["p"][2]

    def parameter_fold_step(at):
        kept = got["p"][1].shape[0] // 2
        send, keep = call(
            functools.partial(parameter_fold, plain=span + nstate, fine=fine),
            "parameter_fold",
            [shape(BF16, small_out + kept, LANES), shape(F32, kept, LANES)],
            *got["p"],
        )
        (send,) = late("p%d" % at, [send])
        got["p"] = [send, keep, trade(send, group << at)]
        got["p%d" % at] = got["p"][2]

    def place_step():
        got["grad_tokens"], got["block_out"], got["vector"] = call(
            functools.partial(place_pieces, span=span),
            "place_pieces",
            [ours, ours, shape(F32, vector_rows, LANES)],
            scal, *got["rows"],
            smem=1,
        )

    def bucket_step():
        blocks = call(
            functools.partial(bucket_sum, group=group, plain=span + nstate, fine=fine),
            "bucket_sum",
            [shape(BF16, block_rows, LANES)] * group,
            scal, got["vector"], *got["p"],
            smem=1,
        )
        got["blocks"] = trade_group(late("plane", blocks))

    def group_step():
        got["group"] = call(
            functools.partial(group_place, part=part, span=span, nstate=nstate, fine=fine, vec=vector_rows),
            "group_place",
            [shape(F32, row_block, share)] * 2
            + [shape(F32, span, share), shape(F32, nstate, share), shape(F32, fine, LANES), shape(F32, vector_rows, LANES)],
            scal, *got["blocks"],
            smem=1,
        )

    named = dict(
        resid=resid_step, turn_up=turn_up_step, turn_out=turn_out_step, mixer=mixer_step, project=project_step,
        tokens=tokens_step, parameters=parameters_step, place=place_step, bucket=bucket_step, group=group_step,
    )
    for name in ORDER:
        if name in named:
            named[name]()
        elif name == "pe":
            for at in range(1, buckets.bit_length() - 1):
                parameter_fold_step(at)
        elif name.startswith("x"):
            add_step(int(name[1:]))
        elif name.startswith("g"):
            grads_step(int(name[1:]))
        elif name.startswith("t"):
            pair_step(int(name[1]), int(name[3]) - 1)
        else:
            i, kind = int(name[1]), name[2:]
            if kind == "s2":
                second_step(i)
            elif kind == "z":
                joint_step(i, 0)
            else:
                for at in range(1, len(bits) - 2):
                    joint_step(i, at)
    plan, ends = [], []
    for i in range(chunks):
        if any(i in m for m in MERGE.values()):
            continue
        columns, at = [], 0
        for c in [*reversed(MERGE.get(i, ())), i]:
            for stream in range(2):
                columns.append((at, at + cuts[c + 1] - cuts[c], stream, cuts[c]))
                at += cuts[c + 1] - cuts[c]
                if c == OUT_IN:
                    columns.append((at, at + share, 2 + stream, 0))
                    at += share
        plan.append((len(got["c%d" % i]), columns))
        ends += got["c%d" % i]
    grad_up, grad_down, grad_out, grad_query = call(
        functools.partial(finish, plan=plan),
        "finish",
        [shape(F32, row_block, hidden)] * 2 + [shape(F32, row_block, share)] * 2,
        *ends,
    )
    grad_down, grad_out = grad_down.T, grad_out.T
    grad_key, grad_value, grad_shift, grad_coef, rest, vectors1 = got["group"]
    block_out, grad_tokens = got["block_out"], got["grad_tokens"]
    grad_g2, grad_c2 = rest[:vector_rows].reshape(2, width)
    grad_rate = rest[fine - 8 : fine - 8 + heads, :nstate]
    grad_g1, grad_c1 = vectors1.reshape(2, width)
    grad_coef = grad_coef.T
    return (
        block_out,
        grad_tokens,
        grad_g1,
        grad_c1,
        grad_query,
        grad_key,
        grad_value,
        grad_shift,
        grad_rate,
        grad_coef,
        grad_out,
        grad_g2,
        grad_c2,
        grad_up,
        grad_down,
    )


def solution(mesh):
    in_specs = (
        P(None, "seq", "ch"),
        P(),
        P(),
        P(),
        P(None, "ch"),
        P(None, "ch"),
        P(None, "ch"),
        P(None, "ch"),
        P("ch", None),
        P("ch", None),
        P("ch", None),
        P(),
        P(),
        P(None, "ch"),
        P("ch", None),
        P(None, "seq", "ch"),
    )
    out_specs = (
        P(None, "seq", "ch"),
        P(None, "seq", "ch"),
        P(),
        P(),
        P("seq", "ch"),
        P("seq", "ch"),
        P("seq", "ch"),
        P(None, "ch"),
        P("ch", None),
        P("ch", None),
        P("ch", "seq"),
        P(),
        P(),
        P("seq", "ch"),
        P("ch", "seq"),
    )
    return jax.shard_map(body, mesh=mesh, in_specs=in_specs, out_specs=out_specs, check_vma=False)
```

```python
import functools

import jax
import jax.numpy as jnp
from jax import lax
from jax.experimental import pallas as pl
from jax.experimental.pallas import tpu as pltpu
from jax.sharding import PartitionSpec as P

LANES = 128
HIGH = lax.Precision.HIGHEST
F32 = jnp.float32
BF16 = jnp.bfloat16
VMEM = pl.BlockSpec(memory_space=pltpu.VMEM)
SMEM = pl.BlockSpec(memory_space=pltpu.SMEM)
MIB = 1024 * 1024

CUTS = (0.34, 0.67)
OUT_IN = 2
MERGE = {}
ORDER = (
    "turn_up", "g0", "resid", "g1", "turn_out", "f0s2", "mixer", "f0z", "t1s1", "g2", "f0e", "project", "f1s2", "t2s1",
    "tokens", "parameters", "vector", "t1s2", "f2s2", "pe", "f1z", "x0", "bucket", "f1e", "f2z", "f2e", "place", "group",
)
LATE = {
    "c2s1": ('d_norm1',),
    "p1": ('c2s1', 'c2s1b'),
}
COST = dict(
    project=1.0, turn=1.0, mix_forward=9.0, gate_out=2.0, feed_forward=0.1, resid_back=0.1, turn_up=0.1, turn_out=0.1,
    grads0=0.1, grads1=0.1, grads2=0.1, mix_backward=10.0, project_back=6.0, tokens_back=0.1, param_grads=10.0, bucket_sum=0.1,
    group_place=0.1, finish=1.0, fold_0s2=0.1, fold_1s2=0.1, fold_0z0=0.1, fold_1z0=0.1, fold_0z1=0.1, fold_1z1=0.1,
    parameter_fold=0.1, place_pieces=0.1, vector_sum=0.1,
)


class Order:
    def __init__(self):
        self.last = None

    def __call__(self, kernel, name, outs, *args, scratch=(), vmem=20 * MIB, smem=0, tag=None, **grid):
        grid.setdefault("in_specs", [SMEM] * smem + [VMEM] * (len(args) - smem))
        grid.setdefault("out_specs", [VMEM] * len(outs))
        args = list(args)
        if self.last is not None:
            args[smem] = after(args[smem], self.last)
        made = pl.pallas_call(
            kernel,
            out_shape=list(outs),
            scratch_shapes=list(scratch),
            compiler_params=pltpu.CompilerParams(vmem_limit_bytes=vmem),
            cost_estimate=pl.CostEstimate(
                flops=int(COST.get(tag or name, 2.0) * 1e9), bytes_accessed=0, transcendentals=0
            ),
            name=name,
            **grid,
        )(*args)
        self.last = made[0]
        return made


def shape(dtype, *dims):
    return jax.ShapeDtypeStruct(dims, dtype)


def trade(value, step):
    count = lax.axis_size("seq")
    return lax.ppermute(value, "seq", [(i, i ^ step) for i in range(count)])


def swap(value):
    return lax.ppermute(value, "ch", [(0, 1), (1, 0)])


def xor_place(x, index):
    count = x.shape[0]
    bit = 1
    while bit < count:
        y = x.reshape((count // (2 * bit), 2, bit) + x.shape[1:])
        flipped = jnp.concatenate([y[:, 1:], y[:, :1]], axis=1)
        x = jnp.where((index & bit) != 0, flipped, y).reshape(x.shape)
        bit *= 2
    return x


def tree_sum(parts):
    parts = list(parts)
    while len(parts) > 1:
        parts = [parts[i] + parts[i + 1] for i in range(0, len(parts), 2)]
    return parts[0]


def in_hbm(x):
    return pltpu.with_memory_space_constraint(x, pltpu.HBM)


def in_vmem(x):
    return pltpu.with_memory_space_constraint(x, pltpu.VMEM)


def after(x, *others):
    return lax.optimization_barrier((x,) + others)[0]


def dot(left, right, contract=(1, 0), out=F32):
    return lax.dot_general(
        left, right, (((contract[0],), (contract[1],)), ((), ())), preferred_element_type=F32
    ).astype(out)


def fdot(left, right, contract=(1, 0)):
    return lax.dot_general(
        left, right, (((contract[0],), (contract[1],)), ((), ())), preferred_element_type=F32, precision=HIGH
    )


def spread(scal, j, share, part, dtype=BF16):
    channel = lax.broadcasted_iota(jnp.int32, (share, LANES), 0)
    lane = lax.broadcasted_iota(jnp.int32, (share, LANES), 1)
    first = lax.bitwise_xor(scal[1], j) * part
    return jnp.where(jnp.where(lane < part, lane + first, -1) == channel, 1.0, 0.0).astype(dtype)


def lanes_of(member, share):
    return pl.ds(pl.multiple_of(member * share, LANES), share)


def centred(x):
    mean = jnp.mean(x, axis=-1, keepdims=True)
    cent = x - mean
    var = jnp.mean(cent * cent, axis=-1, keepdims=True)
    inverse = lax.rsqrt(var + 1e-05)
    return cent * inverse, inverse


def norm_back(d_norm, unit, inverse, gain):
    scaled = d_norm * gain
    first = jnp.mean(scaled, axis=-1, keepdims=True)
    second = jnp.mean(scaled * unit, axis=-1, keepdims=True)
    return (
        inverse * (scaled - first - unit * second),
        jnp.sum(d_norm * unit, axis=0, keepdims=True),
        jnp.sum(d_norm, axis=0, keepdims=True),
    )


def pick_pieces(scal, tokens, d_out, *refs):
    outs, sems = refs[:-1], refs[-1]
    half = len(outs) // 2
    copies = []
    for k in range(half):
        at = lax.bitwise_xor(scal[0], k)
        for i, ref in enumerate((tokens, d_out)):
            copies.append(pltpu.make_async_copy(ref.at[at], outs[half * i + k], sems.at[2 * k + i]))
            copies[-1].start()
    for copy in copies:
        copy.wait()


def by_lanes(x):
    return jnp.concatenate([x[:, at : at + LANES] for at in range(0, x.shape[1], LANES)], axis=0)


def from_lanes(x, columns):
    rows = x.shape[0] // (columns // LANES)
    return jnp.concatenate([x[at : at + rows] for at in range(0, x.shape[0], rows)], axis=1)


def two_parts(x):
    high = x.astype(BF16)
    return jnp.concatenate([high, (x - high.astype(F32)).astype(BF16)], axis=0)


def one_part(x):
    half = x.shape[0] // 2
    return x[:half].astype(F32) + x[half:].astype(F32)


def assemble(*refs):
    rows = refs[0].shape[0]
    for k, ref in enumerate(refs[:-1]):
        refs[-1][pl.ds(k * rows, rows), :] = ref[...]


def project(scal, gain, bias, w_query, w_key, w_value, *refs, buckets, span, group, part):
    own, other, x_ref, norm_ref, half_ref, query_ref = refs[:6]
    kv = refs[6:]
    share = own.shape[-1]
    rows = buckets * span
    mine, others = lanes_of(scal[4], share), lanes_of(1 - scal[4], share)
    x_ref[:, mine] = own[...]
    x_ref[:, others] = other[...]
    unit, _ = centred(x_ref[...].astype(F32))
    norm = (unit * gain[...] + bias[...]).astype(BF16)
    norm_ref[...] = norm
    half_ref[...] = norm_ref[pl.ds(pl.multiple_of(scal[4] * (rows // 2), rows // 2), rows // 2), :]
    keyed = dot(norm, w_key[...], out=BF16)
    valued = dot(norm, w_value[...], out=BF16)
    for j in range(group):
        hot = spread(scal, j, share, part)
        kv[j][0] = dot(keyed, hot, out=BF16).reshape(buckets, span, LANES)
        kv[j][1] = dot(valued, hot, out=BF16).reshape(buckets, span, LANES)
    query_ref[...] = dot(norm, w_query[...], out=BF16)


def gate_out(scal, query, w_out, *refs, rows, part):
    parts, (mixer_ref, gated_ref, branch_ref) = refs[:-3], refs[-3:]
    share = query.shape[-1]
    mixer = jnp.zeros((rows, share), F32)
    for j, ref in enumerate(parts):
        mixer = mixer + dot(ref[...].reshape(rows, LANES), spread(scal, j, share, part), (1, 1))
    mixer_ref[...] = mixer.astype(BF16)
    gated = (query[...].astype(F32) * mixer).astype(BF16)
    gated_ref[...] = gated
    branch_ref[...] = dot(gated, w_out[...], out=BF16)


def resid_of(x, branch, branch_other):
    return x[...].astype(F32) + (branch[...].astype(F32) + branch_other[...].astype(F32))


def feed_forward(
    scal, x, branch, branch_other, gain, bias, own, other, w_up, w_down, norm_ref, g_ref, act_ref, d_hidden_ref, swap_ref, mine_ref
):
    share = mine_ref.shape[-1]
    width = x.shape[-1]
    mine, others = lanes_of(scal[4], share), lanes_of(1 - scal[4], share)
    g_ref[:, mine] = own[...]
    g_ref[:, others] = other[...]
    unit, _ = centred(resid_of(x, branch, branch_other))
    norm = (unit * gain[...] + bias[...]).astype(BF16)
    norm_ref[...] = norm
    hidden = dot(norm, w_up[...])
    d_act = dot(g_ref[...], w_down[...], (1, 1))
    root = 0.7978845608028654
    square = hidden * hidden
    half = 0.5 + 0.5 * jnp.tanh(hidden * (root + (0.044715 * root) * square))
    product = hidden * half
    act = product.astype(BF16)
    act_ref[...] = act
    slope = half + product * (1.0 - half) * (2.0 * root + (6.0 * 0.044715 * root) * square)
    d_hidden = (d_act * slope).astype(BF16)
    d_hidden_ref[...] = d_hidden
    swap_ref[:, :width] = dot(d_hidden, w_up[...], (1, 1), out=BF16)
    swap_ref[:, width:] = dot(act, w_down[:, others], out=BF16)
    resid = x[:, mine].astype(F32) + (branch[:, mine].astype(F32) + branch_other[:, mine].astype(F32))
    mine_ref[...] = resid + dot(act, w_down[:, mine])


def resid_back(
    scal, x, branch, branch_other, mine, other, gain, g, w_out, query, mixer, *refs, buckets, span, group, part
):
    d_branch_ref, d_query_ref, d_mine_ref, vectors = refs[:4]
    outs = refs[4:]
    share = query.shape[-1]
    unit, inverse = centred(resid_of(x, branch, branch_other))
    width = x.shape[-1]
    d_norm2 = mine[:, :width].astype(F32) + other[:, :width].astype(F32)
    d_x, d_gain, d_bias = norm_back(d_norm2, unit, inverse, gain[...])
    d_resid = g[...].astype(F32) + d_x
    d_branch = d_resid.astype(BF16)
    d_branch_ref[...] = d_branch
    d_gated = dot(d_branch, w_out[...], (1, 1))
    d_mixer = (d_gated * query[...].astype(F32)).astype(BF16)
    for j in range(group):
        outs[j][...] = dot(d_mixer, spread(scal, j, share, part), out=BF16).reshape(buckets, span, LANES)
    d_query_ref[...] = (d_gated * mixer[...].astype(F32)).astype(BF16)
    vectors[0:1, :] = d_gain
    vectors[1:2, :] = d_bias
    d_mine_ref[...] = jnp.where(scal[4] == 0, d_resid[:, :share], d_resid[:, share:])


def project_back(scal, d_query, w_query, w_key, w_value, *refs, rows, part):
    parts, d_norm_ref = refs[:-1], refs[-1]
    share = d_query.shape[-1]
    sums = [jnp.zeros((rows, share), F32) for _ in range(2)]
    for j, ref in enumerate(parts):
        hot = spread(scal, j, share, part)
        for i in range(2):
            sums[i] = sums[i] + dot(ref[i].reshape(rows, LANES), hot, (1, 1))
    d_keyed, d_valued = sums[0].astype(BF16), sums[1].astype(BF16)
    d_norm_ref[...] = (
        dot(d_query[...], w_query[...], (1, 1))
        + dot(d_keyed, w_key[...], (1, 1))
        + dot(d_valued, w_value[...], (1, 1))
    ).astype(BF16)


def key_value_grads(scal, norm, mine, theirs, d_kv, total, *, buckets, group):
    rows = norm.shape[0]
    half = buckets // 2
    for i in range(2):
        grad = dot(norm[...], d_kv[0][i].reshape(rows, LANES), (0, 0))
        for j in range(1, group):
            for ref, member in ((mine[j - 1], scal[4]), (theirs[j - 1], 1 - scal[4])):
                right = d_kv[j][i, pl.ds(member * half, half)].reshape(rows // 2, LANES)
                grad = grad + dot(ref[...], right, (0, 0))
        total[:, LANES * i : LANES * i + LANES] = grad


def small_sum(mine, got, plain, fine):
    plains = mine[:plain].astype(F32) + got[:plain].astype(F32)
    return plains, one_part(mine[plain : plain + 2 * fine]) + one_part(got[plain : plain + 2 * fine])


def parameter_fold(mine, keep, got, send, keep_out, *, plain, fine):
    plains, fines = small_sum(mine, got, plain, fine)
    small = plain + 2 * fine
    send[pl.ds(0, plain), :] = plains.astype(BF16)
    send[pl.ds(plain, 2 * fine), :] = two_parts(fines)
    half = keep.shape[0] // 2
    keep_out[...] = keep[:half] + got[small : small + half].astype(F32)
    send[pl.ds(small, half), :] = (keep[half:] + got[small + half :].astype(F32)).astype(BF16)


def vector_sum(*refs, first):
    refs[-1][...] = tree_sum([one_part(ref[first:]) for ref in refs[:-1]])


def place_pieces(scal, *refs, span):
    pieces, (tokens_ref, block_ref) = refs[:-2], refs[-2:]
    share = tokens_ref.shape[-1]
    rows = span * (share // LANES)
    for k, ref in enumerate(pieces):
        at = lax.bitwise_xor(scal[0], k)
        tokens_ref[at] = from_lanes(ref[:rows], share).astype(F32)
        block_ref[at] = from_lanes(ref[rows : 2 * rows], share).astype(F32)


def bucket_sum(scal, vector, mine, keep, got, *outs, group, plain, fine):
    plain_sum, fine_sum = small_sum(mine, got, plain, fine)
    matrix = keep[...] + got[plain + 2 * fine :].astype(F32)
    matrix = from_lanes(matrix, 2 * LANES).astype(BF16)
    total = matrix.shape[0]
    block = total // group
    out_row = lax.broadcasted_iota(jnp.int32, (total, total), 0)
    in_row = lax.broadcasted_iota(jnp.int32, (total, total), 1)
    source = lax.bitwise_xor(out_row // block, scal[1]) * block + lax.rem(out_row, block)
    matrix = dot(jnp.where(source == in_row, 1.0, 0.0).astype(BF16), matrix, out=BF16)
    sums = jnp.concatenate([plain_sum.astype(BF16), two_parts(fine_sum), two_parts(vector[...])], axis=0)
    small = sums.shape[0]
    for j, out in enumerate(outs):
        out[pl.ds(0, small), :] = sums
        out[pl.ds(small, 2 * block), :] = by_lanes(matrix[j * block : j * block + block])


def group_place(scal, *refs, part, span, nstate, fine, vec):
    parts, (key_ref, value_ref, shift_ref, coef_ref, fine_ref, vec_ref) = refs[:-6], refs[-6:]
    share = shift_ref.shape[-1]
    block = key_ref.shape[0]
    plain = span + nstate
    sums = jnp.zeros((plain, share), F32)
    matrix = jnp.zeros((2 * block, share), F32)
    fines, vectors = [], []
    for j, ref in enumerate(parts):
        hot = spread(scal, j, share, part)
        first = plain + 2 * (fine + vec)
        sums = sums + dot(ref[:plain], hot, (1, 1))
        matrix = matrix + dot(ref[first : first + 2 * block], hot, (1, 1))
        fines.append(one_part(ref[plain : plain + 2 * fine]))
        vectors.append(one_part(ref[plain + 2 * fine : first]))
    key_ref[...] = matrix[:block]
    value_ref[...] = matrix[block:]
    shift_ref[...] = sums[:span]
    coef_ref[...] = sums[span:]
    fine_ref[...] = tree_sum(fines)
    vec_ref[...] = tree_sum(vectors)


def turn(*refs, pairs):
    for i in range(pairs):
        source, left, out = refs[2 * i], refs[2 * i + 1], refs[2 * pairs + i]
        width = left.shape[1]
        lane = lax.broadcasted_iota(jnp.int32, (width, LANES), 1)
        hot = jnp.concatenate(
            [jnp.where(source[...] == lane + m, 1.0, 0.0).astype(BF16) for m in range(0, width, LANES)], axis=1
        )
        out[...] = dot(hot, left[...], (1, 1), out=BF16)


def row_grads(*refs, streams):
    pairs = sum(len(s) for s in streams)
    i = 0
    for t, stream in enumerate(streams):
        send, keep = refs[2 * pairs + 2 * t], refs[2 * pairs + 2 * t + 1]
        at = 0
        for first, last in stream:
            turned, right = refs[2 * i], refs[2 * i + 1]
            half = turned.shape[0] // 2
            operand = right[:, first:last]
            send[:, at : at + last - first] = dot(turned[half:], operand, out=BF16)
            keep[:, at : at + last - first] = dot(turned[:half], operand, out=BF16)
            at += last - first
            i += 1


def add(keep, got, out):
    out[...] = keep[...].astype(F32) + got[...].astype(F32)


def finish(*refs, plan):
    outs = refs[sum(terms for terms, _ in plan) :]
    i = 0
    for terms, columns in plan:
        total = refs[i][...].astype(F32)
        if terms == 2:
            total = total + refs[i + 1][...].astype(F32)
        i += terms
        for first, last, out, at in columns:
            outs[out][:, at : at + last - first] = total[:, first:last]


def fold(*refs, pairs):
    ins, outs = refs[: 2 * pairs], refs[2 * pairs :]
    at = 0
    for i in range(pairs):
        keep, got = ins[2 * i], ins[2 * i + 1]
        half, columns = keep.shape[0] // 2, keep.shape[1]
        if len(outs) == 2:
            here, columns_at = outs, pl.ds(at, columns)
        else:
            here, columns_at = outs[2 * i : 2 * i + 2], pl.ds(0, columns)
        here[0][:, columns_at] = (keep[half:].astype(F32) + got[half:].astype(F32)).astype(BF16)
        here[1][:, columns_at] = keep[:half].astype(F32) + got[:half].astype(F32)
        at += columns


def tokens_back(scal, x, d_norm, d_norm_other, gain, d_mine, block_mine, swapped, *refs, span):
    share = d_mine.shape[-1]
    width = x.shape[-1]
    unit, inverse = centred(x[...].astype(F32))
    d_norm1 = d_norm[...].astype(F32) + d_norm_other[...].astype(F32)
    d_x, d_gain, d_bias = norm_back(d_norm1, unit, inverse, gain[...])
    total = (d_mine[...] + jnp.where(scal[4] == 0, d_x[:, :share], d_x[:, share:])).astype(BF16)
    block = (block_mine[...] + swapped[:, width:].astype(F32)).astype(BF16)
    vectors = [by_lanes(d_gain), by_lanes(d_bias)]
    pad = -(2 * (width // LANES)) % 16
    vectors = two_parts(jnp.concatenate(vectors + [jnp.zeros((pad, LANES), F32)] * (pad > 0), axis=0))
    rows = span * (share // LANES)
    for k, out in enumerate(refs):
        out[pl.ds(0, rows), :] = by_lanes(total[k * span : k * span + span])
        out[pl.ds(rows, rows), :] = by_lanes(block[k * span : k * span + span])
        out[pl.ds(2 * rows, vectors.shape[0]), :] = vectors


def rolled(x, r):
    return x if r == 0 else pltpu.roll(x, r % x.shape[0], 0)


def split(x):
    high = x.astype(BF16)
    return high, (x - high.astype(F32)).astype(BF16)


def split_dot(left, right):
    lh, ll = split(left)
    rh, rl = split(right)
    return jnp.dot(
        jnp.concatenate([lh, lh, ll], axis=1),
        jnp.concatenate([rh, rl, rh], axis=0),
        preferred_element_type=F32,
    )


def half_dot(left, right):
    lh, ll = split(left)
    rh = right.astype(BF16)
    return jnp.dot(
        jnp.concatenate([lh, ll], axis=1), jnp.concatenate([rh, rh], axis=0), preferred_element_type=F32
    )


def powers_by_step(rrow, span, reverse, shift):
    step = lax.broadcasted_iota(jnp.int32, (span, LANES), 0).astype(F32)
    step = (span - 1.0 - step) if reverse else step + shift
    return jnp.exp(-step * rrow)


def powers_by_state(rcol, span, reverse, shift):
    step = lax.broadcasted_iota(jnp.int32, (LANES, span), 1).astype(F32)
    step = (span - 1.0 - step) if reverse else step + shift
    return jnp.exp(-step * rcol[:, :span]), step


def chunk_row(scal, j, k, group, span):
    return pl.multiple_of(
        (lax.bitwise_xor(scal[0], k) * group + lax.bitwise_xor(scal[1], j)) * span, span
    )


def wide(ref, first, batch, span):
    return jnp.concatenate(
        [ref[pl.ds(pl.multiple_of((first + i) * span, span), span), :] for i in range(batch)], axis=1
    )


def mix_forward(scal, valid, tabs, rrow, taps, *refs, group, buckets, span, batch):
    kv = refs[:group]
    outs = refs[group : 2 * group]
    kf, vf, shifted_ref, mixed_ref, states, ysc, kern_ref = refs[2 * group :]
    limit = valid[scal[0]]
    rcol, scol, coefm, hm = tabs[0], tabs[1], tabs[3], tabs[4]
    eighths = span // 8
    chunks = group * buckets
    kern_ref[...] = split_dot(powers_by_step(rrow[...], span, False, 0.0), scol * coefm)
    w_end = powers_by_state(rcol, span, True, 0.0)[0] * scol[:, :span]
    p_out = powers_by_step(rrow[...], span, False, 1.0)
    decay = jnp.exp(-float(span) * rcol)
    kf[pl.ds(0, span), :] = jnp.zeros((span, LANES), F32)
    for j in range(group):
        for k in range(buckets):
            row = chunk_row(scal, j, k, group, span)
            kf[pl.ds(row + span, span), :] = kv[j][0, k].astype(F32)
            vf[pl.ds(row, span), :] = kv[j][1, k].astype(F32)
    row_id = lax.broadcasted_iota(jnp.int32, (span, LANES), 0)

    def filtered(c, carry):
        start = pl.multiple_of(c * span, span)
        x = kf[pl.ds(start, 2 * span), :]
        acc = jnp.zeros((span, LANES), F32)
        for r in range(8):
            xr = rolled(x, r)
            for q in range(eighths):
                acc = acc + taps[8 * q + r : 8 * q + r + 1, :] * xr[span - 8 * q : 2 * span - 8 * q]
        shifted_ref[pl.ds(start, span), :] = acc
        mixed_ref[pl.ds(start, span), :] = jnp.where(
            row_id + start < limit, acc * vf[pl.ds(start, span), :], 0.0
        )
        return carry

    lax.fori_loop(0, chunks, filtered, 0)

    def carried(turn, state):
        first = turn * batch
        ends = split_dot(w_end, wide(mixed_ref, first, batch, span))
        begins = []
        for i in range(batch):
            states[first + i] = state
            begins.append(coefm * state)
            state = decay * state + ends[:, LANES * i : LANES * i + LANES] * hm
        y = split_dot(p_out, jnp.concatenate(begins, axis=1))
        for i in range(batch):
            ysc[pl.ds(pl.multiple_of((first + i) * span, span), span), :] = y[:, LANES * i : LANES * i + LANES]
        return state

    lax.fori_loop(0, chunks // batch, carried, jnp.zeros((LANES, LANES), F32))

    def inner(c, carry):
        start = pl.multiple_of(c * span, span)
        mixed = mixed_ref[pl.ds(start, span), :]
        y = ysc[pl.ds(start, span), :]
        tails = [y[8 * i : 8 * i + 8] for i in range(eighths)]
        for r in range(8):
            mr = jnp.where(row_id >= r, rolled(mixed, r), 0.0)
            for q in range(eighths):
                weight = kern_ref[8 * q + r : 8 * q + r + 1, :]
                for i in range(q, eighths):
                    tails[i] = tails[i] + weight * mr[8 * (i - q) : 8 * (i - q) + 8]
        for i in range(eighths):
            ysc[pl.ds(start + 8 * i, 8), :] = tails[i]
        return carry

    lax.fori_loop(0, chunks, inner, 0)
    for j in range(group):
        for k in range(buckets):
            outs[j][k] = ysc[pl.ds(chunk_row(scal, j, k, group, span), span), :].astype(BF16)


def mix_backward(scal, valid, tabs, rrow, taps, vf, shifted_ref, *refs, group, buckets, span, batch):
    d_in = refs[:group]
    outs = refs[group : 2 * group]
    dmf, dsf, adj, dks, dvs, kern_ref = refs[2 * group :]
    limit = valid[scal[0]]
    rcol, scol, coefm = tabs[0], tabs[1], tabs[3]
    kern_ref[...] = split_dot(powers_by_step(rrow[...], span, False, 0.0), scol * coefm)
    p_rev = powers_by_step(rrow[...], span, True, 0.0)
    p_in = powers_by_state(rcol, span, False, 1.0)[0]
    decay = jnp.exp(-float(span) * rcol)
    chunks = group * buckets
    eighths = span // 8
    dsf[pl.ds(chunks * span, span), :] = jnp.zeros((span, LANES), F32)
    for j in range(group):
        for k in range(buckets):
            dmf[pl.ds(chunk_row(scal, j, k, group, span), span), :] = d_in[j][k].astype(F32)
    row_id = lax.broadcasted_iota(jnp.int32, (span, LANES), 0)

    def carried(turn, after):
        first = chunks - batch - turn * batch
        seeds = half_dot(p_in, wide(dmf, first, batch, span))
        ends = [None] * batch
        for i in reversed(range(batch)):
            adj[first + i] = after
            ends[i] = scol * after
            after = decay * after + coefm * seeds[:, LANES * i : LANES * i + LANES]
        y = split_dot(p_rev, jnp.concatenate(ends, axis=1))
        for i in range(batch):
            dks[pl.ds(pl.multiple_of((first + i) * span, span), span), :] = y[:, LANES * i : LANES * i + LANES]
        return after

    lax.fori_loop(0, chunks // batch, carried, jnp.zeros((LANES, LANES), F32))

    def chunk(turn, carry):
        start = pl.multiple_of((chunks - 1 - turn) * span, span)
        dm = dmf[pl.ds(start, span), :]
        y = dks[pl.ds(start, span), :]
        heads = [y[8 * i : 8 * i + 8] for i in range(eighths)]
        for r in range(8):
            mr = jnp.where(row_id < span - r, rolled(dm, -r), 0.0)
            for q in range(eighths):
                weight = kern_ref[8 * q + r : 8 * q + r + 1, :]
                for i in range(eighths - q):
                    heads[i] = heads[i] + weight * mr[8 * (i + q) : 8 * (i + q) + 8]
        d_mixed = jnp.where(row_id + start < limit, jnp.concatenate(heads, axis=0), 0.0)
        dvs[pl.ds(start, span), :] = d_mixed * shifted_ref[pl.ds(start, span), :]
        dsf[pl.ds(start, span), :] = d_mixed * vf[pl.ds(start, span), :]
        x = dsf[pl.ds(start, 2 * span), :]
        acc = jnp.zeros((span, LANES), F32)
        for r in range(8):
            xr = rolled(x, -r)
            for q in range(eighths):
                acc = acc + taps[8 * q + r : 8 * q + r + 1, :] * xr[8 * q : 8 * q + span]
        dks[pl.ds(start, span), :] = acc
        return carry

    lax.fori_loop(0, chunks, chunk, 0)
    for j in range(group):
        for k in range(buckets):
            row = chunk_row(scal, j, k, group, span)
            outs[j][0, k] = dks[pl.ds(row, span), :].astype(BF16)
            outs[j][1, k] = dvs[pl.ds(row, span), :].astype(BF16)


def param_grads(scal, tabs, rrow, kf, mixed_ref, states, dmf, dsf, adj, vectors, norm, *refs, span, batch, nstate, group, buckets):
    mine, theirs = refs[: group - 1], refs[group - 1 : 2 * group - 2]
    d_kv = refs[2 * group - 2 : 3 * group - 2]
    first = 3 * group - 2
    send, keep, out, total, coef_out, rate_out, acc_s, acc_k = refs[first:]
    key_value_grads(scal, norm, mine, theirs, d_kv, total, buckets=buckets, group=group)
    rcol, scol, dscol, coefm, hm = tabs[0], tabs[1], tabs[2], tabs[3], tabs[4]
    p_in, step = powers_by_state(rcol, span, False, 1.0)
    into = jnp.concatenate([p_in, p_in * step], axis=0)
    p_end, step = powers_by_state(rcol, span, True, 0.0)
    ends = jnp.concatenate([p_end, p_end * step], axis=0)
    p_kern, step = powers_by_state(rcol, span, False, 0.0)
    decay = float(span) * jnp.exp(-float(span) * rcol)
    chunks = mixed_ref.shape[0] // span
    eighths = span // 8
    acc_s[...] = jnp.zeros_like(acc_s)
    acc_k[...] = jnp.zeros_like(acc_k)
    coef_out[...] = jnp.zeros_like(coef_out)
    rate_out[...] = jnp.zeros_like(rate_out)
    row_id = lax.broadcasted_iota(jnp.int32, (span, LANES), 0)

    def chunk(c, carry):
        start = pl.multiple_of(c * span, span)
        x = kf[pl.ds(start, 2 * span), :]
        ds = dsf[pl.ds(start, span), :]
        mixed = mixed_ref[pl.ds(start, span), :]
        dm = dmf[pl.ds(start, span), :]
        for r in range(8):
            xr = rolled(x, r)
            mr = jnp.where(row_id >= r, rolled(mixed, r), 0.0)
            for q in range(eighths):
                whole = ds * xr[span - 8 * q : 2 * span - 8 * q]
                acc_s[8 * q + r] += jnp.sum(whole.reshape(eighths, 8, LANES), axis=0)
                part = dm[8 * q :] * mr[: span - 8 * q]
                acc_k[8 * q + r] += jnp.sum(part.reshape(eighths - q, 8, LANES), axis=0)
        return carry

    lax.fori_loop(0, chunks, chunk, 0)

    def rates(turn, carry):
        first = turn * batch
        z = half_dot(into, wide(dmf, first, batch, span))
        u = split_dot(ends, wide(mixed_ref, first, batch, span))
        coef = coef_out[...]
        rate = rate_out[...]
        for i in range(batch):
            state, after = states[first + i], adj[first + i]
            at = slice(LANES * i, LANES * i + LANES)
            coef = coef + state * z[:LANES, at]
            rate = (
                rate
                + after * (dscol * u[:LANES, at] - scol * u[LANES:, at] - decay * state)
                - coefm * state * z[LANES:, at]
            )
        coef_out[...] = coef
        rate_out[...] = rate
        return carry

    lax.fori_loop(0, chunks // batch, rates, 0)
    out[pl.ds(0, span), :] = jnp.sum(acc_s[...], axis=1)
    gk = jnp.sum(acc_k[...], axis=1)
    m = split_dot(jnp.concatenate([p_kern, p_kern * step], axis=0), gk)
    m0, m1 = m[:LANES], m[LANES:]
    coef = (coef_out[...] + scol * m0) * hm
    out[pl.ds(span, nstate), :] = coef[:nstate] + coef[nstate:]
    at = span + nstate
    pieces_across = vectors.shape[1] // LANES
    for v in range(2):
        for i in range(pieces_across):
            out[pl.ds(at + v * pieces_across + i, 1), :] = vectors[v : v + 1, LANES * i : LANES * i + LANES]
    at = out.shape[0] - 8
    done = span + nstate + 2 * pieces_across
    out[pl.ds(done, at - done), :] = jnp.zeros((at - done, LANES), F32)
    rate = rate_out[...] + coefm * (dscol * m0 - scol * m1)
    rate = jnp.broadcast_to(jnp.sum(rate, axis=1, keepdims=True), (LANES, LANES))
    row = lax.broadcasted_iota(jnp.int32, (LANES, LANES), 0)
    lane = lax.broadcasted_iota(jnp.int32, (LANES, LANES), 1)
    rate = jnp.where(lax.rem(row, nstate) == lane, rate, 0.0)
    head = lax.broadcasted_iota(jnp.int32, (8, LANES), 0)
    owner = lax.broadcasted_iota(jnp.int32, (8, LANES), 1) // nstate + scal[3]
    out[pl.ds(at, 8), :] = fdot(jnp.where(head == owner, 1.0, 0.0), rate)
    plain = out[pl.ds(0, span + nstate), :].astype(BF16)
    fine = two_parts(out[pl.ds(span + nstate, out.shape[0] - span - nstate), :])
    plane = total.shape[0] // buckets
    small = plain.shape[0] + fine.shape[0]
    send[pl.ds(0, plain.shape[0]), :] = plain
    send[pl.ds(plain.shape[0], fine.shape[0]), :] = fine
    for k in range(buckets):
        at = pl.multiple_of(lax.bitwise_xor(scal[0], k) * plane, plane)
        rows = total[pl.ds(at, plane), :]
        if k % 2:
            send[pl.ds(small + (k // 2) * 2 * plane, 2 * plane), :] = by_lanes(rows.astype(BF16))
        else:
            keep[pl.ds((k // 2) * 2 * plane, 2 * plane), :] = by_lanes(rows)


def body(
    tokens,
    valid_len,
    ln1_gain,
    ln1_bias,
    w_query,
    w_key,
    w_value,
    shift_kernel,
    ssm_rate,
    ssm_coef,
    w_out,
    ln2_gain,
    ln2_bias,
    w_up,
    w_down,
    d_out,
):
    buckets, span, share = tokens.shape
    rows = buckets * span
    heads, nstate = ssm_rate.shape
    head_width = share // heads
    width, hidden = w_up.shape
    count = lax.axis_size("seq")
    group = count // buckets
    part = share // group
    place = lax.axis_index("seq")
    member = lax.axis_index("ch")
    b, g = place // group, place % group
    first_head = (g * part) // head_width
    scal = jnp.stack([b, g, place, first_head, member]).astype(jnp.int32)
    as_row = lambda v: v.reshape(1, -1)
    ANY = pl.BlockSpec(memory_space=pl.ANY)

    def trade_buckets(pieces):
        return [pieces[0]] + [trade(pieces[k], k * group) for k in range(1, buckets)]

    def trade_group(blocks):
        return [blocks[0]] + [trade(blocks[j], j) for j in range(1, group)]

    call = Order()

    picked = call(
        pick_pieces,
        "pick_pieces",
        [pltpu.VMEM((span, share), BF16)] * (2 * buckets),
        scal,
        in_hbm(tokens),
        in_hbm(d_out),
        scratch=[pltpu.SemaphoreType.DMA((2 * buckets,))],
        in_specs=[SMEM, ANY, ANY],
        smem=1,
    )
    (own,) = call(assemble, "assemble", [shape(BF16, rows, share)], *trade_buckets(picked[:buckets]))
    other = swap(own)
    own_out = trade_buckets(picked[buckets:])

    lane = jnp.arange(LANES, dtype=jnp.int32)
    row_head = first_head + lane // nstate
    hm = (row_head[:, None] == ((g * part + lane) // head_width)[None, :]) & (lane < part)[None, :]
    hm = hm.astype(F32)
    two = lax.dynamic_slice_in_dim(
        jnp.concatenate([ssm_rate, ssm_rate[-1:]], axis=0), first_head, 2, 0
    ).reshape(1, 2 * nstate)
    rate_col = jnp.broadcast_to(two.reshape(-1, 1), (LANES, LANES))
    scale_col = jnp.sqrt(-jnp.expm1(-2.0 * rate_col))
    dscale_col = jnp.exp(-2.0 * rate_col) / scale_col
    coef_part = lax.dynamic_slice_in_dim(ssm_coef, g * part, part, 0)
    coef_part = jnp.pad(coef_part, ((0, LANES - part), (0, 0))).T
    coefm = jnp.concatenate([coef_part, coef_part], axis=0) * hm
    tabs = jnp.stack([rate_col, scale_col, dscale_col, coefm, hm])
    taps = jnp.pad(lax.dynamic_slice_in_dim(shift_kernel, g * part, part, 1), ((0, 0), (0, LANES - part)))

    bits = [1 << i for i in range(count.bit_length() - 1)]
    row_block = width // count

    def source_of(order):
        rel = jnp.arange(width, dtype=jnp.int32)
        at = rel // row_block
        target = jnp.zeros_like(at)
        for i, step in enumerate(order):
            target = target + ((at >> (len(order) - 1 - i)) & 1) * step
        source = (target ^ place) * row_block + rel % row_block
        return jnp.broadcast_to(source[:, None], (width, LANES))

    order_a = bits
    order_b = [bits[1], bits[0]] + bits[2:]
    source_a, source_b = source_of(order_a), source_of(order_b)
    turned_shape = shape(BF16, width, rows)
    half = width // 2

    def turned(*pairs, tag):
        operands = [a for p in pairs for a in p]
        return call(
            functools.partial(turn, pairs=len(pairs)), "turn", [turned_shape] * len(pairs), *operands, tag=tag
        )

    def grads(streams, tag):
        outs = [shape(BF16, half, sum(p[3] - p[2] for p in st)) for st in streams for _ in range(2)]
        operands = [a for st in streams for p in st for a in p[:2]]
        columns = [[p[2:] for p in st] for st in streams]
        return call(functools.partial(row_grads, streams=columns), "row_grads", outs, *operands, tag=tag)

    def folded(ins, joined, tag):
        pairs = len(ins) // 2
        rows_out = ins[0].shape[0] // 2
        columns = [a.shape[1] for a in ins[::2]]
        if rows_out % 16:
            totals = [ins[2 * i].astype(F32) + ins[2 * i + 1].astype(F32) for i in range(pairs)]
            if joined:
                totals = [jnp.concatenate(totals, axis=1)]
            return [v for t in totals for v in (t[rows_out:].astype(BF16), t[:rows_out])]
        if joined:
            columns = [sum(columns)]
        outs = [shape(kind, rows_out, c) for c in columns for kind in (BF16, F32)]
        return call(functools.partial(fold, pairs=pairs), "fold", outs, *ins, tag=tag)

    wide_rows, narrow_rows = shape(BF16, rows, width), shape(BF16, rows, share)
    pair = shape(BF16, 2, buckets, span, LANES)
    small = shape(BF16, buckets, span, LANES)
    sizes = dict(buckets=buckets, span=span, group=group, part=part)
    x, norm1, norm1_half, query, *kv = call(
        functools.partial(project, **sizes),
        "project",
        [pltpu.HBM((rows, width), BF16)] * 2 + [pltpu.HBM((rows // 2, width), BF16), pltpu.HBM((rows, share), BF16)] + [pair] * group,
        scal, as_row(ln1_gain), as_row(ln1_bias), w_query, w_key, w_value, own, other,
        smem=1,
    )
    kv = trade_group(kv)
    mine_halves = [trade(norm1_half, j) for j in range(1, group)]
    length = count * span
    long, longer, per_chunk = shape(F32, length, LANES), shape(F32, length + span, LANES), shape(F32, count, LANES, LANES)
    mix_sizes = dict(group=group, buckets=buckets, span=span, batch=min(count, 8))
    mix_vmem = min(14 * MIB + 12 * length * LANES * 4, 60 * MIB)
    forward_out = call(
        functools.partial(mix_forward, **mix_sizes),
        "mix_forward",
        [small] * group + [longer, long, long, long, per_chunk],
        scal, valid_len, tabs, two, taps, *kv,
        scratch=[pltpu.VMEM((length, LANES), F32), pltpu.VMEM((span, LANES), F32)],
        smem=2,
        vmem=mix_vmem,
    )
    kf, vf, shifted, mixed, states = forward_out[group:]
    mixer_parts = trade_group(forward_out[:group])
    (own_out,) = call(assemble, "assemble", [shape(BF16, rows, share)], *own_out)
    other_out = swap(own_out)
    mixer, gated, branch = call(
        functools.partial(gate_out, rows=rows, part=part),
        "gate_out",
        [narrow_rows, narrow_rows, wide_rows],
        scal, after(query, *mine_halves), w_out, *mixer_parts,
        smem=1,
    )
    branch_other = swap(branch)
    other_halves = [swap(p) for p in mine_halves]
    norm2, grad_full, act, d_hidden, to_swap, block_mine = call(
        feed_forward,
        "feed_forward",
        [wide_rows, wide_rows, shape(BF16, rows, hidden), shape(BF16, rows, hidden), shape(BF16, rows, width + share)]
        + [shape(F32, rows, share)],
        scal, x, branch, branch_other, as_row(ln2_gain), as_row(ln2_bias), own_out, other_out, w_up, w_down,
        smem=1,
    )
    swapped = swap(to_swap)

    plane_rows = width // buckets
    vector_rows = 2 * (width // LANES)
    small_rows = -(-(span + nstate + vector_rows + 8) // 16) * 16
    fine = small_rows - span - nstate
    small_out = span + nstate + 2 * fine
    vec_rows = 2 * (-(-vector_rows // 16) * 16)
    piece_rows = 2 * span * (share // LANES) + vec_rows
    block_rows = span + nstate + 2 * fine + vec_rows + 2 * row_block
    ours = shape(F32, buckets, span, share)
    chunks = len(CUTS) + 1
    cuts = [0] + [int(c * hidden) // LANES * LANES for c in CUTS] + [hidden]
    got = {}

    def sent(name, value, move):
        others = [got[n] for n in LATE.get(name, ())]
        got[name] = move(after(value, *others) if others else value)
        return got[name]

    def sent_all(name, values, move):
        moved = move([after(values[0], *[got[n] for n in LATE[name]])] + list(values[1:]) if name in LATE else values)
        got[name] = moved[1]
        for i, value in enumerate(moved[1:]):
            got[name + str(i + 1)] = value
        return moved

    def late(name, values):
        others = [got[n] for n in LATE.get(name, ())]
        return [after(v, *others) for v in values] if others else list(values)

    def resid_step():
        got["d_branch"], got["d_query"], got["d_mine"], got["vectors2"], *d_mixer = call(
            functools.partial(resid_back, **sizes),
            "resid_back",
            [wide_rows, narrow_rows, shape(F32, rows, share), shape(F32, 2, width)] + [small] * group,
            scal, x, branch, branch_other, to_swap, swapped, as_row(ln2_gain), grad_full, w_out, query, mixer,
            smem=1,
        )
        moved = trade_group(late("dm", d_mixer))
        got["d_mixer"] = moved
        for i in range(1, group):
            got["dm%d" % i] = moved[i]

    def turn_up_step():
        got["turned_a"], got["turned_b"] = turned((source_a, norm2), (source_b, grad_full), tag="turn_up")

    def turn_out_step():
        got["turned_o"], got["turned_q"] = turned((source_a, got["d_branch"]), (source_b, norm1), tag="turn_out")

    def grads_step(i):
        streams = [[(got["turned_a"], d_hidden, cuts[i], cuts[i + 1])], [(got["turned_b"], act, cuts[i], cuts[i + 1])]]
        if i == OUT_IN:
            streams[0].append((got["turned_o"], gated, 0, share))
            streams[1].append((got["turned_q"], got["d_query"], 0, share))
        got["c%d" % i] = grads(streams, "grads%d" % i)
        if "t%ds1" % i not in ORDER:
            pair_step(i, 0)

    def pair_step(i, at):
        name = "c%d" % i
        step = name + "s%d" % (at + 1)
        send_a, keep_a, send_b, keep_b = got[name]
        send_a, send_b = late(step, [send_a, send_b])
        got[name] = [keep_a, trade(send_a, order_a[at]), keep_b, trade(send_b, order_b[at])]
        got[step], got[step + "b"] = got[name][1], got[name][3]

    def second_step(i):
        got["c%d" % i] = folded(got["c%d" % i], False, "fold_%ds2" % i)
        if "t%ds2" % i not in ORDER:
            pair_step(i, 1)

    def add_step(i):
        ins = got["c%d" % i]
        got["c%d" % i] = call(add, "add", [shape(F32, *ins[0].shape)], *ins)

    def joint_step(i, at):
        name = "c%d" % i
        ins = got[name]
        if at == 0:
            for other in MERGE.get(i, ()):
                ins = got["c%d" % other] + ins
        send, keep = folded(ins, True, "fold_%dz%d" % (i, at))
        (send,) = late("%sz%d" % (name, at), [send])
        got[name] = [keep, trade(send, bits[2 + at])]
        got["%sz%d" % (name, at)] = got[name][1]

    def mixer_step():
        outs = call(
            functools.partial(mix_backward, **mix_sizes),
            "mix_backward",
            [pair] * group + [long, longer, per_chunk],
            scal, valid_len, tabs, two, taps, vf, shifted, *got["d_mixer"],
            scratch=[pltpu.VMEM((length, LANES), F32), pltpu.VMEM((length, LANES), F32), pltpu.VMEM((span, LANES), F32)],
            smem=2,
            vmem=mix_vmem,
        )
        got["own_kv"], (got["dmf"], got["dsf"], got["adj"]) = outs[:group], outs[group:]
        got["mixer"] = outs[0]
        got["d_kv"] = trade_group(late("dkv", outs[:group]))
        for i in range(1, group):
            got["dkv%d" % i] = got["d_kv"][i]

    def project_step():
        (d_norm1,) = call(
            functools.partial(project_back, rows=rows, part=part), "project_back", [wide_rows],
            scal, got["d_query"], w_query, w_key, w_value, *got["d_kv"], smem=1,
        )
        got["d_norm1"], got["d_norm1_other"] = d_norm1, swap(d_norm1)

    def tokens_step():
        pieces = call(
            functools.partial(tokens_back, span=span),
            "tokens_back",
            [shape(BF16, piece_rows, LANES)] * buckets,
            scal, x, got["d_norm1"], got["d_norm1_other"], as_row(ln1_gain), got["d_mine"], block_mine, swapped,
            smem=1,
        )
        got["tokens"] = pieces[0]
        got["rows"] = trade_buckets(late("pieces", pieces))
        for i in range(1, buckets):
            got["pieces%d" % i] = got["rows"][i]

    def parameters_step():
        kept = buckets // 2 * 2 * plane_rows
        send, keep = call(
            functools.partial(param_grads, span=span, batch=mix_sizes["batch"], nstate=nstate, group=group, buckets=buckets),
            "param_grads",
            [shape(BF16, small_out + kept, LANES), shape(F32, kept, LANES)],
            scal, tabs, two, kf, mixed, states, got["dmf"], got["dsf"], got["adj"], got["vectors2"],
            norm1, *mine_halves, *other_halves, *got["own_kv"],
            scratch=[pltpu.VMEM((small_rows, LANES), F32), pltpu.VMEM((width, 2 * LANES), F32)]
            + [pltpu.VMEM((LANES, LANES), F32)] * 2
            + [pltpu.VMEM((span, 8, LANES), F32)] * 2,
            smem=1,
            vmem=mix_vmem,
        )
        got["parameters"] = send
        (send,) = late("p0", [send])
        got["p"] = [send, keep, trade(send, group)]
        got["p0"] = got["p"][2]

    def parameter_fold_step(at):
        kept = got["p"][1].shape[0] // 2
        send, keep = call(
            functools.partial(parameter_fold, plain=span + nstate, fine=fine),
            "parameter_fold",
            [shape(BF16, small_out + kept, LANES), shape(F32, kept, LANES)],
            *got["p"],
        )
        (send,) = late("p%d" % at, [send])
        got["p"] = [send, keep, trade(send, group << at)]
        got["p%d" % at] = got["p"][2]

    def vector_step():
        (got["vector"],) = call(
            functools.partial(vector_sum, first=piece_rows - vec_rows),
            "vector_sum",
            [shape(F32, vec_rows // 2, LANES)],
            *got["rows"],
        )

    def place_step():
        got["grad_tokens"], got["block_out"] = call(
            functools.partial(place_pieces, span=span), "place_pieces", [ours, ours], scal, *got["rows"], smem=1
        )

    def bucket_step():
        blocks = call(
            functools.partial(bucket_sum, group=group, plain=span + nstate, fine=fine),
            "bucket_sum",
            [shape(BF16, block_rows, LANES)] * group,
            scal, got["vector"], *got["p"],
            smem=1,
        )
        got["blocks"] = trade_group(late("plane", blocks))

    def group_step():
        got["group"] = call(
            functools.partial(group_place, part=part, span=span, nstate=nstate, fine=fine, vec=vec_rows // 2),
            "group_place",
            [shape(F32, row_block, share)] * 2
            + [shape(F32, span, share), shape(F32, nstate, share), shape(F32, fine, LANES), shape(F32, vec_rows // 2, LANES)],
            scal, *got["blocks"],
            smem=1,
        )

    named = dict(
        resid=resid_step, turn_up=turn_up_step, turn_out=turn_out_step, mixer=mixer_step, project=project_step,
        tokens=tokens_step, parameters=parameters_step, vector=vector_step, place=place_step, bucket=bucket_step, group=group_step,
    )
    for name in ORDER:
        if name in named:
            named[name]()
        elif name == "pe":
            for at in range(1, buckets.bit_length() - 1):
                parameter_fold_step(at)
        elif name.startswith("x"):
            add_step(int(name[1:]))
        elif name.startswith("g"):
            grads_step(int(name[1:]))
        elif name.startswith("t"):
            pair_step(int(name[1]), int(name[3]) - 1)
        else:
            i, kind = int(name[1]), name[2:]
            if kind == "s2":
                second_step(i)
            elif kind == "z":
                joint_step(i, 0)
            else:
                for at in range(1, len(bits) - 2):
                    joint_step(i, at)
    plan, ends = [], []
    for i in range(chunks):
        if any(i in m for m in MERGE.values()):
            continue
        columns, at = [], 0
        for c in [*reversed(MERGE.get(i, ())), i]:
            for stream in range(2):
                columns.append((at, at + cuts[c + 1] - cuts[c], stream, cuts[c]))
                at += cuts[c + 1] - cuts[c]
                if c == OUT_IN:
                    columns.append((at, at + share, 2 + stream, 0))
                    at += share
        plan.append((len(got["c%d" % i]), columns))
        ends += got["c%d" % i]
    grad_up, grad_down, grad_out, grad_query = call(
        functools.partial(finish, plan=plan),
        "finish",
        [shape(F32, row_block, hidden)] * 2 + [shape(F32, row_block, share)] * 2,
        *ends,
    )
    grad_down, grad_out = grad_down.T, grad_out.T
    grad_key, grad_value, grad_shift, grad_coef, rest, vectors1 = got["group"]
    block_out, grad_tokens = got["block_out"], got["grad_tokens"]
    grad_g2, grad_c2 = rest[:vector_rows].reshape(2, width)
    grad_rate = rest[fine - 8 : fine - 8 + heads, :nstate]
    grad_g1, grad_c1 = vectors1[:vector_rows].reshape(2, width)
    grad_coef = grad_coef.T
    return (
        block_out,
        grad_tokens,
        grad_g1,
        grad_c1,
        grad_query,
        grad_key,
        grad_value,
        grad_shift,
        grad_rate,
        grad_coef,
        grad_out,
        grad_g2,
        grad_c2,
        grad_up,
        grad_down,
    )


def solution(mesh):
    in_specs = (
        P(None, "seq", "ch"),
        P(),
        P(),
        P(),
        P(None, "ch"),
        P(None, "ch"),
        P(None, "ch"),
        P(None, "ch"),
        P("ch", None),
        P("ch", None),
        P("ch", None),
        P(),
        P(),
        P(None, "ch"),
        P("ch", None),
        P(None, "seq", "ch"),
    )
    out_specs = (
        P(None, "seq", "ch"),
        P(None, "seq", "ch"),
        P(),
        P(),
        P("seq", "ch"),
        P("seq", "ch"),
        P("seq", "ch"),
        P(None, "ch"),
        P("ch", None),
        P("ch", None),
        P("ch", "seq"),
        P(),
        P(),
        P("seq", "ch"),
        P("ch", "seq"),
    )
    return jax.shard_map(body, mesh=mesh, in_specs=in_specs, out_specs=out_specs, check_vma=False)
```

```python
import functools

import jax
import jax.numpy as jnp
from jax import lax
from jax.experimental import pallas as pl
from jax.experimental.pallas import tpu as pltpu
from jax.sharding import PartitionSpec as P

LANES = 128
HIGH = lax.Precision.HIGHEST
F32 = jnp.float32
BF16 = jnp.bfloat16
VMEM = pl.BlockSpec(memory_space=pltpu.VMEM)
SMEM = pl.BlockSpec(memory_space=pltpu.SMEM)
MIB = 1024 * 1024

CUTS = (0.34, 0.67)
OUT_IN = 2
MERGE = {}
ORDER = (
    "turn_up", "g0", "resid", "g1", "turn_out", "f0s2", "mixer", "f0z", "t1s1", "g2", "f0e", "project", "f1s2", "t2s1",
    "tokens", "parameters", "vector", "t1s2", "f2s2", "pe", "f1z", "x0", "bucket", "f1e", "f2z", "f2e", "place", "group",
)
LATE = {
    "c2s1": ('d_norm1',),
    "p1": ('c2s1', 'c2s1b'),
}
COST = dict(
    project=1.0, turn=1.0, mix_forward=9.0, gate_out=2.0, feed_forward=0.1, resid_back=0.1, turn_up=0.1, turn_out=0.1,
    grads0=0.1, grads1=0.1, grads2=0.1, mix_backward=10.0, project_back=6.0, tokens_back=0.1, param_grads=10.0, bucket_sum=0.1,
    group_place=0.1, finish=1.0, fold_0s2=0.1, fold_1s2=0.1, fold_0z0=0.1, fold_1z0=0.1, fold_0z1=0.1, fold_1z1=0.1,
    parameter_fold=0.1, place_pieces=0.1, vector_sum=0.1,
)


class Order:
    def __init__(self):
        self.last = None

    def __call__(self, kernel, name, outs, *args, scratch=(), vmem=20 * MIB, smem=0, tag=None, **grid):
        grid.setdefault("in_specs", [SMEM] * smem + [VMEM] * (len(args) - smem))
        grid.setdefault("out_specs", [VMEM] * len(outs))
        args = list(args)
        if self.last is not None:
            args[smem] = after(args[smem], self.last)
        made = pl.pallas_call(
            kernel,
            out_shape=list(outs),
            scratch_shapes=list(scratch),
            compiler_params=pltpu.CompilerParams(vmem_limit_bytes=vmem),
            cost_estimate=pl.CostEstimate(
                flops=int(COST.get(tag or name, 2.0) * 1e9), bytes_accessed=0, transcendentals=0
            ),
            name=name,
            **grid,
        )(*args)
        self.last = made[0]
        return made


def shape(dtype, *dims):
    return jax.ShapeDtypeStruct(dims, dtype)


def trade(value, step):
    count = lax.axis_size("seq")
    return lax.ppermute(value, "seq", [(i, i ^ step) for i in range(count)])


def swap(value):
    return lax.ppermute(value, "ch", [(0, 1), (1, 0)])


def xor_place(x, index):
    count = x.shape[0]
    bit = 1
    while bit < count:
        y = x.reshape((count // (2 * bit), 2, bit) + x.shape[1:])
        flipped = jnp.concatenate([y[:, 1:], y[:, :1]], axis=1)
        x = jnp.where((index & bit) != 0, flipped, y).reshape(x.shape)
        bit *= 2
    return x


def tree_sum(parts):
    parts = list(parts)
    while len(parts) > 1:
        parts = [parts[i] + parts[i + 1] for i in range(0, len(parts), 2)]
    return parts[0]


def in_hbm(x):
    return pltpu.with_memory_space_constraint(x, pltpu.HBM)


def in_vmem(x):
    return pltpu.with_memory_space_constraint(x, pltpu.VMEM)


def after(x, *others):
    return lax.optimization_barrier((x,) + others)[0]


def dot(left, right, contract=(1, 0), out=F32):
    return lax.dot_general(
        left, right, (((contract[0],), (contract[1],)), ((), ())), preferred_element_type=F32
    ).astype(out)


def fdot(left, right, contract=(1, 0)):
    return lax.dot_general(
        left, right, (((contract[0],), (contract[1],)), ((), ())), preferred_element_type=F32, precision=HIGH
    )


def spread(scal, j, share, part, dtype=BF16):
    channel = lax.broadcasted_iota(jnp.int32, (share, LANES), 0)
    lane = lax.broadcasted_iota(jnp.int32, (share, LANES), 1)
    first = lax.bitwise_xor(scal[1], j) * part
    return jnp.where(jnp.where(lane < part, lane + first, -1) == channel, 1.0, 0.0).astype(dtype)


def lanes_of(member, share):
    return pl.ds(pl.multiple_of(member * share, LANES), share)


def centred(x):
    mean = jnp.mean(x, axis=-1, keepdims=True)
    cent = x - mean
    var = jnp.mean(cent * cent, axis=-1, keepdims=True)
    inverse = lax.rsqrt(var + 1e-05)
    return cent * inverse, inverse


def norm_back(d_norm, unit, inverse, gain):
    scaled = d_norm * gain
    first = jnp.mean(scaled, axis=-1, keepdims=True)
    second = jnp.mean(scaled * unit, axis=-1, keepdims=True)
    return (
        inverse * (scaled - first - unit * second),
        jnp.sum(d_norm * unit, axis=0, keepdims=True),
        jnp.sum(d_norm, axis=0, keepdims=True),
    )


def pick_pieces(scal, tokens, d_out, *refs):
    outs, sems = refs[:-1], refs[-1]
    half = len(outs) // 2
    copies = []
    for k in range(half):
        at = lax.bitwise_xor(scal[0], k)
        for i, ref in enumerate((tokens, d_out)):
            copies.append(pltpu.make_async_copy(ref.at[at], outs[half * i + k], sems.at[2 * k + i]))
            copies[-1].start()
    for copy in copies:
        copy.wait()


def by_lanes(x):
    return jnp.concatenate([x[:, at : at + LANES] for at in range(0, x.shape[1], LANES)], axis=0)


def from_lanes(x, columns):
    rows = x.shape[0] // (columns // LANES)
    return jnp.concatenate([x[at : at + rows] for at in range(0, x.shape[0], rows)], axis=1)


def two_parts(x):
    high = x.astype(BF16)
    return jnp.concatenate([high, (x - high.astype(F32)).astype(BF16)], axis=0)


def one_part(x):
    half = x.shape[0] // 2
    return x[:half].astype(F32) + x[half:].astype(F32)


def assemble(*refs):
    rows = refs[0].shape[0]
    for k, ref in enumerate(refs[:-1]):
        refs[-1][pl.ds(k * rows, rows), :] = ref[...]


def project(scal, gain, bias, w_query, w_key, w_value, *refs, buckets, span, group, part):
    own, other, x_ref, norm_ref, half_ref, query_ref = refs[:6]
    kv = refs[6:]
    share = own.shape[-1]
    rows = buckets * span
    mine, others = lanes_of(scal[4], share), lanes_of(1 - scal[4], share)
    x_ref[:, mine] = own[...]
    x_ref[:, others] = other[...]
    unit, _ = centred(x_ref[...].astype(F32))
    norm = (unit * gain[...] + bias[...]).astype(BF16)
    norm_ref[...] = norm
    half_ref[...] = norm_ref[pl.ds(pl.multiple_of(scal[4] * (rows // 2), rows // 2), rows // 2), :]
    keyed = dot(norm, w_key[...], out=BF16)
    valued = dot(norm, w_value[...], out=BF16)
    for j in range(group):
        hot = spread(scal, j, share, part)
        kv[j][0] = dot(keyed, hot, out=BF16).reshape(buckets, span, LANES)
        kv[j][1] = dot(valued, hot, out=BF16).reshape(buckets, span, LANES)
    query_ref[...] = dot(norm, w_query[...], out=BF16)


def gate_out(scal, query, w_out, *refs, rows, part):
    parts, (mixer_ref, gated_ref, branch_ref) = refs[:-3], refs[-3:]
    share = query.shape[-1]
    mixer = jnp.zeros((rows, share), F32)
    for j, ref in enumerate(parts):
        mixer = mixer + dot(ref[...].reshape(rows, LANES), spread(scal, j, share, part), (1, 1))
    mixer_ref[...] = mixer.astype(BF16)
    gated = (query[...].astype(F32) * mixer).astype(BF16)
    gated_ref[...] = gated
    branch_ref[...] = dot(gated, w_out[...], out=BF16)


def resid_of(x, branch, branch_other):
    return x[...].astype(F32) + (branch[...].astype(F32) + branch_other[...].astype(F32))


def feed_forward(
    scal, x, branch, branch_other, gain, bias, own, other, w_up, w_down, norm_ref, g_ref, act_ref, d_hidden_ref, swap_ref, mine_ref
):
    share = mine_ref.shape[-1]
    width = x.shape[-1]
    mine, others = lanes_of(scal[4], share), lanes_of(1 - scal[4], share)
    g_ref[:, mine] = own[...]
    g_ref[:, others] = other[...]
    unit, _ = centred(resid_of(x, branch, branch_other))
    norm = (unit * gain[...] + bias[...]).astype(BF16)
    norm_ref[...] = norm
    hidden = dot(norm, w_up[...])
    d_act = dot(g_ref[...], w_down[...], (1, 1))
    root = 0.7978845608028654
    square = hidden * hidden
    half = 0.5 + 0.5 * jnp.tanh(hidden * (root + (0.044715 * root) * square))
    product = hidden * half
    act = product.astype(BF16)
    act_ref[...] = act
    slope = half + product * (1.0 - half) * (2.0 * root + (6.0 * 0.044715 * root) * square)
    d_hidden = (d_act * slope).astype(BF16)
    d_hidden_ref[...] = d_hidden
    swap_ref[:, :width] = dot(d_hidden, w_up[...], (1, 1), out=BF16)
    swap_ref[:, width:] = dot(act, w_down[:, others], out=BF16)
    resid = x[:, mine].astype(F32) + (branch[:, mine].astype(F32) + branch_other[:, mine].astype(F32))
    mine_ref[...] = resid + dot(act, w_down[:, mine])


def resid_back(
    scal, x, branch, branch_other, mine, other, gain, g, w_out, query, mixer, *refs, buckets, span, group, part
):
    d_branch_ref, d_query_ref, d_mine_ref, vectors = refs[:4]
    outs = refs[4:]
    share = query.shape[-1]
    unit, inverse = centred(resid_of(x, branch, branch_other))
    width = x.shape[-1]
    d_norm2 = mine[:, :width].astype(F32) + other[:, :width].astype(F32)
    d_x, d_gain, d_bias = norm_back(d_norm2, unit, inverse, gain[...])
    d_resid = g[...].astype(F32) + d_x
    d_branch = d_resid.astype(BF16)
    d_branch_ref[...] = d_branch
    d_gated = dot(d_branch, w_out[...], (1, 1))
    d_mixer = (d_gated * query[...].astype(F32)).astype(BF16)
    for j in range(group):
        outs[j][...] = dot(d_mixer, spread(scal, j, share, part), out=BF16).reshape(buckets, span, LANES)
    d_query_ref[...] = (d_gated * mixer[...].astype(F32)).astype(BF16)
    vectors[0:1, :] = d_gain
    vectors[1:2, :] = d_bias
    d_mine_ref[...] = jnp.where(scal[4] == 0, d_resid[:, :share], d_resid[:, share:])


def project_back(scal, d_query, w_query, w_key, w_value, *refs, rows, part):
    parts, d_norm_ref = refs[:-1], refs[-1]
    share = d_query.shape[-1]
    sums = [jnp.zeros((rows, share), F32) for _ in range(2)]
    for j, ref in enumerate(parts):
        hot = spread(scal, j, share, part)
        for i in range(2):
            sums[i] = sums[i] + dot(ref[i].reshape(rows, LANES), hot, (1, 1))
    d_keyed, d_valued = sums[0].astype(BF16), sums[1].astype(BF16)
    d_norm_ref[...] = (
        dot(d_query[...], w_query[...], (1, 1))
        + dot(d_keyed, w_key[...], (1, 1))
        + dot(d_valued, w_value[...], (1, 1))
    ).astype(BF16)


def key_value_grads(scal, norm, mine, theirs, d_kv, total, *, buckets, group):
    rows = norm.shape[0]
    half = buckets // 2
    for i in range(2):
        grad = dot(norm[...], d_kv[0][i].reshape(rows, LANES), (0, 0))
        for j in range(1, group):
            for ref, member in ((mine[j - 1], scal[4]), (theirs[j - 1], 1 - scal[4])):
                right = d_kv[j][i, pl.ds(member * half, half)].reshape(rows // 2, LANES)
                grad = grad + dot(ref[...], right, (0, 0))
        total[:, LANES * i : LANES * i + LANES] = grad


def small_sum(mine, got, plain, fine):
    plains = mine[:plain].astype(F32) + got[:plain].astype(F32)
    return plains, one_part(mine[plain : plain + 2 * fine]) + one_part(got[plain : plain + 2 * fine])


def parameter_fold(mine, keep, got, send, keep_out, *, plain, fine):
    plains, fines = small_sum(mine, got, plain, fine)
    small = plain + 2 * fine
    send[pl.ds(0, plain), :] = plains.astype(BF16)
    send[pl.ds(plain, 2 * fine), :] = two_parts(fines)
    half = keep.shape[0] // 2
    keep_out[...] = keep[:half] + got[small : small + half].astype(F32)
    send[pl.ds(small, half), :] = (keep[half:] + got[small + half :].astype(F32)).astype(BF16)


def vector_sum(*refs, first):
    refs[-1][...] = tree_sum([one_part(ref[first:]) for ref in refs[:-1]])


def place_pieces(scal, *refs, span):
    pieces, (tokens_ref, block_ref) = refs[:-2], refs[-2:]
    share = tokens_ref.shape[-1]
    rows = span * (share // LANES)
    for k, ref in enumerate(pieces):
        at = lax.bitwise_xor(scal[0], k)
        tokens_ref[at] = from_lanes(ref[:rows], share).astype(F32)
        block_ref[at] = from_lanes(ref[rows : 2 * rows], share).astype(F32)


def bucket_sum(scal, vector, mine, keep, got, *outs, group, plain, fine):
    plain_sum, fine_sum = small_sum(mine, got, plain, fine)
    matrix = keep[...] + got[plain + 2 * fine :].astype(F32)
    matrix = from_lanes(matrix, 2 * LANES).astype(BF16)
    total = matrix.shape[0]
    block = total // group
    out_row = lax.broadcasted_iota(jnp.int32, (total, total), 0)
    in_row = lax.broadcasted_iota(jnp.int32, (total, total), 1)
    source = lax.bitwise_xor(out_row // block, scal[1]) * block + lax.rem(out_row, block)
    matrix = dot(jnp.where(source == in_row, 1.0, 0.0).astype(BF16), matrix, out=BF16)
    sums = jnp.concatenate([plain_sum.astype(BF16), two_parts(fine_sum), two_parts(vector[...])], axis=0)
    small = sums.shape[0]
    for j, out in enumerate(outs):
        out[pl.ds(0, small), :] = sums
        out[pl.ds(small, 2 * block), :] = by_lanes(matrix[j * block : j * block + block])


def group_place(scal, *refs, part, span, nstate, fine, vec):
    parts, (key_ref, value_ref, shift_ref, coef_ref, fine_ref, vec_ref) = refs[:-6], refs[-6:]
    share = shift_ref.shape[-1]
    block = key_ref.shape[0]
    plain = span + nstate
    sums = jnp.zeros((plain, share), F32)
    matrix = jnp.zeros((2 * block, share), F32)
    fines, vectors = [], []
    for j, ref in enumerate(parts):
        hot = spread(scal, j, share, part)
        first = plain + 2 * (fine + vec)
        sums = sums + dot(ref[:plain], hot, (1, 1))
        matrix = matrix + dot(ref[first : first + 2 * block], hot, (1, 1))
        fines.append(one_part(ref[plain : plain + 2 * fine]))
        vectors.append(one_part(ref[plain + 2 * fine : first]))
    key_ref[...] = matrix[:block]
    value_ref[...] = matrix[block:]
    shift_ref[...] = sums[:span]
    coef_ref[...] = sums[span:]
    fine_ref[...] = tree_sum(fines)
    vec_ref[...] = tree_sum(vectors)


def turn(*refs, pairs):
    for i in range(pairs):
        source, left, out = refs[2 * i], refs[2 * i + 1], refs[2 * pairs + i]
        width = left.shape[1]
        lane = lax.broadcasted_iota(jnp.int32, (width, LANES), 1)
        hot = jnp.concatenate(
            [jnp.where(source[...] == lane + m, 1.0, 0.0).astype(BF16) for m in range(0, width, LANES)], axis=1
        )
        out[...] = dot(hot, left[...], (1, 1), out=BF16)


def row_grads(*refs, streams):
    pairs = sum(len(s) for s in streams)
    i = 0
    for t, stream in enumerate(streams):
        send, keep = refs[2 * pairs + 2 * t], refs[2 * pairs + 2 * t + 1]
        at = 0
        for first, last in stream:
            turned, right = refs[2 * i], refs[2 * i + 1]
            half = turned.shape[0] // 2
            operand = right[:, first:last]
            send[:, at : at + last - first] = dot(turned[half:], operand, out=BF16)
            keep[:, at : at + last - first] = dot(turned[:half], operand, out=BF16)
            at += last - first
            i += 1


def add(keep, got, out):
    out[...] = keep[...].astype(F32) + got[...].astype(F32)


def finish(*refs, plan):
    outs = refs[sum(terms for terms, _ in plan) :]
    i = 0
    for terms, columns in plan:
        total = refs[i][...].astype(F32)
        if terms == 2:
            total = total + refs[i + 1][...].astype(F32)
        i += terms
        for first, last, out, at in columns:
            outs[out][:, at : at + last - first] = total[:, first:last]


def fold(*refs, pairs):
    ins, outs = refs[: 2 * pairs], refs[2 * pairs :]
    at = 0
    for i in range(pairs):
        keep, got = ins[2 * i], ins[2 * i + 1]
        half, columns = keep.shape[0] // 2, keep.shape[1]
        if len(outs) == 2:
            here, columns_at = outs, pl.ds(at, columns)
        else:
            here, columns_at = outs[2 * i : 2 * i + 2], pl.ds(0, columns)
        here[0][:, columns_at] = (keep[half:].astype(F32) + got[half:].astype(F32)).astype(BF16)
        here[1][:, columns_at] = keep[:half].astype(F32) + got[:half].astype(F32)
        at += columns


def tokens_back(scal, x, d_norm, d_norm_other, gain, d_mine, block_mine, swapped, *refs, span):
    share = d_mine.shape[-1]
    width = x.shape[-1]
    unit, inverse = centred(x[...].astype(F32))
    d_norm1 = d_norm[...].astype(F32) + d_norm_other[...].astype(F32)
    d_x, d_gain, d_bias = norm_back(d_norm1, unit, inverse, gain[...])
    total = (d_mine[...] + jnp.where(scal[4] == 0, d_x[:, :share], d_x[:, share:])).astype(BF16)
    block = (block_mine[...] + swapped[:, width:].astype(F32)).astype(BF16)
    vectors = [by_lanes(d_gain), by_lanes(d_bias)]
    pad = -(2 * (width // LANES)) % 16
    vectors = two_parts(jnp.concatenate(vectors + [jnp.zeros((pad, LANES), F32)] * (pad > 0), axis=0))
    rows = span * (share // LANES)
    for k, out in enumerate(refs):
        out[pl.ds(0, rows), :] = by_lanes(total[k * span : k * span + span])
        out[pl.ds(rows, rows), :] = by_lanes(block[k * span : k * span + span])
        out[pl.ds(2 * rows, vectors.shape[0]), :] = vectors


def rolled(x, r):
    return x if r == 0 else pltpu.roll(x, r % x.shape[0], 0)


def split(x):
    high = x.astype(BF16)
    return high, (x - high.astype(F32)).astype(BF16)


def split_dot(left, right):
    lh, ll = split(left)
    rh, rl = split(right)
    return jnp.dot(
        jnp.concatenate([lh, lh, ll], axis=1),
        jnp.concatenate([rh, rl, rh], axis=0),
        preferred_element_type=F32,
    )


def half_dot(left, right):
    lh, ll = split(left)
    rh = right.astype(BF16)
    return jnp.dot(
        jnp.concatenate([lh, ll], axis=1), jnp.concatenate([rh, rh], axis=0), preferred_element_type=F32
    )


def powers_by_step(rrow, span, reverse, shift):
    step = lax.broadcasted_iota(jnp.int32, (span, LANES), 0).astype(F32)
    step = (span - 1.0 - step) if reverse else step + shift
    return jnp.exp(-step * rrow)


def powers_by_state(rcol, span, reverse, shift):
    step = lax.broadcasted_iota(jnp.int32, (LANES, span), 1).astype(F32)
    step = (span - 1.0 - step) if reverse else step + shift
    return jnp.exp(-step * rcol[:, :span]), step


def chunk_row(scal, j, k, group, span):
    return pl.multiple_of(
        (lax.bitwise_xor(scal[0], k) * group + lax.bitwise_xor(scal[1], j)) * span, span
    )


def wide(ref, first, batch, span):
    return jnp.concatenate(
        [ref[pl.ds(pl.multiple_of((first + i) * span, span), span), :] for i in range(batch)], axis=1
    )


def mix_forward(scal, valid, tabs, rrow, taps, *refs, group, buckets, span, batch):
    kv = refs[:group]
    outs = refs[group : 2 * group]
    kf, vf, shifted_ref, mixed_ref, states, ysc, kern_ref = refs[2 * group :]
    limit = valid[scal[0]]
    rcol, scol, coefm, hm = tabs[0], tabs[1], tabs[3], tabs[4]
    eighths = span // 8
    chunks = group * buckets
    kern_ref[...] = split_dot(powers_by_step(rrow[...], span, False, 0.0), scol * coefm)
    w_end = powers_by_state(rcol, span, True, 0.0)[0] * scol[:, :span]
    p_out = powers_by_step(rrow[...], span, False, 1.0)
    decay = jnp.exp(-float(span) * rcol)
    kf[pl.ds(0, span), :] = jnp.zeros((span, LANES), F32)
    for j in range(group):
        for k in range(buckets):
            row = chunk_row(scal, j, k, group, span)
            kf[pl.ds(row + span, span), :] = kv[j][0, k].astype(F32)
            vf[pl.ds(row, span), :] = kv[j][1, k].astype(F32)
    row_id = lax.broadcasted_iota(jnp.int32, (span, LANES), 0)

    def filtered(c, carry):
        start = pl.multiple_of(c * span, span)
        x = kf[pl.ds(start, 2 * span), :]
        acc = jnp.zeros((span, LANES), F32)
        for r in range(8):
            xr = rolled(x, r)
            for q in range(eighths):
                acc = acc + taps[8 * q + r : 8 * q + r + 1, :] * xr[span - 8 * q : 2 * span - 8 * q]
        shifted_ref[pl.ds(start, span), :] = acc
        mixed_ref[pl.ds(start, span), :] = jnp.where(
            row_id + start < limit, acc * vf[pl.ds(start, span), :], 0.0
        )
        return carry

    lax.fori_loop(0, chunks, filtered, 0)

    def carried(turn, state):
        first = turn * batch
        ends = split_dot(w_end, wide(mixed_ref, first, batch, span))
        begins = []
        for i in range(batch):
            states[first + i] = state
            begins.append(coefm * state)
            state = decay * state + ends[:, LANES * i : LANES * i + LANES] * hm
        y = split_dot(p_out, jnp.concatenate(begins, axis=1))
        for i in range(batch):
            ysc[pl.ds(pl.multiple_of((first + i) * span, span), span), :] = y[:, LANES * i : LANES * i + LANES]
        return state

    lax.fori_loop(0, chunks // batch, carried, jnp.zeros((LANES, LANES), F32))

    def inner(c, carry):
        start = pl.multiple_of(c * span, span)
        mixed = mixed_ref[pl.ds(start, span), :]
        y = ysc[pl.ds(start, span), :]
        tails = [y[8 * i : 8 * i + 8] for i in range(eighths)]
        for r in range(8):
            mr = jnp.where(row_id >= r, rolled(mixed, r), 0.0)
            for q in range(eighths):
                weight = kern_ref[8 * q + r : 8 * q + r + 1, :]
                for i in range(q, eighths):
                    tails[i] = tails[i] + weight * mr[8 * (i - q) : 8 * (i - q) + 8]
        for i in range(eighths):
            ysc[pl.ds(start + 8 * i, 8), :] = tails[i]
        return carry

    lax.fori_loop(0, chunks, inner, 0)
    for j in range(group):
        for k in range(buckets):
            outs[j][k] = ysc[pl.ds(chunk_row(scal, j, k, group, span), span), :].astype(BF16)


def mix_backward(scal, valid, tabs, rrow, taps, vf, shifted_ref, *refs, group, buckets, span, batch):
    d_in = refs[:group]
    outs = refs[group : 2 * group]
    dmf, dsf, adj, dks, dvs, kern_ref = refs[2 * group :]
    limit = valid[scal[0]]
    rcol, scol, coefm = tabs[0], tabs[1], tabs[3]
    kern_ref[...] = split_dot(powers_by_step(rrow[...], span, False, 0.0), scol * coefm)
    p_rev = powers_by_step(rrow[...], span, True, 0.0)
    p_in = powers_by_state(rcol, span, False, 1.0)[0]
    decay = jnp.exp(-float(span) * rcol)
    chunks = group * buckets
    eighths = span // 8
    dsf[pl.ds(chunks * span, span), :] = jnp.zeros((span, LANES), F32)
    for j in range(group):
        for k in range(buckets):
            dmf[pl.ds(chunk_row(scal, j, k, group, span), span), :] = d_in[j][k].astype(F32)
    row_id = lax.broadcasted_iota(jnp.int32, (span, LANES), 0)

    def carried(turn, after):
        first = chunks - batch - turn * batch
        seeds = half_dot(p_in, wide(dmf, first, batch, span))
        ends = [None] * batch
        for i in reversed(range(batch)):
            adj[first + i] = after
            ends[i] = scol * after
            after = decay * after + coefm * seeds[:, LANES * i : LANES * i + LANES]
        y = split_dot(p_rev, jnp.concatenate(ends, axis=1))
        for i in range(batch):
            dks[pl.ds(pl.multiple_of((first + i) * span, span), span), :] = y[:, LANES * i : LANES * i + LANES]
        return after

    lax.fori_loop(0, chunks // batch, carried, jnp.zeros((LANES, LANES), F32))

    def chunk(turn, carry):
        start = pl.multiple_of((chunks - 1 - turn) * span, span)
        dm = dmf[pl.ds(start, span), :]
        y = dks[pl.ds(start, span), :]
        heads = [y[8 * i : 8 * i + 8] for i in range(eighths)]
        for r in range(8):
            mr = jnp.where(row_id < span - r, rolled(dm, -r), 0.0)
            for q in range(eighths):
                weight = kern_ref[8 * q + r : 8 * q + r + 1, :]
                for i in range(eighths - q):
                    heads[i] = heads[i] + weight * mr[8 * (i + q) : 8 * (i + q) + 8]
        d_mixed = jnp.where(row_id + start < limit, jnp.concatenate(heads, axis=0), 0.0)
        dvs[pl.ds(start, span), :] = d_mixed * shifted_ref[pl.ds(start, span), :]
        dsf[pl.ds(start, span), :] = d_mixed * vf[pl.ds(start, span), :]
        x = dsf[pl.ds(start, 2 * span), :]
        acc = jnp.zeros((span, LANES), F32)
        for r in range(8):
            xr = rolled(x, -r)
            for q in range(eighths):
                acc = acc + taps[8 * q + r : 8 * q + r + 1, :] * xr[8 * q : 8 * q + span]
        dks[pl.ds(start, span), :] = acc
        return carry

    lax.fori_loop(0, chunks, chunk, 0)
    for j in range(group):
        for k in range(buckets):
            row = chunk_row(scal, j, k, group, span)
            outs[j][0, k] = dks[pl.ds(row, span), :].astype(BF16)
            outs[j][1, k] = dvs[pl.ds(row, span), :].astype(BF16)


def param_grads(scal, tabs, rrow, kf, mixed_ref, states, dmf, dsf, adj, vectors, norm, *refs, span, batch, nstate, group, buckets):
    mine, theirs = refs[: group - 1], refs[group - 1 : 2 * group - 2]
    d_kv = refs[2 * group - 2 : 3 * group - 2]
    first = 3 * group - 2
    send, keep, out, total, coef_out, rate_out, acc_s, acc_k = refs[first:]
    key_value_grads(scal, norm, mine, theirs, d_kv, total, buckets=buckets, group=group)
    rcol, scol, dscol, coefm, hm = tabs[0], tabs[1], tabs[2], tabs[3], tabs[4]
    p_in, step = powers_by_state(rcol, span, False, 1.0)
    into = jnp.concatenate([p_in, p_in * step], axis=0)
    p_end, step = powers_by_state(rcol, span, True, 0.0)
    ends = jnp.concatenate([p_end, p_end * step], axis=0)
    p_kern, step = powers_by_state(rcol, span, False, 0.0)
    decay = float(span) * jnp.exp(-float(span) * rcol)
    chunks = mixed_ref.shape[0] // span
    eighths = span // 8
    acc_s[...] = jnp.zeros_like(acc_s)
    acc_k[...] = jnp.zeros_like(acc_k)
    coef_out[...] = jnp.zeros_like(coef_out)
    rate_out[...] = jnp.zeros_like(rate_out)
    row_id = lax.broadcasted_iota(jnp.int32, (span, LANES), 0)

    def chunk(c, carry):
        start = pl.multiple_of(c * span, span)
        x = kf[pl.ds(start, 2 * span), :]
        ds = dsf[pl.ds(start, span), :]
        mixed = mixed_ref[pl.ds(start, span), :]
        dm = dmf[pl.ds(start, span), :]
        for r in range(8):
            xr = rolled(x, r)
            mr = jnp.where(row_id >= r, rolled(mixed, r), 0.0)
            for q in range(eighths):
                whole = ds * xr[span - 8 * q : 2 * span - 8 * q]
                acc_s[8 * q + r] += jnp.sum(whole.reshape(eighths, 8, LANES), axis=0)
                part = dm[8 * q :] * mr[: span - 8 * q]
                acc_k[8 * q + r] += jnp.sum(part.reshape(eighths - q, 8, LANES), axis=0)
        return carry

    lax.fori_loop(0, chunks, chunk, 0)

    def rates(turn, carry):
        first = turn * batch
        z = half_dot(into, wide(dmf, first, batch, span))
        u = split_dot(ends, wide(mixed_ref, first, batch, span))
        coef = coef_out[...]
        rate = rate_out[...]
        for i in range(batch):
            state, after = states[first + i], adj[first + i]
            at = slice(LANES * i, LANES * i + LANES)
            coef = coef + state * z[:LANES, at]
            rate = (
                rate
                + after * (dscol * u[:LANES, at] - scol * u[LANES:, at] - decay * state)
                - coefm * state * z[LANES:, at]
            )
        coef_out[...] = coef
        rate_out[...] = rate
        return carry

    lax.fori_loop(0, chunks // batch, rates, 0)
    out[pl.ds(0, span), :] = jnp.sum(acc_s[...], axis=1)
    gk = jnp.sum(acc_k[...], axis=1)
    m = split_dot(jnp.concatenate([p_kern, p_kern * step], axis=0), gk)
    m0, m1 = m[:LANES], m[LANES:]
    coef = (coef_out[...] + scol * m0) * hm
    out[pl.ds(span, nstate), :] = coef[:nstate] + coef[nstate:]
    at = span + nstate
    pieces_across = vectors.shape[1] // LANES
    for v in range(2):
        for i in range(pieces_across):
            out[pl.ds(at + v * pieces_across + i, 1), :] = vectors[v : v + 1, LANES * i : LANES * i + LANES]
    at = out.shape[0] - 8
    done = span + nstate + 2 * pieces_across
    out[pl.ds(done, at - done), :] = jnp.zeros((at - done, LANES), F32)
    rate = rate_out[...] + coefm * (dscol * m0 - scol * m1)
    rate = jnp.broadcast_to(jnp.sum(rate, axis=1, keepdims=True), (LANES, LANES))
    row = lax.broadcasted_iota(jnp.int32, (LANES, LANES), 0)
    lane = lax.broadcasted_iota(jnp.int32, (LANES, LANES), 1)
    rate = jnp.where(lax.rem(row, nstate) == lane, rate, 0.0)
    head = lax.broadcasted_iota(jnp.int32, (8, LANES), 0)
    owner = lax.broadcasted_iota(jnp.int32, (8, LANES), 1) // nstate + scal[3]
    out[pl.ds(at, 8), :] = fdot(jnp.where(head == owner, 1.0, 0.0), rate)
    plain = out[pl.ds(0, span + nstate), :].astype(BF16)
    fine = two_parts(out[pl.ds(span + nstate, out.shape[0] - span - nstate), :])
    plane = total.shape[0] // buckets
    small = plain.shape[0] + fine.shape[0]
    send[pl.ds(0, plain.shape[0]), :] = plain
    send[pl.ds(plain.shape[0], fine.shape[0]), :] = fine
    for k in range(buckets):
        at = pl.multiple_of(lax.bitwise_xor(scal[0], k) * plane, plane)
        rows = total[pl.ds(at, plane), :]
        if k % 2:
            send[pl.ds(small + (k // 2) * 2 * plane, 2 * plane), :] = by_lanes(rows.astype(BF16))
        else:
            keep[pl.ds((k // 2) * 2 * plane, 2 * plane), :] = by_lanes(rows)


def body(
    tokens,
    valid_len,
    ln1_gain,
    ln1_bias,
    w_query,
    w_key,
    w_value,
    shift_kernel,
    ssm_rate,
    ssm_coef,
    w_out,
    ln2_gain,
    ln2_bias,
    w_up,
    w_down,
    d_out,
):
    buckets, span, share = tokens.shape
    rows = buckets * span
    heads, nstate = ssm_rate.shape
    head_width = share // heads
    width, hidden = w_up.shape
    count = lax.axis_size("seq")
    group = count // buckets
    part = share // group
    place = lax.axis_index("seq")
    member = lax.axis_index("ch")
    b, g = place // group, place % group
    first_head = (g * part) // head_width
    scal = jnp.stack([b, g, place, first_head, member]).astype(jnp.int32)
    as_row = lambda v: v.reshape(1, -1)
    ANY = pl.BlockSpec(memory_space=pl.ANY)

    def trade_buckets(pieces):
        return [pieces[0]] + [trade(pieces[k], k * group) for k in range(1, buckets)]

    def trade_group(blocks):
        return [blocks[0]] + [trade(blocks[j], j) for j in range(1, group)]

    call = Order()

    picked = call(
        pick_pieces,
        "pick_pieces",
        [pltpu.VMEM((span, share), BF16)] * (2 * buckets),
        scal,
        in_hbm(tokens),
        in_hbm(d_out),
        scratch=[pltpu.SemaphoreType.DMA((2 * buckets,))],
        in_specs=[SMEM, ANY, ANY],
        smem=1,
    )
    (own,) = call(assemble, "assemble", [shape(BF16, rows, share)], *trade_buckets(picked[:buckets]))
    other = swap(own)
    own_out = trade_buckets(picked[buckets:])

    lane = jnp.arange(LANES, dtype=jnp.int32)
    row_head = first_head + lane // nstate
    hm = (row_head[:, None] == ((g * part + lane) // head_width)[None, :]) & (lane < part)[None, :]
    hm = hm.astype(F32)
    two = lax.dynamic_slice_in_dim(
        jnp.concatenate([ssm_rate, ssm_rate[-1:]], axis=0), first_head, 2, 0
    ).reshape(1, 2 * nstate)
    rate_col = jnp.broadcast_to(two.reshape(-1, 1), (LANES, LANES))
    scale_col = jnp.sqrt(-jnp.expm1(-2.0 * rate_col))
    dscale_col = jnp.exp(-2.0 * rate_col) / scale_col
    coef_part = lax.dynamic_slice_in_dim(ssm_coef, g * part, part, 0)
    coef_part = jnp.pad(coef_part, ((0, LANES - part), (0, 0))).T
    coefm = jnp.concatenate([coef_part, coef_part], axis=0) * hm
    tabs = jnp.stack([rate_col, scale_col, dscale_col, coefm, hm])
    taps = jnp.pad(lax.dynamic_slice_in_dim(shift_kernel, g * part, part, 1), ((0, 0), (0, LANES - part)))

    bits = [1 << i for i in range(count.bit_length() - 1)]
    row_block = width // count

    def source_of(order):
        rel = jnp.arange(width, dtype=jnp.int32)
        at = rel // row_block
        target = jnp.zeros_like(at)
        for i, step in enumerate(order):
            target = target + ((at >> (len(order) - 1 - i)) & 1) * step
        source = (target ^ place) * row_block + rel % row_block
        return jnp.broadcast_to(source[:, None], (width, LANES))

    order_a = bits
    order_b = [bits[1], bits[0]] + bits[2:]
    source_a, source_b = source_of(order_a), source_of(order_b)
    turned_shape = shape(BF16, width, rows)
    half = width // 2

    def turned(*pairs, tag):
        operands = [a for p in pairs for a in p]
        return call(
            functools.partial(turn, pairs=len(pairs)), "turn", [turned_shape] * len(pairs), *operands, tag=tag
        )

    def grads(streams, tag):
        outs = [shape(BF16, half, sum(p[3] - p[2] for p in st)) for st in streams for _ in range(2)]
        operands = [a for st in streams for p in st for a in p[:2]]
        columns = [[p[2:] for p in st] for st in streams]
        return call(functools.partial(row_grads, streams=columns), "row_grads", outs, *operands, tag=tag)

    def folded(ins, joined, tag):
        pairs = len(ins) // 2
        rows_out = ins[0].shape[0] // 2
        columns = [a.shape[1] for a in ins[::2]]
        if rows_out % 16:
            totals = [ins[2 * i].astype(F32) + ins[2 * i + 1].astype(F32) for i in range(pairs)]
            if joined:
                totals = [jnp.concatenate(totals, axis=1)]
            return [v for t in totals for v in (t[rows_out:].astype(BF16), t[:rows_out])]
        if joined:
            columns = [sum(columns)]
        outs = [shape(kind, rows_out, c) for c in columns for kind in (BF16, F32)]
        return call(functools.partial(fold, pairs=pairs), "fold", outs, *ins, tag=tag)

    wide_rows, narrow_rows = shape(BF16, rows, width), shape(BF16, rows, share)
    pair = shape(BF16, 2, buckets, span, LANES)
    small = shape(BF16, buckets, span, LANES)
    sizes = dict(buckets=buckets, span=span, group=group, part=part)
    x, norm1, norm1_half, query, *kv = call(
        functools.partial(project, **sizes),
        "project",
        [pltpu.HBM((rows, width), BF16)] * 2 + [pltpu.HBM((rows // 2, width), BF16), pltpu.HBM((rows, share), BF16)] + [pair] * group,
        scal, as_row(ln1_gain), after(as_row(ln1_bias), taps), w_query, w_key, w_value, own, other,
        smem=1,
    )
    kv = trade_group(kv)
    mine_halves = [trade(norm1_half, j) for j in range(1, group)]
    length = count * span
    long, longer, per_chunk = shape(F32, length, LANES), shape(F32, length + span, LANES), shape(F32, count, LANES, LANES)
    mix_sizes = dict(group=group, buckets=buckets, span=span, batch=min(count, 8))
    mix_vmem = min(14 * MIB + 12 * length * LANES * 4, 60 * MIB)
    forward_out = call(
        functools.partial(mix_forward, **mix_sizes),
        "mix_forward",
        [small] * group + [longer, long, long, long, per_chunk],
        scal, valid_len, tabs, two, taps, *kv,
        scratch=[pltpu.VMEM((length, LANES), F32), pltpu.VMEM((span, LANES), F32)],
        smem=2,
        vmem=mix_vmem,
    )
    kf, vf, shifted, mixed, states = forward_out[group:]
    mixer_parts = trade_group(forward_out[:group])
    (own_out,) = call(assemble, "assemble", [shape(BF16, rows, share)], *own_out)
    other_out = swap(own_out)
    mixer, gated, branch = call(
        functools.partial(gate_out, rows=rows, part=part),
        "gate_out",
        [narrow_rows, narrow_rows, wide_rows],
        scal, after(query, *mine_halves), w_out, *mixer_parts,
        smem=1,
    )
    branch_other = swap(branch)
    other_halves = [swap(p) for p in mine_halves]
    norm2, grad_full, act, d_hidden, to_swap, block_mine = call(
        feed_forward,
        "feed_forward",
        [wide_rows, wide_rows, shape(BF16, rows, hidden), shape(BF16, rows, hidden), shape(BF16, rows, width + share)]
        + [shape(F32, rows, share)],
        scal, x, branch, branch_other, as_row(ln2_gain), as_row(ln2_bias), own_out, other_out, w_up, w_down,
        smem=1,
    )
    swapped = swap(to_swap)

    plane_rows = width // buckets
    vector_rows = 2 * (width // LANES)
    small_rows = -(-(span + nstate + vector_rows + 8) // 16) * 16
    fine = small_rows - span - nstate
    small_out = span + nstate + 2 * fine
    vec_rows = 2 * (-(-vector_rows // 16) * 16)
    piece_rows = 2 * span * (share // LANES) + vec_rows
    block_rows = span + nstate + 2 * fine + vec_rows + 2 * row_block
    ours = shape(F32, buckets, span, share)
    chunks = len(CUTS) + 1
    cuts = [0] + [int(c * hidden) // LANES * LANES for c in CUTS] + [hidden]
    got = {}

    def sent(name, value, move):
        others = [got[n] for n in LATE.get(name, ())]
        got[name] = move(after(value, *others) if others else value)
        return got[name]

    def sent_all(name, values, move):
        moved = move([after(values[0], *[got[n] for n in LATE[name]])] + list(values[1:]) if name in LATE else values)
        got[name] = moved[1]
        for i, value in enumerate(moved[1:]):
            got[name + str(i + 1)] = value
        return moved

    def late(name, values):
        others = [got[n] for n in LATE.get(name, ())]
        return [after(v, *others) for v in values] if others else list(values)

    def resid_step():
        got["d_branch"], got["d_query"], got["d_mine"], got["vectors2"], *d_mixer = call(
            functools.partial(resid_back, **sizes),
            "resid_back",
            [wide_rows, narrow_rows, shape(F32, rows, share), shape(F32, 2, width)] + [small] * group,
            scal, x, branch, branch_other, to_swap, swapped, as_row(ln2_gain), grad_full, w_out, query, mixer,
            smem=1,
        )
        moved = trade_group(late("dm", d_mixer))
        got["d_mixer"] = moved
        for i in range(1, group):
            got["dm%d" % i] = moved[i]

    def turn_up_step():
        got["turned_a"], got["turned_b"] = turned((source_a, norm2), (source_b, grad_full), tag="turn_up")

    def turn_out_step():
        got["turned_o"], got["turned_q"] = turned((source_a, got["d_branch"]), (source_b, norm1), tag="turn_out")

    def grads_step(i):
        streams = [[(got["turned_a"], d_hidden, cuts[i], cuts[i + 1])], [(got["turned_b"], act, cuts[i], cuts[i + 1])]]
        if i == OUT_IN:
            streams[0].append((got["turned_o"], gated, 0, share))
            streams[1].append((got["turned_q"], got["d_query"], 0, share))
        got["c%d" % i] = grads(streams, "grads%d" % i)
        if "t%ds1" % i not in ORDER:
            pair_step(i, 0)

    def pair_step(i, at):
        name = "c%d" % i
        step = name + "s%d" % (at + 1)
        send_a, keep_a, send_b, keep_b = got[name]
        send_a, send_b = late(step, [send_a, send_b])
        got[name] = [keep_a, trade(send_a, order_a[at]), keep_b, trade(send_b, order_b[at])]
        got[step], got[step + "b"] = got[name][1], got[name][3]

    def second_step(i):
        got["c%d" % i] = folded(got["c%d" % i], False, "fold_%ds2" % i)
        if "t%ds2" % i not in ORDER:
            pair_step(i, 1)

    def add_step(i):
        ins = got["c%d" % i]
        got["c%d" % i] = call(add, "add", [shape(F32, *ins[0].shape)], *ins)

    def joint_step(i, at):
        name = "c%d" % i
        ins = got[name]
        if at == 0:
            for other in MERGE.get(i, ()):
                ins = got["c%d" % other] + ins
        send, keep = folded(ins, True, "fold_%dz%d" % (i, at))
        (send,) = late("%sz%d" % (name, at), [send])
        got[name] = [keep, trade(send, bits[2 + at])]
        got["%sz%d" % (name, at)] = got[name][1]

    def mixer_step():
        outs = call(
            functools.partial(mix_backward, **mix_sizes),
            "mix_backward",
            [pair] * group + [long, longer, per_chunk],
            scal, valid_len, tabs, two, taps, vf, shifted, *got["d_mixer"],
            scratch=[pltpu.VMEM((length, LANES), F32), pltpu.VMEM((length, LANES), F32), pltpu.VMEM((span, LANES), F32)],
            smem=2,
            vmem=mix_vmem,
        )
        got["own_kv"], (got["dmf"], got["dsf"], got["adj"]) = outs[:group], outs[group:]
        got["mixer"] = outs[0]
        got["d_kv"] = trade_group(late("dkv", outs[:group]))
        for i in range(1, group):
            got["dkv%d" % i] = got["d_kv"][i]

    def project_step():
        (d_norm1,) = call(
            functools.partial(project_back, rows=rows, part=part), "project_back", [wide_rows],
            scal, got["d_query"], w_query, w_key, w_value, *got["d_kv"], smem=1,
        )
        got["d_norm1"], got["d_norm1_other"] = d_norm1, swap(d_norm1)

    def tokens_step():
        pieces = call(
            functools.partial(tokens_back, span=span),
            "tokens_back",
            [shape(BF16, piece_rows, LANES)] * buckets,
            scal, x, got["d_norm1"], got["d_norm1_other"], as_row(ln1_gain), got["d_mine"], block_mine, swapped,
            smem=1,
        )
        got["tokens"] = pieces[0]
        got["rows"] = trade_buckets(late("pieces", pieces))
        for i in range(1, buckets):
            got["pieces%d" % i] = got["rows"][i]

    def parameters_step():
        kept = buckets // 2 * 2 * plane_rows
        send, keep = call(
            functools.partial(param_grads, span=span, batch=mix_sizes["batch"], nstate=nstate, group=group, buckets=buckets),
            "param_grads",
            [shape(BF16, small_out + kept, LANES), shape(F32, kept, LANES)],
            scal, tabs, two, kf, mixed, states, got["dmf"], got["dsf"], got["adj"], got["vectors2"],
            norm1, *mine_halves, *other_halves, *got["own_kv"],
            scratch=[pltpu.VMEM((small_rows, LANES), F32), pltpu.VMEM((width, 2 * LANES), F32)]
            + [pltpu.VMEM((LANES, LANES), F32)] * 2
            + [pltpu.VMEM((span, 8, LANES), F32)] * 2,
            smem=1,
            vmem=mix_vmem,
        )
        got["parameters"] = send
        (send,) = late("p0", [send])
        got["p"] = [send, keep, trade(send, group)]
        got["p0"] = got["p"][2]

    def parameter_fold_step(at):
        kept = got["p"][1].shape[0] // 2
        send, keep = call(
            functools.partial(parameter_fold, plain=span + nstate, fine=fine),
            "parameter_fold",
            [shape(BF16, small_out + kept, LANES), shape(F32, kept, LANES)],
            *got["p"],
        )
        (send,) = late("p%d" % at, [send])
        got["p"] = [send, keep, trade(send, group << at)]
        got["p%d" % at] = got["p"][2]

    def vector_step():
        (got["vector"],) = call(
            functools.partial(vector_sum, first=piece_rows - vec_rows),
            "vector_sum",
            [shape(F32, vec_rows // 2, LANES)],
            *got["rows"],
        )

    def place_step():
        got["grad_tokens"], got["block_out"] = call(
            functools.partial(place_pieces, span=span), "place_pieces", [ours, ours], scal, *got["rows"], smem=1
        )

    def bucket_step():
        blocks = call(
            functools.partial(bucket_sum, group=group, plain=span + nstate, fine=fine),
            "bucket_sum",
            [shape(BF16, block_rows, LANES)] * group,
            scal, got["vector"], *got["p"],
            smem=1,
        )
        got["blocks"] = trade_group(late("plane", blocks))

    def group_step():
        got["group"] = call(
            functools.partial(group_place, part=part, span=span, nstate=nstate, fine=fine, vec=vec_rows // 2),
            "group_place",
            [shape(F32, row_block, share)] * 2
            + [shape(F32, span, share), shape(F32, nstate, share), shape(F32, fine, LANES), shape(F32, vec_rows // 2, LANES)],
            scal, *got["blocks"],
            smem=1,
        )

    named = dict(
        resid=resid_step, turn_up=turn_up_step, turn_out=turn_out_step, mixer=mixer_step, project=project_step,
        tokens=tokens_step, parameters=parameters_step, vector=vector_step, place=place_step, bucket=bucket_step, group=group_step,
    )
    for name in ORDER:
        if name in named:
            named[name]()
        elif name == "pe":
            for at in range(1, buckets.bit_length() - 1):
                parameter_fold_step(at)
        elif name.startswith("x"):
            add_step(int(name[1:]))
        elif name.startswith("g"):
            grads_step(int(name[1:]))
        elif name.startswith("t"):
            pair_step(int(name[1]), int(name[3]) - 1)
        else:
            i, kind = int(name[1]), name[2:]
            if kind == "s2":
                second_step(i)
            elif kind == "z":
                joint_step(i, 0)
            else:
                for at in range(1, len(bits) - 2):
                    joint_step(i, at)
    plan, ends = [], []
    for i in range(chunks):
        if any(i in m for m in MERGE.values()):
            continue
        columns, at = [], 0
        for c in [*reversed(MERGE.get(i, ())), i]:
            for stream in range(2):
                columns.append((at, at + cuts[c + 1] - cuts[c], stream, cuts[c]))
                at += cuts[c + 1] - cuts[c]
                if c == OUT_IN:
                    columns.append((at, at + share, 2 + stream, 0))
                    at += share
        plan.append((len(got["c%d" % i]), columns))
        ends += got["c%d" % i]
    grad_up, grad_down, grad_out, grad_query = call(
        functools.partial(finish, plan=plan),
        "finish",
        [shape(F32, row_block, hidden)] * 2 + [shape(F32, row_block, share)] * 2,
        *ends,
    )
    grad_down, grad_out = grad_down.T, grad_out.T
    grad_key, grad_value, grad_shift, grad_coef, rest, vectors1 = got["group"]
    block_out, grad_tokens = got["block_out"], got["grad_tokens"]
    grad_g2, grad_c2 = rest[:vector_rows].reshape(2, width)
    grad_rate = rest[fine - 8 : fine - 8 + heads, :nstate]
    grad_g1, grad_c1 = vectors1[:vector_rows].reshape(2, width)
    grad_coef = grad_coef.T
    return (
        block_out,
        grad_tokens,
        grad_g1,
        grad_c1,
        grad_query,
        grad_key,
        grad_value,
        grad_shift,
        grad_rate,
        grad_coef,
        grad_out,
        grad_g2,
        grad_c2,
        grad_up,
        grad_down,
    )


def solution(mesh):
    in_specs = (
        P(None, "seq", "ch"),
        P(),
        P(),
        P(),
        P(None, "ch"),
        P(None, "ch"),
        P(None, "ch"),
        P(None, "ch"),
        P("ch", None),
        P("ch", None),
        P("ch", None),
        P(),
        P(),
        P(None, "ch"),
        P("ch", None),
        P(None, "seq", "ch"),
    )
    out_specs = (
        P(None, "seq", "ch"),
        P(None, "seq", "ch"),
        P(),
        P(),
        P("seq", "ch"),
        P("seq", "ch"),
        P("seq", "ch"),
        P(None, "ch"),
        P("ch", None),
        P("ch", None),
        P("ch", "seq"),
        P(),
        P(),
        P("seq", "ch"),
        P("ch", "seq"),
    )
    return jax.shard_map(body, mesh=mesh, in_specs=in_specs, out_specs=out_specs, check_vma=False)
```
